32 devices in a mesh: rows: 16 (over z, y, x), hid: 2 (over core).
Axes of the slice: x: 2, y: 2, z: 4, core: 2. Of those that a mesh axis runs over, the one named last changes fastest.
Arguments:
- hidden_in: bfloat16 [16384, 768], P('rows', 'hid'), may hold values from -6 to 6
- teacher: bfloat16 [16384, 768], P('rows', 'hid'), may hold values from -6 to 6
- segment_ids: int32 [16384], P('rows'), may hold values from 0 to 127, never falling along the last dimension, each value on 1 to 512 neighbouring positions
- valid_mask: int32 [16384], P('rows'), may hold values 0 or 1
- w_query: bfloat16 [768, 768], P(None, 'hid'), may hold values from -0.21875 to 0.21875
- b_query: float32 [768], P('hid'), may hold values from -3 to 3
- w_key: bfloat16 [768, 768], P(None, 'hid'), may hold values from -0.21875 to 0.21875
- w_value: bfloat16 [768, 768], P(None, 'hid'), may hold values from -0.21875 to 0.21875
- b_value: float32 [768], P('hid'), may hold values from -3 to 3
- w_attn_out: bfloat16 [768, 768], P('hid'), may hold values from -1.75 to 1.75
- b_attn_out: float32 [768], P('hid'), may hold values from -3 to 3
- gain_one: float32 [768], P('hid'), may hold values from 0.5 to 1.5
- shift_one: float32 [768], P('hid'), may hold values from -3 to 3
- w_up: bfloat16 [768, 3072], P(None, 'hid'), may hold values from -0.21875 to 0.21875
- b_up: float32 [3072], P('hid'), may hold values from -3 to 3
- w_down: bfloat16 [3072, 768], P('hid'), may hold values from -0.21875 to 0.21875
- b_down: float32 [768], P('hid'), may hold values from -3 to 3
- gain_two: float32 [768], P('hid'), may hold values from 0.5 to 1.5
- shift_two: float32 [768], P('hid'), may hold values from -3 to 3
- head_alpha: float32 [12], P('hid'), may hold values from -3 to 5
- mha_alpha: float32 [1], replicated, may hold values from -0.3 to 0.7
- unit_alpha: float32 [3072], P('hid'), may hold values from -3 to 5
- ffn_alpha: float32 [1], replicated, may hold values from -0.3 to 0.7
- hidden_alpha: float32 [768], P('hid'), may hold values from -2 to 5
- head_noise: float32 [12], P('hid'), may hold values from 0.05 to 0.95
- mha_noise: float32 [1], replicated, may hold values from 0.3 to 0.7
- unit_noise: float32 [3072], P('hid'), may hold values from 0.05 to 0.95
- ffn_noise: float32 [1], replicated, may hold values from 0.3 to 0.7
- hidden_noise: float32 [768], P('hid'), may hold values from 0.05 to 0.95
- lagrange: float32 [2], replicated, may hold values from 1 to 4
Outputs:
- output: bfloat16 [16384, 768], P('rows', 'hid')
- grad_input: float32 [16384, 768], P('rows', 'hid')
- grad_w_query: float32 [768, 768], P(None, 'hid')
- grad_b_query: float32 [768], P('hid')
- grad_w_key: float32 [768, 768], P(None, 'hid')
- grad_w_value: float32 [768, 768], P(None, 'hid')
- grad_b_value: float32 [768], P('hid')
- grad_w_attn_out: float32 [768, 768], P('hid')
- grad_b_attn_out: float32 [768], P('hid')
- grad_gain_one: float32 [768], P('hid')
- grad_shift_one: float32 [768], P('hid')
- grad_w_up: float32 [768, 3072], P(None, 'hid')
- grad_b_up: float32 [3072], P('hid')
- grad_w_down: float32 [3072, 768], P('hid')
- grad_b_down: float32 [768], P('hid')
- grad_gain_two: float32 [768], P('hid')
- grad_shift_two: float32 [768], P('hid')
- grad_head_gate: float32 [12], P('hid')
- grad_mha_gate: float32 [1], replicated
- grad_unit_gate: float32 [3072], P('hid')
- grad_ffn_gate: float32 [1], replicated
- grad_hidden_gate: float32 [768], P('hid')
- grad_head_alpha: float32 [12], P('hid')
- grad_mha_alpha: float32 [1], replicated
- grad_unit_alpha: float32 [3072], P('hid')
- grad_ffn_alpha: float32 [1], replicated
- grad_hidden_alpha: float32 [768], P('hid')
- expected_share: float32 [1], replicated
- penalty: float32 [1], replicated
The draws below stay inside these ranges and needn't reach their ends.
Inputs may be any that keep to these rules, and one draw needn't show every extreme that they name: `segment_ids`: segment numbers never fall along the tokens, and a segment holds at most 512 tokens.
All inputs are finite; a program needn't handle non-finite values. No bound on the sum of `valid_mask` on one device may be relied on, other than what follows from the above.
Results may differ from the reference program's by a relative error of at most 0.013.
Values may be sent and summed in bfloat16 or wider, within the bound.
No kernel may reach another device: no remote copies, remote signals or barrier semaphores. Data moves between devices by JAX's collectives and lax.ppermute only.
A program may use at most 128 MiB of HBM per device.

```python
import math
import jax
import jax.numpy as jnp
import numpy as np
from jax import lax

D = 768
HEADS = 12
HD = 64
FF = 3072
BLOCK = 512
TOKENS = 16384


def touch_ends(values, key, low, top_value):
    spot = [jax.random.randint(jax.random.fold_in(key, axis), (), 0, length) for axis, length in enumerate(values.shape)]
    main_axis = values.shape.index(max(values.shape))
    beside = spot[:main_axis] + [(spot[main_axis] + 1) % values.shape[main_axis]] + spot[main_axis + 1:]
    return values.at[tuple(spot)].set(low).at[tuple(beside)].set(top_value)


def levels(own_key, extent, cuts, low, high):
    level, own = 1.0, jax.random.fold_in(own_key, 6)
    for axis_at, shards_of in cuts:
        heights = jnp.exp(jax.random.uniform(jax.random.fold_in(own, axis_at), (shards_of,), jnp.float32, low / len(cuts), high / len(cuts)))
        level = level * jnp.repeat(heights, extent[axis_at] // shards_of).reshape([-1 if axis == axis_at else 1 for axis in range(len(extent))])
    return level


def profile(count, total, bound, lean):
    loads = [(1 << 20) // math.isqrt(rank ** lean) + 1 for rank in range(2, count + 1)]
    surplus, holding = total - bound - (count - 1), [1] * (count - 1)
    while surplus > 0:
        free = [i for i in range(count - 1) if holding[i] < bound]
        whole, budget = sum([loads[i] for i in free]), surplus
        for i in free:
            more = min(bound - holding[i], max(1, budget * loads[i] // whole), surplus)
            holding[i] = holding[i] + more
            surplus = surplus - more
    return np.array([bound] + holding)


def ragged(key, count, total, bound, lean):
    if count == 2:
        one = jax.random.randint(key, (), max(1, total - bound), min(bound, total - 1) + 1)
        return jnp.stack([one, total - one])
    lengths = jnp.asarray(profile(count, total, bound, lean), jnp.int32)
    twos = (count - 1) // 2
    source_of, receiver = lengths[1:1 + 2 * twos:2], lengths[2:2 + 2 * twos:2]
    room = jnp.minimum(source_of - 1, bound - receiver)
    passed = jax.random.randint(jax.random.fold_in(key, 1), (twos,), 0, 1 << 20) % (room + 1)
    lengths = lengths.at[1:1 + 2 * twos:2].set(source_of - passed).at[2:2 + 2 * twos:2].set(receiver + passed)
    return lengths[jax.random.permutation(jax.random.fold_in(key, 2), count)]


def gaussian(stream_key, dims, deviation, limit, shards=(), dtype=jnp.bfloat16):
    values = deviation * jax.random.normal(stream_key, dims, jnp.float32)
    if shards:
        values = values * levels(stream_key, dims, shards, -0.22, 0.18)
    return jnp.clip(values, -limit, limit).astype(dtype)


def setup_inputs(seed: int = 0) -> dict:
    streams_of = jax.random.split(jax.random.key(seed), 31)
    hidden_in = gaussian(streams_of[0], (TOKENS, D), 1.0, 6.0, ((0, 16), (1, 2)))
    teacher = gaussian(streams_of[1], (TOKENS, D), 1.0, 6.0, ((0, 16), (1, 2)))
    segment_ids = jnp.searchsorted(jnp.cumsum(ragged(streams_of[2], TOKENS // (BLOCK // 4), TOKENS, BLOCK, 2)), jnp.arange(TOKENS), side="right").astype(jnp.int32)
    valid_mask = touch_ends((jax.random.randint(streams_of[3], (TOKENS,), 0, 8) < 7).astype(jnp.int32), jax.random.fold_in(streams_of[3], 1), 0, 1)
    w_query = gaussian(streams_of[4], (D, D), D ** -0.5, 0.21875, ((1, 2),))
    b_query = gaussian(streams_of[5], (D,), 0.5, 3.0, ((0, 2),), jnp.float32)
    w_key = gaussian(streams_of[6], (D, D), D ** -0.5, 0.21875, ((1, 2),))
    w_value = gaussian(streams_of[7], (D, D), D ** -0.5, 0.21875, ((1, 2),))
    b_value = gaussian(streams_of[8], (D,), 0.5, 3.0, ((0, 2),), jnp.float32)
    w_attn_out = gaussian(streams_of[9], (D, D), (D // 64) ** -0.5, 1.75, ((0, 2),))
    b_attn_out = gaussian(streams_of[10], (D,), 0.5, 3.0, ((0, 2),), jnp.float32)
    gain_one = jnp.clip(1.0 + 0.1 * jax.random.normal(streams_of[11], (D,), jnp.float32), 0.5, 1.5)
    shift_one = gaussian(streams_of[12], (D,), 0.5, 3.0, ((0, 2),), jnp.float32)
    w_up = gaussian(streams_of[13], (D, FF), D ** -0.5, 0.21875, ((1, 2),))
    b_up = gaussian(streams_of[14], (FF,), 0.5, 3.0, ((0, 2),), jnp.float32)
    w_down = gaussian(streams_of[15], (FF, D), (FF // 4) ** -0.5, 0.21875, ((0, 2),))
    b_down = gaussian(streams_of[16], (D,), 0.5, 3.0, ((0, 2),), jnp.float32)
    gain_two = jnp.clip(1.0 + 0.1 * jax.random.normal(streams_of[17], (D,), jnp.float32), 0.5, 1.5)
    shift_two = gaussian(streams_of[18], (D,), 0.5, 3.0, ((0, 2),), jnp.float32)
    head_alpha = jnp.clip(-3.0 + 8.0 * jax.random.uniform(streams_of[19], (HEADS,), jnp.float32) ** levels(streams_of[19], (HEADS,), ((0, 2),), -0.2, 0.2), -3.0, 5.0)
    mha_alpha = jnp.clip(jax.random.uniform(streams_of[20], (1,), jnp.float32, -0.3, 0.7), -0.3, 0.7)
    unit_alpha = jnp.clip(-3.0 + 8.0 * jax.random.uniform(streams_of[21], (FF,), jnp.float32) ** levels(streams_of[21], (FF,), ((0, 2),), -0.2, 0.2), -3.0, 5.0)
    ffn_alpha = jnp.clip(jax.random.uniform(streams_of[22], (1,), jnp.float32, -0.3, 0.7), -0.3, 0.7)
    hidden_alpha = jnp.clip(-2.0 + 7.0 * jax.random.uniform(streams_of[23], (D,), jnp.float32) ** levels(streams_of[23], (D,), ((0, 2),), -0.2, 0.2), -2.0, 5.0)
    head_noise = jnp.clip(0.05 + 0.9 * jax.random.uniform(streams_of[24], (HEADS,), jnp.float32) ** levels(streams_of[24], (HEADS,), ((0, 2),), -0.2, 0.2), 0.05, 0.95)
    mha_noise = jnp.clip(jax.random.uniform(streams_of[25], (1,), jnp.float32, 0.3, 0.7), 0.3, 0.7)
    unit_noise = jnp.clip(0.05 + 0.9 * jax.random.uniform(streams_of[26], (FF,), jnp.float32) ** levels(streams_of[26], (FF,), ((0, 2),), -0.2, 0.2), 0.05, 0.95)
    ffn_noise = jnp.clip(jax.random.uniform(streams_of[27], (1,), jnp.float32, 0.3, 0.7), 0.3, 0.7)
    hidden_noise = jnp.clip(0.05 + 0.9 * jax.random.uniform(streams_of[28], (D,), jnp.float32) ** levels(streams_of[28], (D,), ((0, 2),), -0.2, 0.2), 0.05, 0.95)
    lagrange = jnp.clip(jax.random.uniform(streams_of[29], (2,), jnp.float32, 1.0, 4.0), 1.0, 4.0)
    return dict(hidden_in=hidden_in, teacher=teacher, segment_ids=segment_ids, valid_mask=valid_mask, w_query=w_query, b_query=b_query, w_key=w_key, w_value=w_value, b_value=b_value, w_attn_out=w_attn_out, b_attn_out=b_attn_out, gain_one=gain_one, shift_one=shift_one, w_up=w_up, b_up=b_up, w_down=w_down, b_down=b_down, gain_two=gain_two, shift_two=shift_two, head_alpha=head_alpha, mha_alpha=mha_alpha, unit_alpha=unit_alpha, ffn_alpha=ffn_alpha, hidden_alpha=hidden_alpha, head_noise=head_noise, mha_noise=mha_noise, unit_noise=unit_noise, ffn_noise=ffn_noise, hidden_noise=hidden_noise, lagrange=lagrange)


@jax.custom_vjp
def low(v):
    return lax.optimization_barrier(v.astype(jnp.bfloat16)).astype(jnp.float32)

@jax.custom_vjp
def low_back(v):
    return v

def low_keep(v):
    return (low(v), None)

def low_pass(kept, grad):
    return (grad,)

def back_keep(v):
    return (v, None)

def back_low(kept, grad):
    return (low(grad),)
low.defvjp(low_keep, low_pass)
low_back.defvjp(back_keep, back_low)
norm_eps = 1e-05
gate_temper = 2.0 / 3.0
stretch_low = -0.1
stretch_high = 1.1
target_share = 0.4
masked_score = -1000000000.0

def hard_concrete(gate_noise, log_alpha):
    relaxed = jax.nn.sigmoid((jnp.log(gate_noise) - jnp.log(1.0 - gate_noise) + log_alpha) / gate_temper)
    return jnp.clip(relaxed * (stretch_high - stretch_low) + stretch_low, 0.0, 1.0)

def open_share(log_alpha):
    return jax.nn.sigmoid(log_alpha - gate_temper * math.log(-stretch_low / stretch_high))

def lagrangian(head_sum, unit_sum, hidden_sum, mha_alpha, ffn_alpha, lagrange):
    heads_kept = open_share(mha_alpha) * head_sum
    units_kept = open_share(ffn_alpha) * unit_sum
    kept_share = (4.0 * HD * heads_kept + 2.0 * units_kept) * hidden_sum / ((4.0 * D + 2.0 * FF) * D)
    share_gap = kept_share - target_share
    return (lagrange[0:1] * share_gap + lagrange[1:2] * share_gap * share_gap, kept_share)

def exact_dot(first, second):
    return jnp.dot(first, second, precision=lax.Precision.HIGHEST)

def layer_norm(resid, gain, shift):
    row_mean = lax.optimization_barrier(jnp.mean(resid, axis=1, keepdims=True))
    row_var = lax.optimization_barrier(jnp.mean(resid * resid, axis=1, keepdims=True)) - row_mean * row_mean
    return (resid - row_mean) * lax.rsqrt(row_var + norm_eps) * gain + shift

def attend_block(query_block, key_block, value_block, segment, valid):
    row_count = query_block.shape[0]
    head_count = query_block.shape[1] // HD
    query_heads = query_block.reshape(row_count, head_count, HD)
    key_heads = key_block.reshape(row_count, head_count, HD)
    value_heads = value_block.reshape(row_count, head_count, HD)
    raw_scores = low_back(jnp.einsum('qhd,khd->hqk', query_heads, key_heads, precision=lax.Precision.HIGHEST))
    allowed = (segment[:, None] == segment[None, :]) & ((valid[None, :] == 1) | (valid[:, None] == 0))
    scores = jnp.where(allowed[None], raw_scores * HD ** (-0.5), masked_score)
    attn_probs = low(jax.nn.softmax(scores, axis=-1))
    context = low_back(jnp.einsum('hqk,khd->qhd', attn_probs, value_heads, precision=lax.Precision.HIGHEST))
    return context.reshape(row_count, head_count * HD)

def attention(query, key_proj, value, segment_ids, valid_mask):
    count = query.shape[0] // BLOCK
    block_step = jax.checkpoint(attend_block)

    def to_blocks(values_in):
        return values_in.reshape((count, BLOCK) + values_in.shape[1:])

    def run_block(pieces):
        return block_step(pieces[0], pieces[1], pieces[2], pieces[3], pieces[4])
    result = lax.map(run_block, (to_blocks(query), to_blocks(key_proj), to_blocks(value), to_blocks(segment_ids), to_blocks(valid_mask)))
    return result.reshape(query.shape[0], query.shape[1])

def reference(hidden_in, teacher, segment_ids, valid_mask, w_query, b_query, w_key, w_value, b_value, w_attn_out, b_attn_out, gain_one, shift_one, w_up, b_up, w_down, b_down, gain_two, shift_two, head_alpha, mha_alpha, unit_alpha, ffn_alpha, hidden_alpha, head_noise, mha_noise, unit_noise, ffn_noise, hidden_noise, lagrange):
    weights = tuple((item.astype(jnp.float32) for item in (hidden_in, w_query, b_query, w_key, w_value, b_value, w_attn_out, b_attn_out, gain_one, shift_one, w_up, b_up, w_down, b_down, gain_two, shift_two)))
    alphas = (head_alpha, mha_alpha, unit_alpha, ffn_alpha, hidden_alpha)
    noises = (head_noise, mha_noise, unit_noise, ffn_noise, hidden_noise)
    offsets = tuple((jnp.zeros_like(item) for item in alphas))
    target = teacher.astype(jnp.float32)
    valid_col = valid_mask.astype(jnp.float32)[:, None]

    def objective(weights, alphas, offsets):
        source, wt_query, bias_query, wt_key, wt_value, bias_value, wt_attn, bias_attn, gain_a, shift_a, wt_up, bias_up, wt_down, bias_down, gain_b, shift_b = weights
        head_gate = hard_concrete(noises[0], alphas[0]) + offsets[0]
        mha_gate = hard_concrete(noises[1], alphas[1]) + offsets[1]
        unit_gate = hard_concrete(noises[2], alphas[2]) + offsets[2]
        ffn_gate = hard_concrete(noises[3], alphas[3]) + offsets[3]
        hidden_gate = hard_concrete(noises[4], alphas[4]) + offsets[4]
        query = low(low_back(exact_dot(source, wt_query) + bias_query))
        key_proj = low(low_back(exact_dot(source, wt_key)))
        value = low(low_back(exact_dot(source, wt_value) + bias_value))
        context = attention(query, key_proj, value, segment_ids, valid_mask)
        gated_context = low(context * jnp.repeat(head_gate, HD))
        attn_sum = low_back(exact_dot(gated_context, wt_attn))
        hidden_one = layer_norm(source + (attn_sum + bias_attn) * mha_gate * hidden_gate, gain_a, shift_a) * hidden_gate
        pre_act = low_back(exact_dot(low(hidden_one), wt_up) + bias_up)
        mixed = low(jax.nn.gelu(pre_act, approximate=False) * unit_gate)
        ffn_out = low_back(exact_dot(mixed, wt_down))
        final = layer_norm(hidden_one + (ffn_out + bias_down) * ffn_gate * hidden_gate, gain_b, shift_b) * hidden_gate
        task_loss = 0.5 * jnp.sum(valid_col * (final - target) * (final - target))
        penalty, kept_share = lagrangian(jnp.sum(open_share(alphas[0])), jnp.sum(open_share(alphas[2])), jnp.sum(open_share(alphas[4])), alphas[1], alphas[3], lagrange)
        return (task_loss + penalty[0], (final, kept_share, penalty))
    total, back_fn, extras = jax.vjp(objective, weights, alphas, offsets, has_aux=True)
    grad_weights, grad_alphas, grad_gates = back_fn(jnp.ones_like(total))
    final, kept_share, penalty = extras
    return (final.astype(jnp.bfloat16), grad_weights[0], grad_weights[1], grad_weights[2], grad_weights[3], grad_weights[4], grad_weights[5], grad_weights[6], grad_weights[7], grad_weights[8], grad_weights[9], grad_weights[10], grad_weights[11], grad_weights[12], grad_weights[13], grad_weights[14], grad_weights[15], grad_gates[0], grad_gates[1], grad_gates[2], grad_gates[3], grad_gates[4], grad_alphas[0], grad_alphas[1], grad_alphas[2], grad_alphas[3], grad_alphas[4], kept_share, penalty)
```

```python
from functools import partial
import math

import jax
import jax.numpy as jnp
from jax import lax
from jax.sharding import PartitionSpec as P

D = 768
HD = 64
FF = 3072
BLOCK = 512


norm_eps = 1e-05
gate_temper = 2.0 / 3.0
stretch_low = -0.1
stretch_high = 1.1
target_share = 0.4
masked_score = -1000000000.0


def hard_concrete(gate_noise, log_alpha):
    relaxed = jax.nn.sigmoid(
        (jnp.log(gate_noise) - jnp.log(1.0 - gate_noise) + log_alpha) / gate_temper
    )
    return jnp.clip(relaxed * (stretch_high - stretch_low) + stretch_low, 0.0, 1.0)


def open_share(log_alpha):
    return jax.nn.sigmoid(log_alpha - gate_temper * math.log(-stretch_low / stretch_high))


def lagrangian(head_sum, unit_sum, hidden_sum, mha_alpha, ffn_alpha, lagrange):
    heads_kept = open_share(mha_alpha) * head_sum
    units_kept = open_share(ffn_alpha) * unit_sum
    kept_share = (
        (4.0 * HD * heads_kept + 2.0 * units_kept) * hidden_sum / ((4.0 * D + 2.0 * FF) * D)
    )
    share_gap = kept_share - target_share
    return (lagrange[0:1] * share_gap + lagrange[1:2] * share_gap * share_gap, kept_share)


def to_low(values_in):
    return values_in.astype(jnp.bfloat16)


def contract(first, second, first_dim, second_dim):
    return lax.dot_general(
        first, second, (((first_dim,), (second_dim,)), ((), ())), preferred_element_type=jnp.float32
    )


def column_sum(values_in):
    return jnp.sum(values_in, axis=0)


def block_scores(query_block, key_block, segment, valid):
    raw_scores = jnp.einsum(
        "qhd,khd->hqk", query_block, key_block, preferred_element_type=jnp.float32
    )
    allowed = (segment[:, None] == segment[None, :]) & (
        (valid[None, :] == 1) | (valid[:, None] == 0)
    )
    return jnp.where(allowed[None], raw_scores * HD ** (-0.5), masked_score)


def attend_forward(pieces):
    query_block, key_block, value_block, segment, valid = pieces
    scores = block_scores(query_block, key_block, segment, valid)
    row_top = jnp.max(scores, axis=2, keepdims=True)
    exp_total = jnp.sum(jnp.exp(scores - row_top), axis=2, keepdims=True)
    log_total = row_top + jnp.log(exp_total)
    low_probs = to_low(jnp.exp(scores - log_total))
    context = jnp.einsum("hqk,khd->qhd", low_probs, value_block, preferred_element_type=jnp.float32)
    return (context, log_total)


def attend_backward(pieces):
    query_block, key_block, value_block, segment, valid, log_total, grad_block = pieces
    scores = block_scores(query_block, key_block, segment, valid)
    exact_probs = jnp.exp(scores - log_total)
    low_probs = to_low(exact_probs)
    grad_value = jnp.einsum(
        "hqk,qhd->khd", low_probs, grad_block, preferred_element_type=jnp.float32
    )
    grad_probs = jnp.einsum(
        "qhd,khd->hqk", grad_block, value_block, preferred_element_type=jnp.float32
    )
    grad_scores = exact_probs * (
        grad_probs - jnp.sum(grad_probs * exact_probs, axis=2, keepdims=True)
    )
    grad_raw = to_low(grad_scores * HD ** (-0.5))
    grad_query = jnp.einsum("hqk,khd->qhd", grad_raw, key_block, preferred_element_type=jnp.float32)
    grad_key = jnp.einsum("hqk,qhd->khd", grad_raw, query_block, preferred_element_type=jnp.float32)
    return (grad_query, grad_key, grad_value)


def norm_forward(resid, model_width):
    norm_sums = lax.psum((jnp.sum(resid, axis=1), jnp.sum(resid * resid, axis=1)), "hid")
    row_mean = norm_sums[0] / model_width
    row_var = norm_sums[1] / model_width - row_mean * row_mean
    inv_scale = lax.rsqrt(row_var + norm_eps)
    return ((resid - row_mean[:, None]) * inv_scale[:, None], inv_scale)


def norm_backward(grad_normed, normed, inv_scale, model_width):
    back_sums = lax.psum(
        (jnp.sum(grad_normed, axis=1), jnp.sum(grad_normed * normed, axis=1)), "hid"
    )
    return inv_scale[:, None] * (
        grad_normed
        - back_sums[0][:, None] / model_width
        - normed * (back_sums[1][:, None] / model_width)
    )


def alpha_grad(gate_noise, log_alpha, grad_gate):
    _, gate_back = jax.vjp(hard_concrete, gate_noise, log_alpha)
    return gate_back(grad_gate)[1]


def open_grad(log_alpha, grad_total):
    _, open_back = jax.vjp(open_share, log_alpha)
    return open_back(jnp.broadcast_to(grad_total, log_alpha.shape))[0]


def swap_pairs(core_masks):
    rows, cores = lax.axis_size("rows"), lax.axis_size("hid")
    return [
        (row * cores + core, (row ^ core_masks[core]) * cores + core)
        for row in range(rows)
        for core in range(cores)
    ]


def swap(values_in, core_masks):
    return lax.ppermute(values_in, ("rows", "hid"), swap_pairs(core_masks))


def spread_masks():
    rest = lax.axis_size("rows") // 4
    masks = [4 * (2**k * 2 - 1) for k in range(rest.bit_length() - 1)]
    return [(masks[k], masks[len(masks) - 1 - k]) for k in range(len(masks))]


def add_low(first, second):
    return to_low(first.astype(jnp.float32) + second.astype(jnp.float32))


def sum_rows(part):
    core = lax.axis_index("hid")
    row = lax.axis_index("rows")
    low_bit, high_bit = row & 1, (row >> 1) & 1
    first_bit = jnp.where(core == 0, low_bit, high_bit)
    second_bit = jnp.where(core == 0, high_bit, low_bit)
    height, width = part.shape
    quarters = to_low(part).reshape(2, 2, height // 4, width)

    def pick(values_in, at):
        return lax.dynamic_index_in_dim(values_in, at, 0, keepdims=False)

    half = add_low(pick(quarters, first_bit), swap(pick(quarters, 1 - first_bit), (1, 2)))
    own = add_low(pick(half, second_bit), swap(pick(half, 1 - second_bit), (2, 1)))
    for core_masks in spread_masks():
        own = add_low(own, swap(own, core_masks))
    beside = swap(own, (2, 1))
    half = jnp.where(second_bit == 0, jnp.stack((own, beside)), jnp.stack((beside, own)))
    other = swap(half, (1, 2))
    whole = jnp.where(first_bit == 0, jnp.stack((half, other)), jnp.stack((other, half)))
    return whole.reshape(height, width).astype(jnp.float32)


def sum_small(values_in):
    for core_masks in [(1, 2), (2, 1)] + spread_masks():
        values_in = values_in + swap(values_in, core_masks)
    return values_in


def body(
    hidden_in,
    teacher,
    segment_ids,
    valid_mask,
    w_query,
    b_query,
    w_key,
    w_value,
    b_value,
    w_attn_out,
    b_attn_out,
    gain_one,
    shift_one,
    w_up,
    b_up,
    w_down,
    b_down,
    gain_two,
    shift_two,
    head_alpha,
    mha_alpha,
    unit_alpha,
    ffn_alpha,
    hidden_alpha,
    head_noise,
    mha_noise,
    unit_noise,
    ffn_noise,
    hidden_noise,
    lagrange,
):
    model_width = w_query.shape[0]
    row_count = hidden_in.shape[0]
    local_width = hidden_in.shape[1]
    head_count = local_width // HD
    blocks = row_count // BLOCK
    head_gate = hard_concrete(head_noise, head_alpha)
    mha_gate = hard_concrete(mha_noise, mha_alpha)
    unit_gate = hard_concrete(unit_noise, unit_alpha)
    ffn_gate = hard_concrete(ffn_noise, ffn_alpha)
    hidden_gate = hard_concrete(hidden_noise, hidden_alpha)
    head_cols = jnp.repeat(head_gate, HD)
    source = hidden_in.astype(jnp.float32)

    def to_blocks(values_in):
        return values_in.reshape(blocks, BLOCK, head_count, HD)

    block_segments = segment_ids.reshape(blocks, BLOCK)
    block_valid = valid_mask.reshape(blocks, BLOCK)
    inputs_full = lax.all_gather(hidden_in, "hid", axis=1, tiled=True)
    query_low = to_low(jnp.dot(inputs_full, w_query, preferred_element_type=jnp.float32) + b_query)
    key_low = to_low(jnp.dot(inputs_full, w_key, preferred_element_type=jnp.float32))
    value_low = to_low(jnp.dot(inputs_full, w_value, preferred_element_type=jnp.float32) + b_value)
    context, log_total = lax.map(
        attend_forward,
        (
            to_blocks(query_low),
            to_blocks(key_low),
            to_blocks(value_low),
            block_segments,
            block_valid,
        ),
    )
    context = context.reshape(row_count, local_width)
    gated_context = to_low(context * head_cols)
    attn_sum = lax.psum_scatter(
        jnp.dot(gated_context, w_attn_out, preferred_element_type=jnp.float32),
        "hid",
        scatter_dimension=1,
        tiled=True,
    )
    attn_biased = attn_sum + b_attn_out
    resid_one = source + attn_biased * mha_gate * hidden_gate
    normed_one, inv_one = norm_forward(resid_one, model_width)
    ln_one = normed_one * gain_one + shift_one
    hidden_one = ln_one * hidden_gate
    hidden_full = lax.all_gather(to_low(hidden_one), "hid", axis=1, tiled=True)
    pre_act = jnp.dot(hidden_full, w_up, preferred_element_type=jnp.float32) + b_up
    activated, gelu_back = jax.vjp(partial(jax.nn.gelu, approximate=False), pre_act)
    mixed_low = to_low(activated * unit_gate)
    ffn_out = lax.psum_scatter(
        jnp.dot(mixed_low, w_down, preferred_element_type=jnp.float32),
        "hid",
        scatter_dimension=1,
        tiled=True,
    )
    ffn_biased = ffn_out + b_down
    resid_two = hidden_one + ffn_biased * ffn_gate * hidden_gate
    normed_two, inv_two = norm_forward(resid_two, model_width)
    ln_two = normed_two * gain_two + shift_two
    final = ln_two * hidden_gate
    grad_final = (final - teacher.astype(jnp.float32)) * valid_mask.astype(jnp.float32)[:, None]
    grad_gate_hidden = column_sum(grad_final * ln_two)
    grad_ln_two = grad_final * hidden_gate
    grad_gain_two = column_sum(grad_ln_two * normed_two)
    grad_shift_two = column_sum(grad_ln_two)
    grad_resid_two = norm_backward(grad_ln_two * gain_two, normed_two, inv_two, model_width)
    grad_gate_hidden = grad_gate_hidden + column_sum(grad_resid_two * ffn_biased * ffn_gate)
    ffn_scalar = jnp.reshape(jnp.sum(grad_resid_two * ffn_biased * hidden_gate), (1,))
    grad_ffn = grad_resid_two * ffn_gate * hidden_gate
    grad_b_down = column_sum(grad_ffn)
    grad_ffn_full = lax.all_gather(to_low(grad_ffn), "hid", axis=1, tiled=True)
    grad_mixed = contract(grad_ffn_full, w_down, 1, 1)
    grad_w_down = contract(mixed_low, grad_ffn_full, 0, 0)
    grad_gate_unit = column_sum(grad_mixed * activated)
    grad_pre = to_low(gelu_back(grad_mixed * unit_gate)[0])
    grad_b_up = column_sum(grad_pre.astype(jnp.float32))
    grad_w_up = contract(hidden_full, grad_pre, 0, 0)
    grad_hidden_part = lax.psum_scatter(
        contract(grad_pre, w_up, 1, 1), "hid", scatter_dimension=1, tiled=True
    )
    grad_hidden_one = grad_resid_two + grad_hidden_part
    grad_gate_hidden = grad_gate_hidden + column_sum(grad_hidden_one * ln_one)
    grad_ln_one = grad_hidden_one * hidden_gate
    grad_gain_one = column_sum(grad_ln_one * normed_one)
    grad_shift_one = column_sum(grad_ln_one)
    grad_resid_one = norm_backward(grad_ln_one * gain_one, normed_one, inv_one, model_width)
    grad_gate_hidden = grad_gate_hidden + column_sum(grad_resid_one * attn_biased * mha_gate)
    mha_scalar = jnp.reshape(jnp.sum(grad_resid_one * attn_biased * hidden_gate), (1,))
    grad_attn = grad_resid_one * mha_gate * hidden_gate
    grad_b_attn_out = column_sum(grad_attn)
    grad_attn_full = lax.all_gather(to_low(grad_attn), "hid", axis=1, tiled=True)
    grad_context = contract(grad_attn_full, w_attn_out, 1, 1)
    grad_w_attn_out = contract(gated_context, grad_attn_full, 0, 0)
    grad_gate_head = jnp.sum(
        (grad_context * context).reshape(row_count, head_count, HD), axis=(0, 2)
    )
    grad_context_low = to_low(grad_context * head_cols)
    grad_q, grad_k, grad_v = lax.map(
        attend_backward,
        (
            to_blocks(query_low),
            to_blocks(key_low),
            to_blocks(value_low),
            block_segments,
            block_valid,
            log_total,
            to_blocks(grad_context_low),
        ),
    )
    grad_query = to_low(grad_q.reshape(row_count, local_width))
    grad_key = to_low(grad_k.reshape(row_count, local_width))
    grad_value = to_low(grad_v.reshape(row_count, local_width))
    grad_b_query = column_sum(grad_query.astype(jnp.float32))
    grad_b_value = column_sum(grad_value.astype(jnp.float32))
    grad_w_query = contract(inputs_full, grad_query, 0, 0)
    grad_w_key = contract(inputs_full, grad_key, 0, 0)
    grad_w_value = contract(inputs_full, grad_value, 0, 0)
    back_sum = (
        contract(grad_query, w_query, 1, 1)
        + contract(grad_key, w_key, 1, 1)
        + contract(grad_value, w_value, 1, 1)
    )
    grad_input = grad_resid_one + lax.psum_scatter(
        back_sum.astype(jnp.bfloat16), "hid", scatter_dimension=1, tiled=True
    ).astype(jnp.float32)
    small_parts = (
        grad_b_up,
        grad_b_down,
        grad_gain_two,
        grad_shift_two,
        grad_gate_unit,
        ffn_scalar,
        grad_b_query,
        grad_b_value,
        grad_b_attn_out,
        grad_gain_one,
        grad_shift_one,
        grad_gate_head,
        grad_gate_hidden,
        mha_scalar,
    )
    small = sum_small(jnp.concatenate(small_parts))
    sums = []
    start = 0
    for part in small_parts:
        sums.append(small[start : start + part.shape[0]])
        start += part.shape[0]
    (
        sum_b_up,
        sum_b_down,
        sum_gain_two,
        sum_shift_two,
        sum_gate_unit,
        sum_ffn_scalar,
        sum_b_query,
        sum_b_value,
        sum_b_attn_out,
        sum_gain_one,
        sum_shift_one,
        sum_gate_head,
        sum_gate_hidden,
        sum_mha_scalar,
    ) = sums
    sum_w_down = sum_rows(grad_w_down)
    sum_w_up = sum_rows(grad_w_up)
    attn_width = grad_w_attn_out.shape[0]
    attn_chunk = jnp.concatenate(
        (
            grad_w_query,
            grad_w_key,
            grad_w_value,
            grad_w_attn_out[:, :attn_width],
            grad_w_attn_out[:, attn_width:],
        ),
        axis=0,
    )
    attn_sums = sum_rows(attn_chunk)
    sum_w_query = attn_sums[:model_width]
    sum_w_key = attn_sums[model_width : 2 * model_width]
    sum_w_value = attn_sums[2 * model_width : 3 * model_width]
    sum_w_attn_out = jnp.concatenate(
        (attn_sums[3 * model_width : 3 * model_width + attn_width], attn_sums[3 * model_width + attn_width :]), axis=1
    )
    gate_sums = lax.psum(
        (
            sum_mha_scalar,
            sum_ffn_scalar,
            jnp.sum(open_share(head_alpha)),
            jnp.sum(open_share(unit_alpha)),
            jnp.sum(open_share(hidden_alpha)),
        ),
        "hid",
    )
    grad_mha_gate, grad_ffn_gate, head_sum, unit_sum, hidden_sum = gate_sums

    def penalty_part(head_total, unit_total, hidden_total, mha_log, ffn_log):
        return lagrangian(head_total, unit_total, hidden_total, mha_log, ffn_log, lagrange)

    penalty, penalty_back, kept_share = jax.vjp(
        penalty_part, head_sum, unit_sum, hidden_sum, mha_alpha, ffn_alpha, has_aux=True
    )
    grad_head_sum, grad_unit_sum, grad_hidden_sum, grad_mha_open, grad_ffn_open = penalty_back(
        jnp.ones_like(penalty)
    )
    grad_head_alpha = alpha_grad(head_noise, head_alpha, sum_gate_head) + open_grad(
        head_alpha, grad_head_sum
    )
    grad_unit_alpha = alpha_grad(unit_noise, unit_alpha, sum_gate_unit) + open_grad(
        unit_alpha, grad_unit_sum
    )
    grad_hidden_alpha = alpha_grad(hidden_noise, hidden_alpha, sum_gate_hidden) + open_grad(
        hidden_alpha, grad_hidden_sum
    )
    grad_mha_alpha = alpha_grad(mha_noise, mha_alpha, grad_mha_gate) + grad_mha_open
    grad_ffn_alpha = alpha_grad(ffn_noise, ffn_alpha, grad_ffn_gate) + grad_ffn_open
    return (
        final.astype(jnp.bfloat16),
        grad_input,
        sum_w_query,
        sum_b_query,
        sum_w_key,
        sum_w_value,
        sum_b_value,
        sum_w_attn_out,
        sum_b_attn_out,
        sum_gain_one,
        sum_shift_one,
        sum_w_up,
        sum_b_up,
        sum_w_down,
        sum_b_down,
        sum_gain_two,
        sum_shift_two,
        sum_gate_head,
        grad_mha_gate,
        sum_gate_unit,
        grad_ffn_gate,
        sum_gate_hidden,
        grad_head_alpha,
        grad_mha_alpha,
        grad_unit_alpha,
        grad_ffn_alpha,
        grad_hidden_alpha,
        kept_share,
        penalty,
    )


def solution(mesh):
    in_specs = (
        P("rows", "hid"),
        P("rows", "hid"),
        P("rows"),
        P("rows"),
        P(None, "hid"),
        P("hid"),
        P(None, "hid"),
        P(None, "hid"),
        P("hid"),
        P("hid", None),
        P("hid"),
        P("hid"),
        P("hid"),
        P(None, "hid"),
        P("hid"),
        P("hid", None),
        P("hid"),
        P("hid"),
        P("hid"),
        P("hid"),
        P(),
        P("hid"),
        P(),
        P("hid"),
        P("hid"),
        P(),
        P("hid"),
        P(),
        P("hid"),
        P(),
    )
    out_specs = (
        P("rows", "hid"),
        P("rows", "hid"),
        P(None, "hid"),
        P("hid"),
        P(None, "hid"),
        P(None, "hid"),
        P("hid"),
        P("hid", None),
        P("hid"),
        P("hid"),
        P("hid"),
        P(None, "hid"),
        P("hid"),
        P("hid", None),
        P("hid"),
        P("hid"),
        P("hid"),
        P("hid"),
        P(),
        P("hid"),
        P(),
        P("hid"),
        P("hid"),
        P(),
        P("hid"),
        P(),
        P("hid"),
        P(),
        P(),
    )
    return jax.shard_map(body, mesh=mesh, in_specs=in_specs, out_specs=out_specs, check_vma=False)
```

```python
from functools import partial
import math

import jax
import jax.numpy as jnp
from jax import lax
from jax.experimental import pallas as pl
from jax.experimental.pallas import tpu as pltpu
from jax.sharding import PartitionSpec as P

HD = 64
BLOCK = 512
LANES = 128
TILE = 512

norm_eps = 1e-05
gate_temper = 2.0 / 3.0
stretch_low = -0.1
stretch_high = 1.1
target_share = 0.4
masked_score = -1000000000.0
open_shift = gate_temper * math.log(-stretch_low / stretch_high)
vmem_bytes = 58 * 2**20

f32 = jnp.float32
bf16 = jnp.bfloat16


def to_low(values_in):
    return values_in.astype(bf16)


def contract(first, second, first_dim, second_dim):
    return lax.dot_general(
        first, second, (((first_dim,), (second_dim,)), ((), ())), preferred_element_type=f32
    )


def column_sum(values_in):
    return jnp.sum(values_in, axis=0, keepdims=True)


def row_sum(values_in):
    return jnp.sum(values_in, axis=1, keepdims=True)


def sigmoid(values_in):
    return 1.0 / (1.0 + jnp.exp(-values_in))


def stretched(gate_noise, log_alpha):
    relaxed = sigmoid(
        (jnp.log(gate_noise) - jnp.log(1.0 - gate_noise) + log_alpha) / gate_temper
    )
    return relaxed, relaxed * (stretch_high - stretch_low) + stretch_low


def hard_concrete(gate_noise, log_alpha):
    return jnp.clip(stretched(gate_noise, log_alpha)[1], 0.0, 1.0)


def gate_slope(gate_noise, log_alpha):
    relaxed, wide = stretched(gate_noise, log_alpha)
    slope = relaxed * (1.0 - relaxed) * ((stretch_high - stretch_low) / gate_temper)
    return jnp.where((wide > 0.0) & (wide < 1.0), slope, 0.0)


def open_share(log_alpha):
    return sigmoid(log_alpha - open_shift)


class Pack:
    def __init__(self, width, units):
        self.width, self.units = width, units
        at = 0
        for name in ("b_query", "b_value", "b_attn_out", "gain_one", "shift_one"):
            setattr(self, name, (at, width))
            at += width
        for name in ("b_down", "gain_two", "shift_two", "hidden_alpha", "hidden_noise"):
            setattr(self, name, (at, width))
            at += width
        for name in ("b_up", "unit_alpha", "unit_noise"):
            setattr(self, name, (at, units))
            at += units
        for name in ("head_alpha", "head_noise", "scalars"):
            setattr(self, name, (at, LANES))
            at += LANES
        self.total = at


def take(pack_ref, spot):
    return pack_ref[:, spot[0] : spot[0] + spot[1]]


def natural(core, own, peer):
    at_peer = core.astype(f32)
    at_own = 1.0 - at_peer
    return jnp.concatenate((own * at_own + peer * at_peer, peer * at_own + own * at_peer), axis=1)


def both(core, own_ref, peer_ref, spot):
    return natural(core, take(own_ref, spot), take(peer_ref, spot))


def hidden_gates(core, pack, own_ref, peer_ref):
    return hard_concrete(
        both(core, own_ref, peer_ref, pack.hidden_noise),
        both(core, own_ref, peer_ref, pack.hidden_alpha),
    )


def head_row(pack, own_ref, peer_ref, heads):
    parts = []
    for ref in (own_ref, peer_ref):
        gates = hard_concrete(take(ref, pack.head_noise), take(ref, pack.head_alpha))
        for at in range(heads):
            parts.append(jnp.broadcast_to(gates[:, at : at + 1], (1, HD)))
    return jnp.concatenate(parts, axis=1)


def scalar_gate(pack, own_ref, at):
    numbers = take(own_ref, pack.scalars)
    return hard_concrete(numbers[:, at + 1 : at + 2], numbers[:, at : at + 1])


def half_mask(side, dtype):
    lane = lax.broadcasted_iota(jnp.int32, (1, LANES), 1)
    inside = (lane < HD) if side == 0 else (lane >= HD)
    return jnp.where(inside, 1.0, 0.0).astype(dtype)


def pick_half(first, second):
    lane = lax.broadcasted_iota(jnp.int32, (1, LANES), 1)
    return jnp.where(lane < HD, first, second)


def norm_back(grad_normed, normed, inv_scale):
    width = normed.shape[1]
    mean_grad = row_sum(grad_normed) * (1.0 / width)
    mean_both = row_sum(grad_normed * normed) * (1.0 / width)
    return inv_scale * (grad_normed - mean_grad - normed * mean_both)


def norm_forward(resid):
    width = resid.shape[1]
    row_mean = row_sum(resid) * (1.0 / width)
    row_var = row_sum(resid * resid) * (1.0 / width) - row_mean * row_mean
    inv_scale = lax.rsqrt(row_var + norm_eps)
    return (resid - row_mean) * inv_scale, inv_scale


def own_rows(ref, core):
    return ref[pl.ds(pl.multiple_of(core * BLOCK, BLOCK), BLOCK), :]


def attend_kernel(
    pack,
    core_ref,
    x_own,
    x_peer,
    wq_own,
    wk_own,
    wv_own,
    wq_peer,
    wk_peer,
    wv_peer,
    wa_own,
    wa_peer,
    pack_own,
    pack_peer,
    segments,
    valid,
    weights_out,
    query_out,
    key_out,
    value_out,
    context_out,
    gated_own_out,
    gated_peer_out,
    stats_out,
    biased_out,
    normed_out,
    hidden_out,
    x_nat,
    mask_bias,
    gate_row,
    gated,
):
    pair = pl.program_id(0)
    core = core_ref[0]
    width = pack.width
    heads = width // HD

    @pl.when(pair == 0)
    def _():
        own_at = pl.multiple_of(core * width, LANES)
        peer_at = pl.multiple_of((1 - core) * width, LANES)
        x_nat[:, pl.ds(own_at, width)] = own_rows(x_own, core)
        x_nat[:, pl.ds(peer_at, width)] = own_rows(x_peer, core)
        source = x_nat[...]
        for at, query_ref, key_ref, value_ref, row in (
            (0, wq_own, wk_own, wv_own, pack_own),
            (width, wq_peer, wk_peer, wv_peer, pack_peer),
        ):
            query = to_low(contract(source, query_ref[...], 1, 0) + take(row, pack.b_query))
            query_out[:, at : at + width] = query * jnp.asarray(HD ** (-0.5), bf16)
            key_out[:, at : at + width] = to_low(contract(source, key_ref[...], 1, 0))
            value_out[:, at : at + width] = to_low(
                contract(source, value_ref[...], 1, 0) + take(row, pack.b_value)
            )
        gate_row[...] = head_row(pack, pack_own, pack_peer, heads)

        lanes_of = BLOCK // LANES
        start = core * lanes_of

        def line(ref):
            return jnp.concatenate(
                [ref[pl.ds(start + at, 1), :] for at in range(lanes_of)], axis=1
            ).astype(f32)

        segment_line, valid_line = line(segments), line(valid)
        segment_side = jnp.broadcast_to(segment_line, (LANES, BLOCK)).T[:, 0:1]
        valid_side = jnp.broadcast_to(valid_line, (LANES, BLOCK)).T[:, 0:1]
        allowed = (segment_side == segment_line) & ((valid_line == 1.0) | (valid_side == 0.0))
        mask_bias[...] = jnp.where(allowed, 0.0, masked_score)

    columns = pl.ds(pl.multiple_of(pair * LANES, LANES), LANES)
    query, key, value = query_out[:, columns], key_out[:, columns], value_out[:, columns]
    ones = jnp.ones((BLOCK, LANES), bf16)
    value_wide = jnp.concatenate((value, ones), axis=1)
    contexts = []
    lane = lax.broadcasted_iota(jnp.int32, (1, LANES), 1)
    stats = stats_out[...]
    for side in range(2):
        scores = contract(query * half_mask(side, bf16), key, 1, 1) + mask_bias[...]
        row_top = jnp.max(scores, axis=1, keepdims=True)
        weights = to_low(jnp.exp(scores - row_top))
        weights_out[side] = weights
        summed = contract(weights, value_wide, 1, 0)
        inverse = 1.0 / summed[:, LANES : 2 * LANES]
        contexts.append(summed[:, :LANES] * inverse)
        stats = jnp.where(lane == 2 * pair + side, inverse, stats)
    stats_out[...] = stats
    context = pick_half(contexts[0], contexts[1])
    context_out[:, columns] = to_low(context)
    gated[:, columns] = to_low(context * gate_row[:, columns])

    @pl.when(pair == pl.num_programs(0) - 1)
    def _():
        gated_own, gated_peer = gated[:, :width], gated[:, width:]
        gated_own_out[...] = gated_own
        gated_peer_out[...] = gated_peer
        attn_sum = contract(gated_own, wa_own[...], 1, 0) + contract(gated_peer, wa_peer[...], 1, 0)
        biased = attn_sum + both(core, pack_own, pack_peer, pack.b_attn_out)
        biased_out[...] = biased
        gates = hidden_gates(core, pack, pack_own, pack_peer)
        mha_gate = scalar_gate(pack, pack_own, 0)
        resid = x_nat[...].astype(f32) + biased * (mha_gate * gates)
        normed, inv_scale = norm_forward(resid)
        normed_out[...] = normed
        gain = both(core, pack_own, pack_peer, pack.gain_one)
        shift = both(core, pack_own, pack_peer, pack.shift_one)
        hidden_out[...] = to_low((normed * gain + shift) * gates)
        stats_out[...] = jnp.where(lane == LANES - 1, inv_scale, stats)


def gelu_parts(pre_act):
    size = jnp.abs(pre_act) * (0.5**0.5)
    inverse = 1.0 / (1.0 + 0.3275911 * size)
    falling = jnp.exp(-size * size)
    poly = 1.061405429 * inverse - 1.453152027
    poly = poly * inverse + 1.421413741
    poly = poly * inverse - 0.284496736
    poly = poly * inverse + 0.254829592
    tail = 0.5 * poly * inverse * falling
    return jnp.where(pre_act >= 0.0, 1.0 - tail, tail), falling * (1.0 / math.sqrt(2.0 * math.pi))


def ffn_forward_kernel(
    pack,
    core_ref,
    hidden,
    normed,
    up_own,
    up_peer,
    down_own,
    down_peer,
    pack_own,
    pack_peer,
    teacher_own,
    teacher_peer,
    valid,
    mixed_own_out,
    mixed_peer_out,
    active_out,
    slope_out,
    output_own,
    output_peer,
    grad_resid_out,
    grad_ffn_out,
    sums_out,
    total,
):
    step = pl.program_id(0)
    core = core_ref[0]
    own_steps = pl.num_programs(0) // 2
    width, units = pack.width, pack.units

    def tile(at, up_ref, down_ref, pack_ref, mixed_ref):
        spot = pl.multiple_of(at * TILE, TILE)

        def cut(place):
            return pack_ref[:, pl.ds(place[0] + spot, TILE)]

        pre_act = contract(hidden[...], up_ref[...], 1, 0) + cut(pack.b_up)
        whole, density = gelu_parts(pre_act)
        active = pre_act * whole
        unit_gate = hard_concrete(cut(pack.unit_noise), cut(pack.unit_alpha))
        mixed = to_low(active * unit_gate)
        mixed_ref[...] = mixed
        active_out[...] = to_low(active)
        slope_out[...] = to_low((whole + pre_act * density) * unit_gate)
        return contract(mixed, down_ref[...], 1, 0)

    @pl.when(step == 0)
    def _():
        total[...] = tile(step, up_own, down_own, pack_own, mixed_own_out)

    @pl.when((step > 0) & (step < own_steps))
    def _():
        total[...] += tile(step, up_own, down_own, pack_own, mixed_own_out)

    @pl.when(step >= own_steps)
    def _():
        total[...] += tile(step - own_steps, up_peer, down_peer, pack_peer, mixed_peer_out)

    @pl.when(step == pl.num_programs(0) - 1)
    def _():
        gates = hidden_gates(core, pack, pack_own, pack_peer)
        ffn_gate = scalar_gate(pack, pack_own, 2)

        def vector(spot):
            return both(core, pack_own, pack_peer, spot)

        biased = total[...] + vector(pack.b_down)
        hidden_one = (normed[...] * vector(pack.gain_one) + vector(pack.shift_one)) * gates
        normed_two, inv_two = norm_forward(hidden_one + biased * (ffn_gate * gates))
        gain = vector(pack.gain_two)
        final = (normed_two * gain + vector(pack.shift_two)) * gates
        final_low = to_low(final)

        def split(own_ref, peer_ref, values_in):
            @pl.when(core == 0)
            def _():
                own_ref[...] = values_in[:, :width]
                peer_ref[...] = values_in[:, width:]

            @pl.when(core == 1)
            def _():
                own_ref[...] = values_in[:, width:]
                peer_ref[...] = values_in[:, :width]

        split(output_own, output_peer, final_low)
        lanes_of = BLOCK // LANES
        start = core * lanes_of
        valid_line = jnp.concatenate(
            [valid[pl.ds(start + at, 1), :] for at in range(lanes_of)], axis=1
        ).astype(f32)
        valid_side = jnp.broadcast_to(valid_line, (LANES, BLOCK)).T[:, 0:1]
        own_at = pl.multiple_of(core * width, LANES)
        peer_at = pl.multiple_of((1 - core) * width, LANES)
        grad_resid_out[:, pl.ds(own_at, width)] = own_rows(teacher_own, core).astype(f32)
        grad_resid_out[:, pl.ds(peer_at, width)] = own_rows(teacher_peer, core).astype(f32)
        grad_final = (final - grad_resid_out[...]) * valid_side
        grad_resid = norm_back(grad_final * (gates * gain), normed_two, inv_two)
        grad_resid_out[...] = grad_resid
        grad_ffn_out[...] = to_low(grad_resid * (ffn_gate * gates))
        sums_out[0:1, :] = column_sum(grad_final * normed_two)
        sums_out[1:2, :] = column_sum(grad_final)
        sums_out[2:3, :] = column_sum(grad_resid * biased)
        sums_out[3:4, :] = column_sum(grad_resid)


def ffn_backward_kernel(
    pack,
    core_ref,
    grad_ffn,
    grad_resid_two,
    normed,
    biased,
    stats,
    active,
    slope,
    up_own,
    up_peer,
    down_own,
    down_peer,
    pack_own,
    pack_peer,
    grad_pre_own,
    grad_pre_peer,
    grad_resid_out,
    grad_attn_out,
    sums_out,
    unit_sums_out,
    total,
):
    step = pl.program_id(0)
    core = core_ref[0]
    own_steps = pl.num_programs(0) // 2
    units = pack.units

    def tile(at, side, up_ref, down_ref, pre_ref):
        grad_mixed = contract(grad_ffn[...], down_ref[...], 1, 1)
        grad_pre = to_low(grad_mixed * slope[...].astype(f32))
        pre_ref[...] = grad_pre
        spot = pl.multiple_of(side * units + at * TILE, TILE)
        unit_sums_out[0:1, pl.ds(spot, TILE)] = column_sum(grad_mixed * active[...].astype(f32))
        unit_sums_out[1:2, pl.ds(spot, TILE)] = column_sum(grad_pre.astype(f32))
        return contract(grad_pre, up_ref[...], 1, 1)

    @pl.when(step == 0)
    def _():
        total[...] = grad_resid_two[...] + tile(step, core, up_own, down_own, grad_pre_own)

    @pl.when((step > 0) & (step < own_steps))
    def _():
        total[...] += tile(step, core, up_own, down_own, grad_pre_own)

    @pl.when(step >= own_steps)
    def _():
        total[...] += tile(step - own_steps, 1 - core, up_peer, down_peer, grad_pre_peer)

    @pl.when(step == pl.num_programs(0) - 1)
    def _():
        gates = hidden_gates(core, pack, pack_own, pack_peer)
        mha_gate = scalar_gate(pack, pack_own, 0)
        gain = both(core, pack_own, pack_peer, pack.gain_one)
        grad_hidden = total[...]
        sums_out[0:1, :] = column_sum(grad_hidden * normed[...])
        sums_out[1:2, :] = column_sum(grad_hidden)
        inv_scale = stats[:, LANES - 1 : LANES]
        grad_resid = norm_back(grad_hidden * (gates * gain), normed[...], inv_scale)
        grad_resid_out[...] = grad_resid
        grad_attn_out[...] = to_low(grad_resid * (mha_gate * gates))
        sums_out[2:3, :] = column_sum(grad_resid * biased[...])
        sums_out[3:4, :] = column_sum(grad_resid)


def attend_back_kernel(
    pack,
    core_ref,
    weights,
    query_ref,
    key_ref,
    value_ref,
    context_ref,
    stats,
    grad_attn,
    wa_own,
    wa_peer,
    pack_own,
    pack_peer,
    grad_own_out,
    grad_peer_out,
    sums_out,
    gate_row,
):
    pair = pl.program_id(0)
    core = core_ref[0]
    width = pack.width
    own_pairs = pl.num_programs(0) // 2

    @pl.when(pair == 0)
    def _():
        gate_row[...] = head_row(pack, pack_own, pack_peer, width // HD)

    columns = pl.ds(pl.multiple_of(pair * LANES, LANES), LANES)
    lane = lax.broadcasted_iota(jnp.int32, (1, LANES), 1)

    def run(at, side_of, wa_ref, out_ref):
        query, key, value = query_ref[:, columns], key_ref[:, columns], value_ref[:, columns]
        context = context_ref[:, columns].astype(f32)
        grad_context = contract(grad_attn[...], wa_ref[...], 1, 1)
        spot = pl.ds(pl.multiple_of(side_of * width + at * LANES, LANES), LANES)
        sums_out[0:1, spot] = column_sum(grad_context * context)
        inverses = [
            row_sum(jnp.where(lane == 2 * pair + side, stats[...], 0.0)) for side in range(2)
        ]
        grad_low = to_low(grad_context * gate_row[:, columns] * pick_half(inverses[0], inverses[1]))
        product = grad_low.astype(f32) * context
        found = []
        for side in range(2):
            mask = half_mask(side, f32)
            level = row_sum(product * mask)
            grad_probs = contract(grad_low * mask.astype(bf16), value, 1, 1)
            chosen = weights[side]
            grad_raw = to_low(chosen.astype(f32) * (grad_probs - level))
            found.append(
                (
                    contract(grad_raw, key, 1, 0),
                    contract(grad_raw, query, 0, 0),
                    contract(chosen, grad_low, 0, 0),
                )
            )
        grad_query = to_low(pick_half(found[0][0], found[1][0]) * HD ** (-0.5))
        grad_key = to_low(pick_half(found[0][1], found[1][1]))
        grad_value = to_low(pick_half(found[0][2], found[1][2]))
        for place, grad in enumerate((grad_query, grad_key, grad_value)):
            at_lane = pl.multiple_of(place * width + at * LANES, LANES)
            out_ref[:, pl.ds(at_lane, LANES)] = grad
        sums_out[1:2, spot] = column_sum(grad_query.astype(f32))
        sums_out[2:3, spot] = column_sum(grad_value.astype(f32))

    @pl.when(pair < own_pairs)
    def _():
        run(pair, core, wa_own, grad_own_out)

    @pl.when(pair >= own_pairs)
    def _():
        run(pair - own_pairs, 1 - core, wa_peer, grad_peer_out)


def down_grad_kernel(half_ref, mixed, mixed_near, grad, grad_near, out_ref):
    summed = contract(mixed[...], grad[...], 0, 0) + contract(mixed_near[...], grad_near[...], 0, 0)
    out_ref[...] = to_low(summed)


def up_grad_kernel(half_ref, hidden, hidden_near, grad, grad_near, out_ref):
    summed = contract(hidden[...], grad[...], 0, 0) + contract(hidden_near[...], grad_near[...], 0, 0)
    out_ref[...] = to_low(summed)


def attend_grad_kernel(
    width,
    half_ref,
    core_ref,
    x_own,
    x_peer,
    grad,
    grad_near,
    gated,
    gated_near,
    grad_attn,
    grad_attn_near,
    out_ref,
):
    core = core_ref[0]
    half = half_ref[0]

    def from_source(x_ref, at, columns):
        rows = pl.ds(pl.multiple_of(at * width, LANES), width)
        summed = contract(own_rows(x_ref, core), grad[:, columns], 0, 0) + contract(
            own_rows(x_ref, 1 - core), grad_near[:, columns], 0, 0
        )
        for place in range(summed.shape[1] // width):
            out_ref[place, rows, :] = to_low(summed[:, place * width : (place + 1) * width])

    @pl.when(half == 0)
    def _():
        from_source(x_own, core, slice(0, 2 * width))
        from_source(x_peer, 1 - core, slice(0, 2 * width))

    @pl.when(half == 1)
    def _():
        from_source(x_own, core, slice(2 * width, 3 * width))
        from_source(x_peer, 1 - core, slice(2 * width, 3 * width))
        summed = contract(gated[...], grad_attn[...], 0, 0) + contract(
            gated_near[...], grad_attn_near[...], 0, 0
        )
        out_ref[1, :width, :] = to_low(summed[:, :width])
        out_ref[1, width:, :] = to_low(summed[:, width:])


def input_grad_kernel(
    width,
    core_ref,
    grad_resid,
    grad_own,
    grad_peer,
    wq_own,
    wk_own,
    wv_own,
    wq_peer,
    wk_peer,
    wv_peer,
    own_out,
    peer_out,
):
    core = core_ref[0]
    summed = grad_resid[...]
    for grad, weights in (
        (grad_own, (wq_own, wk_own, wv_own)),
        (grad_peer, (wq_peer, wk_peer, wv_peer)),
    ):
        for place, weight in enumerate(weights):
            summed = summed + contract(
                grad[:, place * width : (place + 1) * width], weight[...], 1, 1
            )

    @pl.when(core == 0)
    def _():
        own_out[...] = summed[:, :width]
        peer_out[...] = summed[:, width:]

    @pl.when(core == 1)
    def _():
        own_out[...] = summed[:, width:]
        peer_out[...] = summed[:, :width]


def place_kernel(bit_ref, half, other, out_ref):
    step = pl.program_id(0)

    @pl.when(step < 2)
    def _():
        out_ref[...] = half[...].astype(f32)

    @pl.when(step >= 2)
    def _():
        out_ref[...] = other[...].astype(f32)


def place_attend_kernel(bit_ref, half, other, query_out, key_out, value_out, attn_out):
    width = attn_out.shape[0]

    def put(first, second):
        query_out[...] = first[0].astype(f32)
        key_out[...] = first[1].astype(f32)
        value_out[...] = second[0].astype(f32)
        attn_out[:, :width] = second[1, :width, :].astype(f32)
        attn_out[:, width:] = second[1, width:, :].astype(f32)

    @pl.when(bit_ref[0] == 0)
    def _():
        put(half, other)

    @pl.when(bit_ref[0] == 1)
    def _():
        put(other, half)


def finish_kernel(
    pack,
    core_ref,
    sums,
    pack_own,
    pack_peer,
    b_query,
    b_value,
    b_attn_out,
    gain_one,
    shift_one,
    b_up,
    b_down,
    gain_two,
    shift_two,
    head_gate,
    mha_gate,
    unit_gate,
    ffn_gate,
    hidden_gate,
    head_alpha,
    mha_alpha,
    unit_alpha,
    ffn_alpha,
    hidden_alpha,
    share_out,
    penalty_out,
):
    core = core_ref[0]
    width, units = pack.width, pack.units
    columns = pl.ds(pl.multiple_of(core * width, LANES), width)
    heads = width // HD

    def own(row):
        return sums[row : row + 1, columns]

    def vector(spot):
        return take(pack_own, spot)

    gates = hard_concrete(vector(pack.hidden_noise), vector(pack.hidden_alpha))
    mha, ffn = scalar_gate(pack, pack_own, 0), scalar_gate(pack, pack_own, 2)
    gain_two[...] = gates * own(0)
    shift_two[...] = gates * own(1)
    b_down[...] = (ffn * gates) * own(3)
    gain_one[...] = gates * own(4)
    shift_one[...] = gates * own(5)
    b_attn_out[...] = (mha * gates) * own(7)
    b_query[...] = own(9)
    b_value[...] = own(10)
    grad_hidden = (
        vector(pack.gain_two) * own(0)
        + vector(pack.shift_two) * own(1)
        + ffn * own(2)
        + vector(pack.gain_one) * own(4)
        + vector(pack.shift_one) * own(5)
        + mha * own(6)
    )
    hidden_gate[...] = grad_hidden
    all_gates = hidden_gates(core, pack, pack_own, pack_peer)
    grad_ffn_gate = row_sum(all_gates * sums[2:3, :])
    grad_mha_gate = row_sum(all_gates * sums[6:7, :])
    ffn_gate[...] = grad_ffn_gate
    mha_gate[...] = grad_mha_gate

    unit_rows = units // (2 * width)

    def unit_line(first):
        at = first + core * unit_rows
        return jnp.concatenate([sums[pl.ds(at + k, 1), :] for k in range(unit_rows)], axis=1)

    grad_unit = unit_line(11)
    b_up[...] = unit_line(11 + 2 * unit_rows)
    unit_gate[...] = grad_unit
    by_head = own(8)
    lane = lax.broadcasted_iota(jnp.int32, (1, LANES), 1)
    grad_head = jnp.zeros((1, LANES), f32)
    for at in range(heads):
        grad_head = jnp.where(
            lane == at, row_sum(by_head[:, at * HD : (at + 1) * HD]), grad_head
        )
    head_gate[...] = grad_head[:, :heads]

    numbers = vector(pack.scalars)
    mha_open, ffn_open = open_share(numbers[:, 0:1]), open_share(numbers[:, 2:3])
    first_weight, second_weight = numbers[:, 4:5], numbers[:, 5:6]

    def open_total(spot, count):
        return row_sum(open_share(take(pack_own, spot)[:, :count])) + row_sum(
            open_share(take(pack_peer, spot)[:, :count])
        )

    head_sum = open_total(pack.head_alpha, heads)
    unit_sum = open_total(pack.unit_alpha, units)
    hidden_sum = open_total(pack.hidden_alpha, width)
    model, inner = 2.0 * width, 2.0 * units
    scale = 1.0 / ((4.0 * model + 2.0 * inner) * model)
    kept = 4.0 * HD * mha_open * head_sum + 2.0 * ffn_open * unit_sum
    share = kept * hidden_sum * scale
    gap = share - target_share
    share_out[...] = share
    penalty_out[...] = first_weight * gap + second_weight * gap * gap
    slope = (first_weight + 2.0 * second_weight * gap) * scale
    by_heads = slope * hidden_sum * (4.0 * HD)
    by_units = slope * hidden_sum * 2.0

    def alpha_grad(noise, alpha, grad_gate, grad_open):
        opened = open_share(alpha)
        return gate_slope(noise, alpha) * grad_gate + grad_open * (opened * (1.0 - opened))

    head_alpha[...] = alpha_grad(
        vector(pack.head_noise), vector(pack.head_alpha), grad_head, by_heads * mha_open
    )[:, :heads]
    unit_alpha[...] = alpha_grad(
        vector(pack.unit_noise), vector(pack.unit_alpha), grad_unit, by_units * ffn_open
    )
    hidden_alpha[...] = alpha_grad(
        vector(pack.hidden_noise), vector(pack.hidden_alpha), grad_hidden, slope * kept
    )
    mha_alpha[...] = alpha_grad(
        numbers[:, 1:2], numbers[:, 0:1], grad_mha_gate, by_heads * head_sum
    )
    ffn_alpha[...] = alpha_grad(
        numbers[:, 3:4], numbers[:, 2:3], grad_ffn_gate, by_units * unit_sum
    )


def full(shape):
    return pl.BlockSpec(shape, lambda *at: (0,) * len(shape))


def one_number():
    return pl.BlockSpec(memory_space=pltpu.SMEM)


def shaped(shape, dtype):
    return jax.ShapeDtypeStruct(shape, dtype)


def call(kernel, grid, in_specs, out_specs, out_shape, scratch, cost, args):
    return pl.pallas_call(
        kernel,
        grid=grid,
        in_specs=in_specs,
        out_specs=out_specs,
        out_shape=out_shape,
        scratch_shapes=scratch,
        compiler_params=pltpu.CompilerParams(vmem_limit_bytes=vmem_bytes),
        cost_estimate=pl.CostEstimate(
            flops=int(cost[0] * 1e9), bytes_accessed=int(cost[1] * 1e6), transcendentals=int(cost[2] * 1e6)
        ),
    )(*args)


def call_by_half(kernel, grid, in_specs, out_specs, out_shape, cost, half, args):
    return pl.pallas_call(
        kernel,
        grid_spec=pltpu.PrefetchScalarGridSpec(
            num_scalar_prefetch=1, grid=grid, in_specs=in_specs, out_specs=out_specs
        ),
        out_shape=out_shape,
        compiler_params=pltpu.CompilerParams(vmem_limit_bytes=vmem_bytes),
        cost_estimate=pl.CostEstimate(
            flops=int(cost[0] * 1e9), bytes_accessed=int(cost[1] * 1e6), transcendentals=0
        ),
    )(half, *args)


def swap_pairs(core_masks):
    rows, cores = lax.axis_size("rows"), lax.axis_size("hid")
    return [
        (row * cores + core, (row ^ core_masks[core]) * cores + core)
        for row in range(rows)
        for core in range(cores)
    ]


def swap(values_in, core_masks):
    return lax.ppermute(values_in, ("rows", "hid"), swap_pairs(core_masks))


def near(values_in):
    return lax.ppermute(values_in, "hid", [(0, 1), (1, 0)])


def spread_masks():
    rest = lax.axis_size("rows") // 4
    masks = [4 * (2**k * 2 - 1) for k in range(rest.bit_length() - 1)]
    return [(masks[k], masks[len(masks) - 1 - k]) for k in range(len(masks))]


def add_low(first, second):
    return to_low(first.astype(f32) + second.astype(f32))


def pick(values_in, at):
    return lax.dynamic_index_in_dim(values_in, at, 0, keepdims=False)


def reduce_rows(make_half, first_bit, second_bit):
    sent = swap(make_half(1 - first_bit), (1, 2))
    kept = make_half(first_bit)
    to_send = add_low(pick(kept, 1 - second_bit), pick(sent, 1 - second_bit))
    to_keep = add_low(pick(kept, second_bit), pick(sent, second_bit))
    own = add_low(to_keep, swap(to_send, (2, 1)))
    for core_masks in spread_masks():
        own = add_low(own, swap(own, core_masks))
    beside = swap(own, (2, 1))
    half = jnp.where(second_bit == 0, jnp.stack((own, beside)), jnp.stack((beside, own)))
    return half, swap(half, (1, 2))


def sum_small(values_in):
    values_in = values_in + near(values_in)
    for core_masks in [(1, 2), (2, 1)] + spread_masks():
        values_in = values_in + swap(values_in, core_masks)
    return values_in


def body(
    hidden_in,
    teacher,
    segment_ids,
    valid_mask,
    w_query,
    b_query,
    w_key,
    w_value,
    b_value,
    w_attn_out,
    b_attn_out,
    gain_one,
    shift_one,
    w_up,
    b_up,
    w_down,
    b_down,
    gain_two,
    shift_two,
    head_alpha,
    mha_alpha,
    unit_alpha,
    ffn_alpha,
    hidden_alpha,
    head_noise,
    mha_noise,
    unit_noise,
    ffn_noise,
    hidden_noise,
    lagrange,
):
    model, width = w_query.shape
    units = w_up.shape[1]
    heads = width // HD
    pairs = model // LANES
    tokens = hidden_in.shape[0] // 2
    pack = Pack(width, units)
    core = lax.axis_index("hid")
    row = lax.axis_index("rows")
    core_at = jnp.reshape(core, (1,)).astype(jnp.int32)
    low_bit, high_bit = row & 1, (row >> 1) & 1
    first_bit = jnp.where(core == 0, low_bit, high_bit).astype(jnp.int32)
    second_bit = jnp.where(core == 0, high_bit, low_bit).astype(jnp.int32)

    def filled(values_in, fill):
        return jnp.pad(values_in, (0, LANES - values_in.shape[0]), constant_values=fill)

    scalars = jnp.concatenate((mha_alpha, mha_noise, ffn_alpha, ffn_noise, lagrange))
    pack_own = jnp.concatenate(
        (
            b_query,
            b_value,
            b_attn_out,
            gain_one,
            shift_one,
            b_down,
            gain_two,
            shift_two,
            hidden_alpha,
            hidden_noise,
            b_up,
            unit_alpha,
            unit_noise,
            filled(head_alpha, 0.0),
            filled(head_noise, 0.5),
            filled(scalars, 0.5),
        )
    ).reshape(1, -1)
    x_peer = near(hidden_in)
    pack_peer = near(pack_own)
    wq_peer, wk_peer, wv_peer = near(w_query), near(w_key), near(w_value)
    wa_peer = near(w_attn_out)
    up_peer, down_peer = near(w_up), near(w_down)
    teacher_peer = near(teacher)
    segments = segment_ids.reshape(-1, LANES)
    valid = valid_mask.reshape(-1, LANES)
    packs = [full((1, pack.total))] * 2
    token_low = shaped((tokens, model), bf16)
    token_wide = shaped((tokens, model), f32)
    token_half = shaped((tokens, width), bf16)

    (
        weights,
        query,
        key,
        value,
        context,
        gated_own,
        gated_peer,
        stats,
        biased,
        normed,
        hidden,
    ) = call(
        partial(attend_kernel, pack),
        (pairs,),
        [one_number()]
        + [full(hidden_in.shape)] * 2
        + [full((model, width))] * 6
        + [full((width, model))] * 2
        + packs
        + [full(segments.shape)] * 2,
        [pl.BlockSpec((2, BLOCK, BLOCK), lambda i: (i, 0, 0))]
        + [full((tokens, model))] * 4
        + [full((tokens, width))] * 2
        + [full((tokens, LANES))]
        + [full((tokens, model))] * 3,
        [
            shaped((2 * pairs, BLOCK, BLOCK), bf16),
            token_low,
            token_low,
            token_low,
            token_low,
            token_half,
            token_half,
            shaped((tokens, LANES), f32),
            token_wide,
            token_wide,
            token_low,
        ],
        [
            pltpu.VMEM((tokens, model), bf16),
            pltpu.VMEM((BLOCK, BLOCK), f32),
            pltpu.VMEM((1, model), f32),
            pltpu.VMEM((tokens, model), bf16),
        ],
        (4.0, 20, 3),
        (
            core_at,
            hidden_in,
            x_peer,
            w_query,
            w_key,
            w_value,
            wq_peer,
            wk_peer,
            wv_peer,
            w_attn_out,
            wa_peer,
            pack_own,
            pack_peer,
            segments,
            valid,
        ),
    )
    hidden_near = near(hidden)
    gated_near = near(gated_peer)

    tiles = units // TILE

    def early(shape, dim):
        return pl.BlockSpec(
            shape, lambda i: tuple(jnp.minimum(i, tiles - 1) if d == dim else 0 for d in range(2))
        )

    def late(shape, dim):
        return pl.BlockSpec(
            shape, lambda i: tuple(jnp.maximum(i - tiles, 0) if d == dim else 0 for d in range(2))
        )

    def every(shape, dim):
        return pl.BlockSpec(shape, lambda i: tuple(i if d == dim else 0 for d in range(2)))

    (
        mixed_own,
        mixed_peer,
        active,
        slope,
        output_own,
        output_peer,
        grad_resid_two,
        grad_ffn,
        sums_two,
    ) = call(
        partial(ffn_forward_kernel, pack),
        (2 * tiles,),
        [one_number(), full((tokens, model)), full((tokens, model))]
        + [early((model, TILE), 1), late((model, TILE), 1)]
        + [early((TILE, model), 0), late((TILE, model), 0)]
        + packs
        + [full(teacher.shape)] * 2
        + [full(valid.shape)],
        [early((tokens, TILE), 1), late((tokens, TILE), 1)]
        + [every((tokens, TILE), 1)] * 2
        + [full((tokens, width))] * 2
        + [full((tokens, model))] * 2
        + [full((4, model))],
        [
            shaped((tokens, units), bf16),
            shaped((tokens, units), bf16),
            shaped((tokens, 2 * units), bf16),
            shaped((tokens, 2 * units), bf16),
            token_half,
            token_half,
            token_wide,
            token_low,
            shaped((4, model), f32),
        ],
        [pltpu.VMEM((tokens, model), f32)],
        (5.0, 25, 3),
        (
            core_at,
            hidden,
            normed,
            w_up,
            up_peer,
            w_down,
            down_peer,
            pack_own,
            pack_peer,
            teacher,
            teacher_peer,
            valid,
        ),
    )
    mixed_near = near(mixed_peer)
    grad_ffn_near = near(grad_ffn)
    output_near = near(output_peer)

    grad_pre_own, grad_pre_peer, grad_resid_one, grad_attn, sums_one, unit_sums = call(
        partial(ffn_backward_kernel, pack),
        (2 * tiles,),
        [one_number()]
        + [full((tokens, model))] * 4
        + [full((tokens, LANES))]
        + [every((tokens, TILE), 1)] * 2
        + [early((model, TILE), 1), late((model, TILE), 1)]
        + [early((TILE, model), 0), late((TILE, model), 0)]
        + packs,
        [early((tokens, TILE), 1), late((tokens, TILE), 1)]
        + [full((tokens, model))] * 2
        + [full((4, model)), full((2, 2 * units))],
        [
            shaped((tokens, units), bf16),
            shaped((tokens, units), bf16),
            token_wide,
            token_low,
            shaped((4, model), f32),
            shaped((2, 2 * units), f32),
        ],
        [pltpu.VMEM((tokens, model), f32)],
        (5.0, 25, 0),
        (
            core_at,
            grad_ffn,
            grad_resid_two,
            normed,
            biased,
            stats,
            active,
            slope,
            w_up,
            up_peer,
            w_down,
            down_peer,
            pack_own,
            pack_peer,
        ),
    )
    grad_pre_near = near(grad_pre_peer)
    grad_attn_near = near(grad_attn)

    half_units = units // 2
    step_units = half_units // 3

    def down_half(half):
        blocks = half_units // step_units
        by_units = pl.BlockSpec((tokens, step_units), lambda i, t: (0, t[0] * blocks + i))
        whole = pl.BlockSpec((tokens, model), lambda i, t: (0, 0))
        out = call_by_half(
            down_grad_kernel,
            (blocks,),
            [by_units, by_units, whole, whole],
            pl.BlockSpec((step_units, model), lambda i, t: (i, 0)),
            shaped((half_units, model), bf16),
            (1.2, 4.5),
            jnp.reshape(half, (1,)),
            (mixed_own, mixed_near, grad_ffn, grad_ffn_near),
        )
        return out.reshape(2, half_units // 2, model)

    def up_half(half):
        by_features = pl.BlockSpec((tokens, width), lambda i, t: (0, t[0]))
        by_units = pl.BlockSpec((tokens, TILE), lambda i, t: (0, i))
        out = call_by_half(
            up_grad_kernel,
            (tiles,),
            [by_features, by_features, by_units, by_units],
            pl.BlockSpec((width, TILE), lambda i, t: (0, i)),
            shaped((width, units), bf16),
            (1.2, 5.1),
            jnp.reshape(half, (1,)),
            (hidden, hidden_near, grad_pre_own, grad_pre_near),
        )
        return out.reshape(2, width // 2, units)

    down_sums = reduce_rows(down_half, first_bit, second_bit)
    up_sums = reduce_rows(up_half, first_bit, second_bit)

    own_pairs = pairs // 2
    grad_own, grad_peer, sums_attn = call(
        partial(attend_back_kernel, pack),
        (pairs,),
        [one_number(), pl.BlockSpec((2, BLOCK, BLOCK), lambda i: (i, 0, 0))]
        + [full((tokens, model))] * 4
        + [full((tokens, LANES)), full((tokens, model))]
        + [
            pl.BlockSpec((LANES, model), lambda i: (jnp.minimum(i, own_pairs - 1), 0)),
            pl.BlockSpec((LANES, model), lambda i: (jnp.maximum(i - own_pairs, 0), 0)),
        ]
        + packs,
        [full((tokens, 3 * width))] * 2 + [full((3, model))],
        [
            shaped((tokens, 3 * width), bf16),
            shaped((tokens, 3 * width), bf16),
            shaped((3, model), f32),
        ],
        [pltpu.VMEM((1, model), f32)],
        (4.0, 20, 0),
        (
            core_at,
            weights,
            query,
            key,
            value,
            context,
            stats,
            grad_attn,
            w_attn_out,
            wa_peer,
            pack_own,
            pack_peer,
        ),
    )
    grad_near = near(grad_peer)

    def attend_half(half):
        return call(
            partial(attend_grad_kernel, width),
            (),
            [one_number()] * 2
            + [full(hidden_in.shape)] * 2
            + [full((tokens, 3 * width))] * 2
            + [full((tokens, width))] * 2
            + [full((tokens, model))] * 2,
            full((2, model, width)),
            shaped((2, model, width), bf16),
            [],
            (1.2, 8, 0),
            (
                jnp.reshape(half, (1,)),
                core_at,
                hidden_in,
                x_peer,
                grad_own,
                grad_near,
                gated_own,
                gated_near,
                grad_attn,
                grad_attn_near,
            ),
        )

    attend_sums = reduce_rows(attend_half, first_bit, second_bit)

    input_own, input_peer = call(
        partial(input_grad_kernel, width),
        (),
        [one_number(), full((tokens, model))]
        + [full((tokens, 3 * width))] * 2
        + [full((model, width))] * 6,
        [full((tokens, width))] * 2,
        [shaped((tokens, width), f32)] * 2,
        [],
        (1.8, 8, 0),
        (
            core_at,
            grad_resid_one,
            grad_own,
            grad_peer,
            w_query,
            w_key,
            w_value,
            wq_peer,
            wk_peer,
            wv_peer,
        ),
    )
    input_near = near(input_peer)

    def by_token(own, other):
        return jnp.where(
            core == 0, jnp.concatenate((own, other), axis=0), jnp.concatenate((other, own), axis=0)
        )

    output = by_token(output_own, output_near)
    grad_input = by_token(input_own, input_near)

    small = sum_small(
        jnp.concatenate((sums_two, sums_one, sums_attn, unit_sums.reshape(-1, model)), axis=0)
    )
    sizes = (width,) * 5 + (units,) + (width,) * 3 + (heads, 1, units, 1, width)
    sizes = sizes + (heads, 1, units, 1, width, 1, 1)
    finished = call(
        partial(finish_kernel, pack),
        (),
        [one_number(), full(small.shape)] + packs,
        [full((1, size)) for size in sizes],
        [shaped((1, size), f32) for size in sizes],
        [],
        (0.01, 0.3, 0.1),
        (core_at, small, pack_own, pack_peer),
    )
    done = [item.reshape(-1) for item in finished]

    bit_at = jnp.reshape(first_bit, (1,))

    def place(pieces):
        _, height, across = pieces[0].shape

        def block(at):
            return pl.BlockSpec((1, height, across), at)

        out = call_by_half(
            place_kernel,
            (4,),
            [
                block(lambda i, t: (jnp.minimum(i, 1), 0, 0)),
                block(lambda i, t: (jnp.maximum(i - 2, 0), 0, 0)),
            ],
            block(lambda i, t: (2 * lax.rem(t[0] + i // 2, 2) + lax.rem(i, 2), 0, 0)),
            shaped((4, height, across), f32),
            (0.001, 7),
            bit_at,
            pieces,
        )
        return out.reshape(4 * height, across)

    sum_down = place(down_sums)
    sum_up = place(up_sums)
    sum_query, sum_key, sum_value, sum_attn = call(
        place_attend_kernel,
        (),
        [one_number()] + [full((2, model, width))] * 2,
        [full((model, width))] * 3 + [full((width, model))],
        [shaped((model, width), f32)] * 3 + [shaped((width, model), f32)],
        [],
        (0.001, 7, 0),
        (bit_at, *attend_sums),
    )
    return (
        output,
        grad_input,
        sum_query,
        done[0],
        sum_key,
        sum_value,
        done[1],
        sum_attn,
        done[2],
        done[3],
        done[4],
        sum_up,
        done[5],
        sum_down,
        *done[6:],
    )


def solution(mesh):
    in_specs = (
        P("rows", "hid"),
        P("rows", "hid"),
        P("rows"),
        P("rows"),
        P(None, "hid"),
        P("hid"),
        P(None, "hid"),
        P(None, "hid"),
        P("hid"),
        P("hid", None),
        P("hid"),
        P("hid"),
        P("hid"),
        P(None, "hid"),
        P("hid"),
        P("hid", None),
        P("hid"),
        P("hid"),
        P("hid"),
        P("hid"),
        P(),
        P("hid"),
        P(),
        P("hid"),
        P("hid"),
        P(),
        P("hid"),
        P(),
        P("hid"),
        P(),
    )
    out_specs = (
        P("rows", "hid"),
        P("rows", "hid"),
        P(None, "hid"),
        P("hid"),
        P(None, "hid"),
        P(None, "hid"),
        P("hid"),
        P("hid", None),
        P("hid"),
        P("hid"),
        P("hid"),
        P(None, "hid"),
        P("hid"),
        P("hid", None),
        P("hid"),
        P("hid"),
        P("hid"),
        P("hid"),
        P(),
        P("hid"),
        P(),
        P("hid"),
        P("hid"),
        P(),
        P("hid"),
        P(),
        P("hid"),
        P(),
        P(),
    )
    return jax.shard_map(body, mesh=mesh, in_specs=in_specs, out_specs=out_specs, check_vma=False)
```

```python
from functools import partial
import math

import jax
import jax.numpy as jnp
from jax import lax
from jax.experimental import pallas as pl
from jax.experimental.pallas import tpu as pltpu
from jax.sharding import PartitionSpec as P

HD = 64
BLOCK = 512
LANES = 128
TILE = 512

norm_eps = 1e-05
gate_temper = 2.0 / 3.0
stretch_low = -0.1
stretch_high = 1.1
target_share = 0.4
masked_score = -1000000000.0
open_shift = gate_temper * math.log(-stretch_low / stretch_high)


f32 = jnp.float32
bf16 = jnp.bfloat16


def to_low(values_in):
    return values_in.astype(bf16)


def contract(first, second, first_dim, second_dim):
    return lax.dot_general(
        first, second, (((first_dim,), (second_dim,)), ((), ())), preferred_element_type=f32
    )


def column_sum(values_in):
    return jnp.sum(values_in, axis=0, keepdims=True)


def row_sum(values_in):
    return jnp.sum(values_in, axis=1, keepdims=True)


def sigmoid(values_in):
    return 1.0 / (1.0 + jnp.exp(-values_in))


def stretched(gate_noise, log_alpha):
    relaxed = sigmoid(
        (jnp.log(gate_noise) - jnp.log(1.0 - gate_noise) + log_alpha) / gate_temper
    )
    return relaxed, relaxed * (stretch_high - stretch_low) + stretch_low


def hard_concrete(gate_noise, log_alpha):
    return jnp.clip(stretched(gate_noise, log_alpha)[1], 0.0, 1.0)


def gate_slope(gate_noise, log_alpha):
    relaxed, wide = stretched(gate_noise, log_alpha)
    slope = relaxed * (1.0 - relaxed) * ((stretch_high - stretch_low) / gate_temper)
    return jnp.where((wide > 0.0) & (wide < 1.0), slope, 0.0)


def open_share(log_alpha):
    return sigmoid(log_alpha - open_shift)


class Pack:
    def __init__(self, width, units):
        self.width, self.units = width, units
        at = 0
        for name in ("b_query", "b_value", "b_attn_out", "gain_one", "shift_one"):
            setattr(self, name, (at, width))
            at += width
        for name in ("b_down", "gain_two", "shift_two", "hidden_alpha", "hidden_noise"):
            setattr(self, name, (at, width))
            at += width
        for name in ("b_up", "unit_alpha", "unit_noise"):
            setattr(self, name, (at, units))
            at += units
        for name in ("head_alpha", "head_noise", "scalars"):
            setattr(self, name, (at, LANES))
            at += LANES
        self.total = at


def pack_kernel(pack, counts, *refs):
    out_ref = refs[-1]
    out_ref[...] = jnp.full(out_ref.shape, 0.5, f32)
    for ref, (spot, lane) in zip(refs[:-1], counts):
        size = ref.shape[0]
        out_ref[:, spot[0] + lane : spot[0] + lane + size] = ref[...].reshape(1, size)


def take(pack_ref, spot):
    return pack_ref[:, spot[0] : spot[0] + spot[1]]


def natural(core, own, peer):
    at_peer = core.astype(f32)
    at_own = 1.0 - at_peer
    return jnp.concatenate((own * at_own + peer * at_peer, peer * at_own + own * at_peer), axis=1)


def both(core, own_ref, peer_ref, spot):
    return natural(core, take(own_ref, spot), take(peer_ref, spot))


def hidden_gates(core, pack, own_ref, peer_ref):
    return hard_concrete(
        both(core, own_ref, peer_ref, pack.hidden_noise),
        both(core, own_ref, peer_ref, pack.hidden_alpha),
    )


def head_row(pack, own_ref, peer_ref, heads):
    parts = []
    for ref in (own_ref, peer_ref):
        gates = hard_concrete(take(ref, pack.head_noise), take(ref, pack.head_alpha))
        for at in range(heads):
            parts.append(jnp.broadcast_to(gates[:, at : at + 1], (1, HD)))
    return jnp.concatenate(parts, axis=1)


def scalar_gate(pack, own_ref, at):
    numbers = take(own_ref, pack.scalars)
    return hard_concrete(numbers[:, at + 1 : at + 2], numbers[:, at : at + 1])


def half_mask(side, dtype):
    lane = lax.broadcasted_iota(jnp.int32, (1, LANES), 1)
    inside = (lane < HD) if side == 0 else (lane >= HD)
    return jnp.where(inside, 1.0, 0.0).astype(dtype)


def pick_half(first, second):
    lane = lax.broadcasted_iota(jnp.int32, (1, LANES), 1)
    return jnp.where(lane < HD, first, second)


def norm_back(grad_normed, normed, inv_scale):
    width = normed.shape[1]
    mean_grad = row_sum(grad_normed) * (1.0 / width)
    mean_both = row_sum(grad_normed * normed) * (1.0 / width)
    return inv_scale * (grad_normed - mean_grad - normed * mean_both)


def norm_forward(resid):
    width = resid.shape[1]
    row_mean = row_sum(resid) * (1.0 / width)
    row_var = row_sum(resid * resid) * (1.0 / width) - row_mean * row_mean
    inv_scale = lax.rsqrt(row_var + norm_eps)
    return (resid - row_mean) * inv_scale, inv_scale


def own_rows(ref, core):
    return ref[pl.ds(pl.multiple_of(core * BLOCK, BLOCK), BLOCK), :]


def token_line(ref, core):
    lanes_of = BLOCK // LANES
    rows = [ref[pl.ds(core * lanes_of + at, 1), :] for at in range(lanes_of)]
    return jnp.concatenate(rows, axis=1).astype(f32)


def to_side(line):
    return jnp.broadcast_to(line, (LANES, BLOCK)).T[:, 0:1]


def rows_in(core, width, own_ref, peer_ref, out_ref, sems):
    rows = pl.ds(pl.multiple_of(core * BLOCK, BLOCK), BLOCK)
    own_at = pl.multiple_of(core * width, LANES)
    peer_at = pl.multiple_of((1 - core) * width, LANES)
    return (
        pltpu.make_async_copy(own_ref.at[rows, :], out_ref.at[:, pl.ds(own_at, width)], sems.at[0]),
        pltpu.make_async_copy(
            peer_ref.at[rows, :], out_ref.at[:, pl.ds(peer_at, width)], sems.at[1]
        ),
    )


def attend_kernel(
    pack,
    core_ref,
    x_own,
    x_peer,
    wq_own,
    wk_own,
    wv_own,
    wq_peer,
    wk_peer,
    wv_peer,
    wa_own,
    wa_peer,
    pack_own,
    pack_peer,
    segments,
    valid,
    weights_out,
    query_out,
    key_out,
    value_out,
    context_out,
    gated_own_out,
    gated_peer_out,
    stats_out,
    biased_out,
    normed_out,
    hidden_out,
    x_nat,
    mask_bias,
    gate_row,
    weight_in,
    weight_out,
    biases,
    total,
    sems,
):
    pair = pl.program_id(0)
    core = core_ref[0]
    width = pack.width
    heads = width // HD
    own_pairs = pl.num_programs(0) // 2

    @pl.when(pair == 0)
    def _():
        copies = rows_in(core, width, x_own, x_peer, x_nat, sems)
        for copy in copies:
            copy.start()
        gate_row[...] = head_row(pack, pack_own, pack_peer, heads)
        segment_line, valid_line = token_line(segments, core), token_line(valid, core)
        segment_side, valid_side = to_side(segment_line), to_side(valid_line)
        allowed = (segment_side == segment_line) & ((valid_line == 1.0) | (valid_side == 0.0))
        mask_bias[...] = jnp.where(allowed, 0.0, masked_score)
        for copy in copies:
            copy.wait()

    def load(at, pack_ref, query_ref, key_ref, value_ref, out_ref):
        weight_in[:, :LANES] = query_ref[...]
        weight_in[:, LANES : 2 * LANES] = key_ref[...]
        weight_in[:, 2 * LANES :] = value_ref[...]
        weight_out[...] = out_ref[...]
        spot = pl.multiple_of(at * LANES, LANES)
        biases[0:1, :] = pack_ref[:, pl.ds(pack.b_query[0] + spot, LANES)]
        biases[1:2, :] = pack_ref[:, pl.ds(pack.b_value[0] + spot, LANES)]

    @pl.when(pair < own_pairs)
    def _():
        load(pair, pack_own, wq_own, wk_own, wv_own, wa_own)

    @pl.when(pair >= own_pairs)
    def _():
        load(pair - own_pairs, pack_peer, wq_peer, wk_peer, wv_peer, wa_peer)

    columns = pl.ds(pl.multiple_of(pair * LANES, LANES), LANES)
    projected = contract(x_nat[...], weight_in[...], 1, 0)
    query = to_low(projected[:, :LANES] + biases[0:1, :]) * jnp.asarray(HD ** (-0.5), bf16)
    key = to_low(projected[:, LANES : 2 * LANES])
    value = to_low(projected[:, 2 * LANES :] + biases[1:2, :])
    query_out[...] = query
    key_out[...] = key
    value_out[...] = value
    value_wide = jnp.concatenate((value, jnp.ones((BLOCK, LANES), bf16)), axis=1)
    contexts = []
    lane = lax.broadcasted_iota(jnp.int32, (1, LANES), 1)
    stats = stats_out[...]
    for side in range(2):
        scores = contract(query * half_mask(side, bf16), key, 1, 1) + mask_bias[...]
        row_top = jnp.max(scores, axis=1, keepdims=True)
        weights = to_low(jnp.exp(scores - row_top))
        weights_out[side] = weights
        summed = contract(weights, value_wide, 1, 0)
        inverse = 1.0 / summed[:, LANES : 2 * LANES]
        contexts.append(summed[:, :LANES] * inverse)
        stats = jnp.where(lane == 2 * pair + side, inverse, stats)
    stats_out[...] = stats
    context = pick_half(contexts[0], contexts[1])
    context_out[...] = to_low(context)
    gated = to_low(context * gate_row[:, columns])
    attn_part = contract(gated, weight_out[...], 1, 0)

    @pl.when(pair == 0)
    def _():
        total[...] = attn_part

    @pl.when(pair > 0)
    def _():
        total[...] += attn_part

    @pl.when(pair < own_pairs)
    def _():
        gated_own_out[...] = gated

    @pl.when(pair >= own_pairs)
    def _():
        gated_peer_out[...] = gated

    @pl.when(pair == pl.num_programs(0) - 1)
    def _():
        biased = total[...] + both(core, pack_own, pack_peer, pack.b_attn_out)
        biased_out[...] = biased
        gates = hidden_gates(core, pack, pack_own, pack_peer)
        mha_gate = scalar_gate(pack, pack_own, 0)
        resid = x_nat[...].astype(f32) + biased * (mha_gate * gates)
        normed, inv_scale = norm_forward(resid)
        normed_out[...] = normed
        gain = both(core, pack_own, pack_peer, pack.gain_one)
        shift = both(core, pack_own, pack_peer, pack.shift_one)
        hidden_out[...] = to_low((normed * gain + shift) * gates)
        stats_out[...] = jnp.where(lane == LANES - 1, inv_scale, stats)


def gelu_parts(pre_act):
    whole = 0.5 + 0.5 * lax.erf(pre_act * (0.5**0.5))
    return whole, jnp.exp(-0.5 * pre_act * pre_act) * (1.0 / math.sqrt(2.0 * math.pi))


def ffn_forward_kernel(
    pack,
    core_ref,
    hidden,
    normed,
    up_own,
    up_peer,
    down_own,
    down_peer,
    pack_own,
    pack_peer,
    teacher_own,
    teacher_peer,
    valid,
    mixed_own_out,
    mixed_peer_out,
    active_out,
    slope_out,
    output_own,
    output_peer,
    grad_resid_out,
    grad_ffn_out,
    sums_out,
    total,
    normed_in,
    target,
    sems,
):
    step = pl.program_id(0)
    core = core_ref[0]
    own_steps = pl.num_programs(0) // 2
    width = pack.width
    copies = (
        pltpu.make_async_copy(normed, normed_in, sems.at[2]),
        *rows_in(core, width, teacher_own, teacher_peer, target, sems),
    )

    def tile(at, up_ref, down_ref, pack_ref, mixed_ref):
        spot = pl.multiple_of(at * TILE, TILE)

        def cut(place):
            return pack_ref[:, pl.ds(place[0] + spot, TILE)]

        pre_act = contract(hidden[...], up_ref[...], 1, 0) + cut(pack.b_up)
        whole, density = gelu_parts(pre_act)
        active = pre_act * whole
        unit_gate = hard_concrete(cut(pack.unit_noise), cut(pack.unit_alpha))
        mixed = to_low(active * unit_gate)
        mixed_ref[...] = mixed
        active_out[...] = to_low(active)
        slope_out[...] = to_low((whole + pre_act * density) * unit_gate)
        return contract(mixed, down_ref[...], 1, 0)

    @pl.when(step == 0)
    def _():
        for copy in copies:
            copy.start()
        total[...] = tile(step, up_own, down_own, pack_own, mixed_own_out)

    @pl.when((step > 0) & (step < own_steps))
    def _():
        total[...] += tile(step, up_own, down_own, pack_own, mixed_own_out)

    @pl.when(step >= own_steps)
    def _():
        total[...] += tile(step - own_steps, up_peer, down_peer, pack_peer, mixed_peer_out)

    @pl.when(step == pl.num_programs(0) - 1)
    def _():
        gates = hidden_gates(core, pack, pack_own, pack_peer)
        ffn_gate = scalar_gate(pack, pack_own, 2)

        def vector(spot):
            return both(core, pack_own, pack_peer, spot)

        for copy in copies:
            copy.wait()
        biased = total[...] + vector(pack.b_down)
        hidden_one = (normed_in[...] * vector(pack.gain_one) + vector(pack.shift_one)) * gates
        normed_two, inv_two = norm_forward(hidden_one + biased * (ffn_gate * gates))
        gain = vector(pack.gain_two)
        final = (normed_two * gain + vector(pack.shift_two)) * gates
        final_low = to_low(final)

        def split(own_ref, peer_ref, values_in):
            @pl.when(core == 0)
            def _():
                own_ref[...] = values_in[:, :width]
                peer_ref[...] = values_in[:, width:]

            @pl.when(core == 1)
            def _():
                own_ref[...] = values_in[:, width:]
                peer_ref[...] = values_in[:, :width]

        split(output_own, output_peer, final_low)
        valid_side = to_side(token_line(valid, core))
        grad_final = (final - target[...].astype(f32)) * valid_side
        grad_resid = norm_back(grad_final * (gates * gain), normed_two, inv_two)
        grad_resid_out[...] = grad_resid
        grad_ffn_out[...] = to_low(grad_resid * (ffn_gate * gates))
        sums_out[0:1, :] = column_sum(grad_final * normed_two)
        sums_out[1:2, :] = column_sum(grad_final)
        sums_out[2:3, :] = column_sum(grad_resid * biased)
        sums_out[3:4, :] = column_sum(grad_resid)


def ffn_pre_kernel(
    pack,
    core_ref,
    grad_ffn,
    active,
    slope,
    down_own,
    down_peer,
    grad_pre_own,
    grad_pre_peer,
    unit_sums_out,
):
    step = pl.program_id(0)
    core = core_ref[0]
    own_steps = pl.num_programs(0) // 2
    units = pack.units

    def tile(at, side, down_ref, pre_ref):
        grad_mixed = contract(grad_ffn[...], down_ref[...], 1, 1)
        grad_pre = to_low(grad_mixed * slope[...].astype(f32))
        pre_ref[...] = grad_pre
        spot = pl.multiple_of(side * units + at * TILE, TILE)
        unit_sums_out[0:1, pl.ds(spot, TILE)] = column_sum(grad_mixed * active[...].astype(f32))
        unit_sums_out[1:2, pl.ds(spot, TILE)] = column_sum(grad_pre.astype(f32))

    @pl.when(step < own_steps)
    def _():
        tile(step, core, down_own, grad_pre_own)

    @pl.when(step >= own_steps)
    def _():
        tile(step - own_steps, 1 - core, down_peer, grad_pre_peer)


def ffn_backward_kernel(
    pack,
    core_ref,
    grad_pre_own,
    grad_pre_peer,
    grad_resid_two,
    normed,
    biased,
    stats,
    up_own,
    up_peer,
    pack_own,
    pack_peer,
    grad_resid_out,
    grad_attn_out,
    sums_out,
    total,
    resid_in,
    normed_in,
    biased_in,
    sems,
):
    step = pl.program_id(0)
    core = core_ref[0]
    own_steps = pl.num_programs(0) // 2
    copies = (
        pltpu.make_async_copy(grad_resid_two, resid_in, sems.at[0]),
        pltpu.make_async_copy(normed, normed_in, sems.at[1]),
        pltpu.make_async_copy(biased, biased_in, sems.at[2]),
    )

    @pl.when(step == 0)
    def _():
        for copy in copies:
            copy.start()
        total[...] = contract(grad_pre_own[...], up_own[...], 1, 1)

    @pl.when((step > 0) & (step < own_steps))
    def _():
        total[...] += contract(grad_pre_own[...], up_own[...], 1, 1)

    @pl.when(step >= own_steps)
    def _():
        total[...] += contract(grad_pre_peer[...], up_peer[...], 1, 1)

    @pl.when(step == pl.num_programs(0) - 1)
    def _():
        gates = hidden_gates(core, pack, pack_own, pack_peer)
        mha_gate = scalar_gate(pack, pack_own, 0)
        gain = both(core, pack_own, pack_peer, pack.gain_one)
        for copy in copies:
            copy.wait()
        grad_hidden = resid_in[...] + total[...]
        normed_one = normed_in[...]
        sums_out[0:1, :] = column_sum(grad_hidden * normed_one)
        sums_out[1:2, :] = column_sum(grad_hidden)
        inv_scale = stats[:, LANES - 1 : LANES]
        grad_resid = norm_back(grad_hidden * (gates * gain), normed_one, inv_scale)
        grad_resid_out[...] = grad_resid
        grad_attn_out[...] = to_low(grad_resid * (mha_gate * gates))
        sums_out[2:3, :] = column_sum(grad_resid * biased_in[...])
        sums_out[3:4, :] = column_sum(grad_resid)


def attend_back_kernel(
    pack,
    side_is_own,
    core_ref,
    weights,
    query_ref,
    key_ref,
    value_ref,
    context_ref,
    stats,
    grad_attn,
    wa_ref,
    pack_own,
    pack_peer,
    out_ref,
    sums_out,
    gate_row,
):
    at = pl.program_id(0)
    core = core_ref[0]
    width = pack.width
    pair = at if side_is_own else at + pl.num_programs(0)

    @pl.when(at == 0)
    def _():
        gate_row[...] = head_row(pack, pack_own, pack_peer, width // HD)

    columns = pl.ds(pl.multiple_of(pair * LANES, LANES), LANES)
    lane = lax.broadcasted_iota(jnp.int32, (1, LANES), 1)

    query, key, value = query_ref[...], key_ref[...], value_ref[...]
    context = context_ref[...].astype(f32)
    grad_context = contract(grad_attn[...], wa_ref[...], 1, 1)
    spot = pl.ds(pl.multiple_of(at * LANES, LANES), LANES)
    sums_out[0:1, spot] = column_sum(grad_context * context)
    inverses = [
        row_sum(jnp.where(lane == 2 * pair + side, stats[...], 0.0)) for side in range(2)
    ]
    grad_low = to_low(grad_context * gate_row[:, columns] * pick_half(inverses[0], inverses[1]))
    product = grad_low.astype(f32) * context
    found = []
    for side in range(2):
        mask = half_mask(side, f32)
        level = row_sum(product * mask)
        grad_probs = contract(grad_low * mask.astype(bf16), value, 1, 1)
        chosen = weights[side]
        grad_raw = to_low(chosen.astype(f32) * (grad_probs - level))
        found.append(
            (
                contract(grad_raw, key, 1, 0),
                contract(grad_raw, query, 0, 0),
                contract(chosen, grad_low, 0, 0),
            )
        )
    grad_query = to_low(pick_half(found[0][0], found[1][0]) * HD ** (-0.5))
    grad_key = to_low(pick_half(found[0][1], found[1][1]))
    grad_value = to_low(pick_half(found[0][2], found[1][2]))
    for place, grad in enumerate((grad_query, grad_key, grad_value)):
        at_lane = pl.multiple_of(place * width + at * LANES, LANES)
        out_ref[:, pl.ds(at_lane, LANES)] = grad
    sums_out[1:2, spot] = column_sum(grad_query.astype(f32))
    sums_out[2:3, spot] = column_sum(grad_value.astype(f32))


def down_grad_kernel(bit_ref, mixed, mixed_near, grad, grad_near, sent_out, kept_out):
    summed = to_low(
        contract(mixed[...], grad[...], 0, 0) + contract(mixed_near[...], grad_near[...], 0, 0)
    )
    first = pl.program_id(0) < pl.num_programs(0) // 2

    @pl.when(first)
    def _():
        sent_out[...] = summed

    @pl.when(jnp.logical_not(first))
    def _():
        kept_out[...] = summed


def attn_out_grad_kernel(bit_ref, gated, gated_near, grad, grad_near, sent_out, kept_out):
    width = gated.shape[1]
    part = width // 4
    summed = to_low(
        contract(gated[...], grad[...], 0, 0) + contract(gated_near[...], grad_near[...], 0, 0)
    )

    def put(ref):
        for at in range(4):
            ref[:, at * width : (at + 1) * width] = summed[at * part : (at + 1) * part]

    @pl.when(pl.program_id(0) == 0)
    def _():
        put(sent_out)

    @pl.when(pl.program_id(0) == 1)
    def _():
        put(kept_out)


def attend_grad_kernel(
    half_ref,
    core_ref,
    x_own,
    x_peer,
    grad,
    grad_near,
    out_ref,
    source,
    sem,
):
    core = core_ref[0]

    @pl.when(half_ref[0] == core)
    def _():
        copy = pltpu.make_async_copy(x_own, source, sem)
        copy.start()
        copy.wait()

    @pl.when(half_ref[0] != core)
    def _():
        copy = pltpu.make_async_copy(x_peer, source, sem)
        copy.start()
        copy.wait()

    summed = contract(own_rows(source, core), grad[...], 0, 0) + contract(
        own_rows(source, 1 - core), grad_near[...], 0, 0
    )
    out_ref[...] = to_low(summed)


def input_grad_kernel(
    width,
    core_ref,
    grad_resid,
    grad_own,
    grad_peer,
    wq_own,
    wk_own,
    wv_own,
    wq_peer,
    wk_peer,
    wv_peer,
    own_out,
    peer_out,
):
    core = core_ref[0]
    summed = grad_resid[...]
    for grad, weights in (
        (grad_own, (wq_own, wk_own, wv_own)),
        (grad_peer, (wq_peer, wk_peer, wv_peer)),
    ):
        for place, weight in enumerate(weights):
            summed = summed + contract(
                grad[:, place * width : (place + 1) * width], weight[...], 1, 1
            )

    @pl.when(core == 0)
    def _():
        own_out[...] = summed[:, :width]
        peer_out[...] = summed[:, width:]

    @pl.when(core == 1)
    def _():
        own_out[...] = summed[:, width:]
        peer_out[...] = summed[:, :width]


def place_kernel(bit_ref, half, other, out_ref):
    step = pl.program_id(0)

    @pl.when(step < 2)
    def _():
        out_ref[...] = half[...].astype(f32)

    @pl.when(step >= 2)
    def _():
        out_ref[...] = other[...].astype(f32)


def place_up_kernel(bit_ref, half, other, up_out, attn_out):
    width = attn_out.shape[1]
    rows = up_out.shape[0]
    part = width // 4

    def put(ref):
        up_out[...] = ref[:rows, :].astype(f32)
        for at in range(4):
            attn_out[at * part : (at + 1) * part, :] = ref[
                rows:, at * width : (at + 1) * width
            ].astype(f32)

    @pl.when(pl.program_id(0) == 0)
    def _():
        put(half)

    @pl.when(pl.program_id(0) == 1)
    def _():
        put(other)


def place_attend_kernel(bit_ref, half, other, query_out, key_out, value_out):
    width = query_out.shape[1]

    def put(ref):
        for at, out in enumerate((query_out, key_out, value_out)):
            out[...] = ref[:, at * width : (at + 1) * width].astype(f32)

    @pl.when(pl.program_id(0) == 0)
    def _():
        put(half)

    @pl.when(pl.program_id(0) == 1)
    def _():
        put(other)


def finish_kernel(
    pack,
    core_ref,
    sums,
    pack_own,
    pack_peer,
    b_query,
    b_value,
    b_attn_out,
    gain_one,
    shift_one,
    b_up,
    b_down,
    gain_two,
    shift_two,
    head_gate,
    mha_gate,
    unit_gate,
    ffn_gate,
    hidden_gate,
    head_alpha,
    mha_alpha,
    unit_alpha,
    ffn_alpha,
    hidden_alpha,
    share_out,
    penalty_out,
):
    core = core_ref[0]
    width, units = pack.width, pack.units
    columns = pl.ds(pl.multiple_of(core * width, LANES), width)
    heads = width // HD

    def put(out_ref, line):
        out_ref[...] = line.reshape(out_ref.shape)

    def own(row):
        return sums[row : row + 1, columns]

    def vector(spot):
        return take(pack_own, spot)

    gates = hard_concrete(vector(pack.hidden_noise), vector(pack.hidden_alpha))
    mha, ffn = scalar_gate(pack, pack_own, 0), scalar_gate(pack, pack_own, 2)
    put(gain_two, gates * own(0))
    put(shift_two, gates * own(1))
    put(b_down, (ffn * gates) * own(3))
    put(gain_one, gates * own(4))
    put(shift_one, gates * own(5))
    put(b_attn_out, (mha * gates) * own(7))
    put(b_query, own(9))
    put(b_value, own(10))
    grad_hidden = (
        vector(pack.gain_two) * own(0)
        + vector(pack.shift_two) * own(1)
        + ffn * own(2)
        + vector(pack.gain_one) * own(4)
        + vector(pack.shift_one) * own(5)
        + mha * own(6)
    )
    put(hidden_gate, grad_hidden)
    all_gates = hidden_gates(core, pack, pack_own, pack_peer)
    grad_ffn_gate = row_sum(all_gates * sums[2:3, :])
    grad_mha_gate = row_sum(all_gates * sums[6:7, :])
    put(ffn_gate, grad_ffn_gate)
    put(mha_gate, grad_mha_gate)

    unit_rows = units // (2 * width)

    def unit_line(first):
        at = first + core * unit_rows
        return jnp.concatenate([sums[pl.ds(at + k, 1), :] for k in range(unit_rows)], axis=1)

    grad_unit = unit_line(11)
    put(b_up, unit_line(11 + 2 * unit_rows))
    put(unit_gate, grad_unit)
    by_head = own(8)
    lane = lax.broadcasted_iota(jnp.int32, (1, LANES), 1)
    grad_head = jnp.zeros((1, LANES), f32)
    for at in range(heads):
        grad_head = jnp.where(
            lane == at, row_sum(by_head[:, at * HD : (at + 1) * HD]), grad_head
        )
    put(head_gate, grad_head[:, :heads])

    numbers = vector(pack.scalars)
    mha_open, ffn_open = open_share(numbers[:, 0:1]), open_share(numbers[:, 2:3])
    first_weight, second_weight = numbers[:, 4:5], numbers[:, 5:6]

    def open_total(spot, count):
        return row_sum(open_share(take(pack_own, spot)[:, :count])) + row_sum(
            open_share(take(pack_peer, spot)[:, :count])
        )

    head_sum = open_total(pack.head_alpha, heads)
    unit_sum = open_total(pack.unit_alpha, units)
    hidden_sum = open_total(pack.hidden_alpha, width)
    model, inner = 2.0 * width, 2.0 * units
    scale = 1.0 / ((4.0 * model + 2.0 * inner) * model)
    kept = 4.0 * HD * mha_open * head_sum + 2.0 * ffn_open * unit_sum
    share = kept * hidden_sum * scale
    gap = share - target_share
    put(share_out, share)
    put(penalty_out, first_weight * gap + second_weight * gap * gap)
    slope = (first_weight + 2.0 * second_weight * gap) * scale
    by_heads = slope * hidden_sum * (4.0 * HD)
    by_units = slope * hidden_sum * 2.0

    def alpha_grad(noise, alpha, grad_gate, grad_open):
        opened = open_share(alpha)
        return gate_slope(noise, alpha) * grad_gate + grad_open * (opened * (1.0 - opened))

    put(
        head_alpha,
        alpha_grad(
            vector(pack.head_noise), vector(pack.head_alpha), grad_head, by_heads * mha_open
        )[:, :heads],
    )
    put(
        unit_alpha,
        alpha_grad(
            vector(pack.unit_noise), vector(pack.unit_alpha), grad_unit, by_units * ffn_open
        ),
    )
    put(
        hidden_alpha,
        alpha_grad(
            vector(pack.hidden_noise), vector(pack.hidden_alpha), grad_hidden, slope * kept
        ),
    )
    put(
        mha_alpha,
        alpha_grad(numbers[:, 1:2], numbers[:, 0:1], grad_mha_gate, by_heads * head_sum),
    )
    put(
        ffn_alpha,
        alpha_grad(numbers[:, 3:4], numbers[:, 2:3], grad_ffn_gate, by_units * unit_sum),
    )


def full(shape):
    return pl.BlockSpec(shape, lambda *at: (0,) * len(shape), pipeline_mode=pl.Buffered(1))


def anywhere():
    return pl.BlockSpec(memory_space=pl.ANY)


def every(shape, dim):
    return pl.BlockSpec(shape, lambda i: tuple(i if d == dim else 0 for d in range(2)))


def sides(steps):
    def early(shape, dim):
        return pl.BlockSpec(
            shape, lambda i: tuple(jnp.minimum(i, steps - 1) if d == dim else 0 for d in range(2))
        )

    def late(shape, dim):
        return pl.BlockSpec(
            shape, lambda i: tuple(jnp.maximum(i - steps, 0) if d == dim else 0 for d in range(2))
        )

    return early, late


def one_number():
    return pl.BlockSpec(memory_space=pltpu.SMEM)


def shaped(shape, dtype):
    return jax.ShapeDtypeStruct(shape, dtype)


class Order:
    def __init__(self):
        self.last = ()
        self.share = 1.0

    def tie(self, values_in):
        if not self.last:
            return values_in
        return lax.optimization_barrier((values_in, *self.last))[0]

    def mark(self, *values_in):
        self.last = values_in


def call(order, kernel, grid, in_specs, out_specs, out_shape, scratch, cost, args, mib=62):
    out = pl.pallas_call(
        kernel,
        grid=grid,
        in_specs=in_specs,
        out_specs=out_specs,
        out_shape=out_shape,
        scratch_shapes=scratch,
        compiler_params=pltpu.CompilerParams(vmem_limit_bytes=mib * 2**20),
        cost_estimate=pl.CostEstimate(
            flops=int(cost[0] * 1e9 * order.share),
            bytes_accessed=int(cost[1] * 1e6 * order.share),
            transcendentals=0,
        ),
    )(order.tie(args[0]), *args[1:])
    order.mark(jax.tree.leaves(out)[-1])
    return out


def call_by_half(order, kernel, grid, in_specs, out_specs, out_shape, cost, half, args, mib=62):
    out = pl.pallas_call(
        kernel,
        grid_spec=pltpu.PrefetchScalarGridSpec(
            num_scalar_prefetch=1, grid=grid, in_specs=in_specs, out_specs=out_specs
        ),
        out_shape=out_shape,
        compiler_params=pltpu.CompilerParams(vmem_limit_bytes=mib * 2**20),
        cost_estimate=pl.CostEstimate(
            flops=int(cost[0] * 1e9 * order.share),
            bytes_accessed=int(cost[1] * 1e6 * order.share),
            transcendentals=0,
        ),
    )(order.tie(half), *args)
    order.mark(jax.tree.leaves(out)[-1])
    return out


def swap_pairs(core_masks):
    rows, cores = lax.axis_size("rows"), lax.axis_size("hid")
    return [
        (row * cores + core, (row ^ core_masks[core]) * cores + core)
        for row in range(rows)
        for core in range(cores)
    ]


def swap(values_in, core_masks):
    return lax.ppermute(values_in, ("rows", "hid"), swap_pairs(core_masks))


def along(values_in, steps):
    rows, cores = lax.axis_size("rows"), lax.axis_size("hid")
    pairs = [
        (row * cores + core, (row + 4 * (steps[row // 4 % 4] - row // 4 % 4)) * cores + core)
        for row in range(rows)
        if row // 4 % 4 in steps
        for core in range(cores)
    ]
    return lax.ppermute(values_in, ("rows", "hid"), pairs)


def near(values_in):
    return lax.ppermute(values_in, "hid", [(0, 1), (1, 0)])


def spread_masks():
    rest = lax.axis_size("rows") // 4
    masks = [4 * (2**k * 2 - 1) for k in range(rest.bit_length() - 1)]
    return [(masks[k], masks[len(masks) - 1 - k]) for k in range(len(masks))]


def add_low(first, second):
    return to_low(first.astype(f32) + second.astype(f32))


def pick(values_in, at):
    return lax.dynamic_index_in_dim(values_in, at, 0, keepdims=False)


class RowSum:
    def __init__(self, order, sent_half, first_bit, second_bit):
        self.order = order
        self.first_bit, self.second_bit = first_bit, second_bit
        self.near = swap(sent_half, (1, 2))

    def halve(self, kept):
        at = self.second_bit
        kept = self.order.tie(kept)
        to_send = add_low(pick(kept, 1 - at), pick(self.near, 1 - at))
        self.own = add_low(pick(kept, at), pick(self.near, at))
        self.near = swap(to_send, (2, 1))
        self.order.mark(to_send, self.own)

    def halve_with(self, kept, below, below_near):
        kept = add_low(self.order.tie(kept), self.near)
        below = add_low(self.order.tie(below), below_near)
        rows = (kept.shape[0] + below.shape[0]) // 2
        first, second = kept[:rows], jnp.concatenate((kept[rows:], below), axis=0)
        to_send = jnp.where(self.second_bit == 0, second, first)
        self.own = jnp.where(self.second_bit == 0, first, second)
        self.near = swap(to_send, (2, 1))
        self.order.mark(to_send, self.own)

    def quarter(self, path=False):
        self.own = add_low(self.order.tie(self.own), self.near)
        masks = spread_masks()
        self.left = [partial(swap, core_masks=pair) for pair in masks]
        self.inner = None
        if path:
            steps = [{0: 1, 3: 2}, {1: 2, 2: 1}, {1: 0, 2: 3}]
            self.left = [partial(along, steps=item) for item in steps] + self.left[2:]
            at = lax.rem(lax.axis_index("rows") // 4, 4)
            self.inner = (at == 1) | (at == 2)
            self.until_out = 3
        self.near = self.left.pop(0)(self.own)
        self.order.mark(self.own)

    def spread(self):
        own = self.order.tie(self.own)
        if self.inner is not None:
            self.until_out -= 1
        if self.inner is not None and self.until_out == 0:
            self.own = jnp.where(self.inner, own, self.near)
        else:
            self.own = add_low(own, self.near)
        self.near = self.left.pop(0)(self.own) if self.left else swap(self.own, (2, 1))
        self.order.mark(self.own)

    def spread_all(self):
        while self.left:
            self.spread()
        self.spread()

    def widen(self):
        own, near = self.order.tie(self.own), self.near
        self.half = jnp.where(
            self.second_bit == 0, jnp.stack((own, near)), jnp.stack((near, own))
        )
        self.order.mark(self.half)
        self.near = swap(self.half, (1, 2))

    def parts(self):
        return self.half, self.near


class SmallSum:
    def __init__(self, order, values_in):
        self.order, self.own = order, values_in
        self.left = [(1, 2), (2, 1)] + spread_masks()
        self.near = near(values_in)

    def step(self):
        self.own = self.order.tie(self.own) + self.near
        self.order.mark(self.own)
        if self.left:
            self.near = swap(self.own, self.left.pop(0))
            return True
        return False

    def rest(self):
        while self.step():
            pass
        return self.own


def body(
    hidden_in,
    teacher,
    segment_ids,
    valid_mask,
    w_query,
    b_query,
    w_key,
    w_value,
    b_value,
    w_attn_out,
    b_attn_out,
    gain_one,
    shift_one,
    w_up,
    b_up,
    w_down,
    b_down,
    gain_two,
    shift_two,
    head_alpha,
    mha_alpha,
    unit_alpha,
    ffn_alpha,
    hidden_alpha,
    head_noise,
    mha_noise,
    unit_noise,
    ffn_noise,
    hidden_noise,
    lagrange,
):
    model, width = w_query.shape
    units = w_up.shape[1]
    heads = width // HD
    pairs = model // LANES
    tokens = hidden_in.shape[0] // 2
    pack = Pack(width, units)
    order = Order()
    core = lax.axis_index("hid")
    row = lax.axis_index("rows")
    core_at = jnp.reshape(core, (1,)).astype(jnp.int32)
    low_bit, high_bit = row & 1, (row >> 1) & 1
    first_bit = jnp.where(core == 0, low_bit, high_bit).astype(jnp.int32)
    second_bit = jnp.where(core == 0, high_bit, low_bit).astype(jnp.int32)

    packed = (
        (b_query, pack.b_query, 0),
        (b_value, pack.b_value, 0),
        (b_attn_out, pack.b_attn_out, 0),
        (gain_one, pack.gain_one, 0),
        (shift_one, pack.shift_one, 0),
        (b_down, pack.b_down, 0),
        (gain_two, pack.gain_two, 0),
        (shift_two, pack.shift_two, 0),
        (hidden_alpha, pack.hidden_alpha, 0),
        (hidden_noise, pack.hidden_noise, 0),
        (b_up, pack.b_up, 0),
        (unit_alpha, pack.unit_alpha, 0),
        (unit_noise, pack.unit_noise, 0),
        (head_alpha, pack.head_alpha, 0),
        (head_noise, pack.head_noise, 0),
        (mha_alpha, pack.scalars, 0),
        (mha_noise, pack.scalars, 1),
        (ffn_alpha, pack.scalars, 2),
        (ffn_noise, pack.scalars, 3),
        (lagrange, pack.scalars, 4),
    )
    pack_own = call(
        order,
        partial(pack_kernel, pack, [item[1:] for item in packed]),
        (),
        [full(item[0].shape) for item in packed],
        full((1, pack.total)),
        shaped((1, pack.total), f32),
        [],
        (0.001, 0.1, 0),
        tuple(item[0] for item in packed),
    )
    x_peer = near(hidden_in)
    pack_peer = near(pack_own)
    wq_peer, wk_peer, wv_peer = near(w_query), near(w_key), near(w_value)
    wa_peer = near(w_attn_out)
    first_peers = (x_peer, pack_peer, wq_peer, wk_peer, wv_peer, wa_peer)
    *first_peers, up_sent, down_sent, teacher_sent = lax.optimization_barrier(
        (*first_peers, w_up, w_down, teacher)
    )
    x_peer, pack_peer, wq_peer, wk_peer, wv_peer, wa_peer = first_peers
    up_peer, down_peer, teacher_peer = near(up_sent), near(down_sent), near(teacher_sent)
    segments = segment_ids.reshape(-1, LANES)
    valid = valid_mask.reshape(-1, LANES)
    packs = [full((1, pack.total))] * 2
    pair_early, pair_late = sides(pairs // 2)
    token_low = shaped((tokens, model), bf16)
    token_wide = shaped((tokens, model), f32)
    token_half = shaped((tokens, width), bf16)

    (
        weights,
        query,
        key,
        value,
        context,
        gated_own,
        gated_peer,
        stats,
        biased,
        normed,
        hidden,
    ) = call(
        order,
        partial(attend_kernel, pack),
        (pairs,),
        [one_number()]
        + [anywhere()] * 2
        + [pair_early((model, LANES), 1)] * 3
        + [pair_late((model, LANES), 1)] * 3
        + [pair_early((LANES, model), 0), pair_late((LANES, model), 0)]
        + packs
        + [full(segments.shape)] * 2,
        [pl.BlockSpec((2, BLOCK, BLOCK), lambda i: (i, 0, 0))]
        + [every((tokens, LANES), 1)] * 4
        + [pair_early((tokens, LANES), 1), pair_late((tokens, LANES), 1)]
        + [full((tokens, LANES))]
        + [full((tokens, model))] * 3,
        [
            shaped((2 * pairs, BLOCK, BLOCK), bf16),
            token_low,
            token_low,
            token_low,
            token_low,
            token_half,
            token_half,
            shaped((tokens, LANES), f32),
            token_wide,
            token_wide,
            token_low,
        ],
        [
            pltpu.VMEM((tokens, model), bf16),
            pltpu.VMEM((BLOCK, BLOCK), f32),
            pltpu.VMEM((1, model), f32),
            pltpu.VMEM((model, 3 * LANES), bf16),
            pltpu.VMEM((LANES, model), bf16),
            pltpu.VMEM((8, LANES), f32),
            pltpu.VMEM((tokens, model), f32),
            pltpu.SemaphoreType.DMA((2,)),
        ],
        (4.0, 20, 3),
        (
            core_at,
            hidden_in,
            x_peer,
            w_query,
            w_key,
            w_value,
            wq_peer,
            wk_peer,
            wv_peer,
            w_attn_out,
            wa_peer,
            pack_own,
            pack_peer,
            segments,
            valid,
        ),
    )
    hidden_near = near(hidden)
    gated_near = near(gated_peer)

    tiles = units // TILE
    early, late = sides(tiles)

    (
        mixed_own,
        mixed_peer,
        active,
        slope,
        output_own,
        output_peer,
        grad_resid_two,
        grad_ffn,
        sums_two,
    ) = call(
        order,
        partial(ffn_forward_kernel, pack),
        (2 * tiles,),
        [one_number(), full((tokens, model)), anywhere()]
        + [early((model, TILE), 1), late((model, TILE), 1)]
        + [early((TILE, model), 0), late((TILE, model), 0)]
        + packs
        + [anywhere()] * 2
        + [full(valid.shape)],
        [early((tokens, TILE), 1), late((tokens, TILE), 1)]
        + [every((tokens, TILE), 1)] * 2
        + [full((tokens, width))] * 2
        + [full((tokens, model))] * 2
        + [full((4, model))],
        [
            shaped((tokens, units), bf16),
            shaped((tokens, units), bf16),
            shaped((tokens, 2 * units), bf16),
            shaped((tokens, 2 * units), bf16),
            token_half,
            token_half,
            token_wide,
            token_low,
            shaped((4, model), f32),
        ],
        [
            pltpu.VMEM((tokens, model), f32),
            pltpu.VMEM((tokens, model), f32),
            pltpu.VMEM((tokens, model), bf16),
            pltpu.SemaphoreType.DMA((3,)),
        ],
        (5.0, 25, 3),
        (
            core_at,
            hidden,
            normed,
            w_up,
            up_peer,
            w_down,
            down_peer,
            pack_own,
            pack_peer,
            teacher,
            teacher_peer,
            valid,
        ),
    )
    mixed_near = near(mixed_peer)
    grad_ffn_near = near(grad_ffn)
    output_near = near(output_peer)

    grad_pre_own, grad_pre_peer, unit_sums = call(
        order,
        partial(ffn_pre_kernel, pack),
        (2 * tiles,),
        [one_number(), full((tokens, model))]
        + [every((tokens, TILE), 1)] * 2
        + [early((TILE, model), 0), late((TILE, model), 0)],
        [early((tokens, TILE), 1), late((tokens, TILE), 1), full((2, 2 * units))],
        [
            shaped((tokens, units), bf16),
            shaped((tokens, units), bf16),
            shaped((2, 2 * units), f32),
        ],
        [],
        (50, 300, 0),
        (core_at, grad_ffn, active, slope, w_down, down_peer),
    )
    grad_pre_near = near(grad_pre_peer)

    bit_at = jnp.reshape(first_bit, (1,))

    def at_half(i, steps, bit):
        return jnp.where(i < steps, 1 - bit[0], bit[0])

    def sent_then_kept(shape, steps, dim):
        return [
            pl.BlockSpec(
                shape,
                lambda i, t, at=at: tuple(at(i) if d == dim else 0 for d in range(2)),
            )
            for at in (
                lambda i: jnp.minimum(i, steps - 1),
                lambda i: jnp.maximum(i - steps, 0),
            )
        ]

    half_units = units // 2
    step_units = half_units // 2
    by_units = pl.BlockSpec(
        (tokens, step_units), lambda i, t: (0, at_half(i, 2, t) * 2 + lax.rem(i, 2))
    )
    down_sent, down_kept = call_by_half(
        order,
        down_grad_kernel,
        (4,),
        [by_units, by_units] + [full((tokens, model))] * 2,
        sent_then_kept((step_units, model), 2, 0),
        [shaped((half_units, model), bf16)] * 2,
        (48, 180),
        bit_at,
        (mixed_own, mixed_near, grad_ffn, grad_ffn_near),
    )
    down_sent, down_kept = (
        item.reshape(2, half_units // 2, model) for item in (down_sent, down_kept)
    )
    down_chunk = RowSum(order, down_sent, first_bit, second_bit)

    up_rows = width + width // 4
    by_features = pl.BlockSpec((tokens, width), lambda i, t: (0, at_half(i, 2, t)))
    by_units = pl.BlockSpec((tokens, half_units), lambda i, t: (0, lax.rem(i, 2)))
    up_sent, up_kept = call_by_half(
        order,
        down_grad_kernel,
        (4,),
        [by_features, by_features, by_units, by_units],
        sent_then_kept((width, half_units), 2, 1),
        [shaped((width, units), bf16)] * 2,
        (2.4, 12),
        bit_at,
        (hidden, hidden_near, grad_pre_own, grad_pre_near),
    )
    up_chunk = RowSum(order, up_sent, first_bit, second_bit)

    grad_resid_one, grad_attn, sums_one = call(
        order,
        partial(ffn_backward_kernel, pack),
        (2 * tiles,),
        [one_number()]
        + [early((tokens, TILE), 1), late((tokens, TILE), 1)]
        + [anywhere()] * 3
        + [full((tokens, LANES))]
        + [early((model, TILE), 1), late((model, TILE), 1)]
        + packs,
        [full((tokens, model))] * 2 + [full((4, model))],
        [token_wide, token_low, shaped((4, model), f32)],
        [pltpu.VMEM((tokens, model), f32)] * 4 + [pltpu.SemaphoreType.DMA((3,))],
        (2.5, 15, 0),
        (
            core_at,
            grad_pre_own,
            grad_pre_peer,
            grad_resid_two,
            normed,
            biased,
            stats,
            w_up,
            up_peer,
            pack_own,
            pack_peer,
        ),
    )
    grad_attn_near = near(grad_attn)
    own_pairs = pairs // 2

    def attend_back(side_is_own, wa_ref):
        first = 0 if side_is_own else own_pairs
        return call(
            order,
            partial(attend_back_kernel, pack, side_is_own),
            (own_pairs,),
            [one_number(), pl.BlockSpec((2, BLOCK, BLOCK), lambda i: (i + first, 0, 0))]
            + [pl.BlockSpec((tokens, LANES), lambda i: (0, i + first))] * 4
            + [full((tokens, LANES)), full((tokens, model))]
            + [pl.BlockSpec((LANES, model), lambda i: (i, 0))]
            + packs,
            [full((tokens, 3 * width)), full((3, width))],
            [shaped((tokens, 3 * width), bf16), shaped((3, width), f32)],
            [pltpu.VMEM((1, model), f32)],
            (2.0, 10, 0),
            (
                core_at,
                weights,
                query,
                key,
                value,
                context,
                stats,
                grad_attn,
                wa_ref,
                pack_own,
                pack_peer,
            ),
        )

    grad_peer, sums_peer = attend_back(False, wa_peer)
    grad_near = near(grad_peer)
    down_chunk.halve(down_kept)
    by_columns = pl.BlockSpec((tokens, width), lambda i, t: (0, at_half(i, 1, t)))
    attn_sent, attn_kept = call_by_half(
        order,
        attn_out_grad_kernel,
        (2,),
        [full((tokens, width))] * 2 + [by_columns] * 2,
        [full((width // 4, units))] * 2,
        [shaped((width // 4, units), bf16)] * 2,
        (0.6, 3),
        bit_at,
        (gated_own, gated_near, grad_attn, grad_attn_near),
    )
    attn_near = swap(attn_sent, (1, 2))
    grad_own, sums_own = attend_back(True, w_attn_out)
    up_chunk.halve_with(up_kept, attn_kept, attn_near)
    down_chunk.quarter(path=True)
    sums_attn = jnp.where(
        core == 0,
        jnp.concatenate((sums_own, sums_peer), axis=1),
        jnp.concatenate((sums_peer, sums_own), axis=1),
    )

    def attend_half(half):
        out = call(
            order,
            attend_grad_kernel,
            (),
            [one_number()] * 2 + [anywhere()] * 2 + [full((tokens, 3 * width))] * 2,
            full((width, 3 * width)),
            shaped((width, 3 * width), bf16),
            [pltpu.VMEM(hidden_in.shape, bf16), pltpu.SemaphoreType.DMA],
            (24, 100, 0),
            (jnp.reshape(half, (1,)), core_at, hidden_in, x_peer, grad_own, grad_near),
        )
        return out.reshape(2, width // 2, 3 * width)

    attend_sent = attend_half(1 - first_bit)
    attend_chunk = RowSum(order, attend_sent, first_bit, second_bit)
    up_chunk.quarter()
    down_chunk.spread()
    small = SmallSum(
        order,
        jnp.concatenate((sums_two, sums_one, sums_attn, unit_sums.reshape(-1, model)), axis=0),
    )
    attend_kept = attend_half(first_bit)
    attend_chunk.halve(attend_kept)
    small.step()

    input_own, input_peer = call(
        order,
        partial(input_grad_kernel, width),
        (),
        [one_number(), full((tokens, model))]
        + [full((tokens, 3 * width))] * 2
        + [full((model, width))] * 6,
        [full((tokens, width))] * 2,
        [shaped((tokens, width), f32)] * 2,
        [],
        (1.8, 8, 0),
        (
            core_at,
            grad_resid_one,
            grad_own,
            grad_peer,
            w_query,
            w_key,
            w_value,
            wq_peer,
            wk_peer,
            wv_peer,
        ),
    )
    input_near = near(input_peer)

    def by_token(own, other):
        own = order.tie(own)
        out = jnp.where(
            core == 0, jnp.concatenate((own, other), axis=0), jnp.concatenate((other, own), axis=0)
        )
        order.mark(out)
        return out

    up_chunk.spread()
    down_chunk.spread()
    attend_chunk.quarter()
    small.step()
    output = by_token(output_own, output_near)
    grad_input = by_token(input_own, input_near)
    up_chunk.spread()
    down_chunk.spread()
    attend_chunk.spread()
    small.step()
    up_chunk.widen()
    down_chunk.widen()
    attend_chunk.spread()
    small.step()
    attend_chunk.widen()
    small_sums = small.rest()
    sizes = (width,) * 5 + (units,) + (width,) * 3 + (heads, 1, units, 1, width)
    sizes = sizes + (heads, 1, units, 1, width, 1, 1)
    finished = call(
        order,
        partial(finish_kernel, pack),
        (),
        [one_number(), full(small_sums.shape)] + packs,
        [full((size,)) for size in sizes],
        [shaped((size,), f32) for size in sizes],
        [],
        (0.01, 0.3, 0.1),
        (core_at, small_sums, pack_own, pack_peer),
    )

    def place(pieces):
        _, height, across = pieces[0].shape

        def block(at):
            return pl.BlockSpec((1, height, across), at)

        out = call_by_half(
            order,
            place_kernel,
            (4,),
            [
                block(lambda i, t: (jnp.minimum(i, 1), 0, 0)),
                block(lambda i, t: (jnp.maximum(i - 2, 0), 0, 0)),
            ],
            block(lambda i, t: (2 * lax.rem(t[0] + i // 2, 2) + lax.rem(i, 2), 0, 0)),
            shaped((4, height, across), f32),
            (0.001, 7),
            bit_at,
            pieces,
        )
        return out.reshape(4 * height, across)

    def by_half(pieces):
        return tuple(piece.reshape(-1, piece.shape[-1]) for piece in pieces)

    def own_half(shape, dim):
        return pl.BlockSpec(
            shape, lambda i, t: tuple(lax.rem(t[0] + i, 2) if d == dim else 0 for d in range(2))
        )

    sum_up, sum_attn = call_by_half(
        order,
        place_up_kernel,
        (2,),
        [full((up_rows, units))] * 2,
        [own_half((width, units), 0), own_half((width, width), 1)],
        [shaped((model, units), f32), shaped((width, model), f32)],
        (0.001, 10),
        bit_at,
        by_half(up_chunk.parts()),
    )
    sum_down = place(down_chunk.parts())
    sum_query, sum_key, sum_value = call_by_half(
        order,
        place_attend_kernel,
        (2,),
        [full((width, 3 * width))] * 2,
        [own_half((width, width), 0)] * 3,
        [shaped((model, width), f32)] * 3,
        (0.001, 7),
        bit_at,
        by_half(attend_chunk.parts()),
    )
    return (
        output,
        grad_input,
        sum_query,
        finished[0],
        sum_key,
        sum_value,
        finished[1],
        sum_attn,
        finished[2],
        finished[3],
        finished[4],
        sum_up,
        finished[5],
        sum_down,
        *finished[6:],
    )


def solution(mesh):
    in_specs = (
        P("rows", "hid"),
        P("rows", "hid"),
        P("rows"),
        P("rows"),
        P(None, "hid"),
        P("hid"),
        P(None, "hid"),
        P(None, "hid"),
        P("hid"),
        P("hid", None),
        P("hid"),
        P("hid"),
        P("hid"),
        P(None, "hid"),
        P("hid"),
        P("hid", None),
        P("hid"),
        P("hid"),
        P("hid"),
        P("hid"),
        P(),
        P("hid"),
        P(),
        P("hid"),
        P("hid"),
        P(),
        P("hid"),
        P(),
        P("hid"),
        P(),
    )
    out_specs = (
        P("rows", "hid"),
        P("rows", "hid"),
        P(None, "hid"),
        P("hid"),
        P(None, "hid"),
        P(None, "hid"),
        P("hid"),
        P("hid", None),
        P("hid"),
        P("hid"),
        P("hid"),
        P(None, "hid"),
        P("hid"),
        P("hid", None),
        P("hid"),
        P("hid"),
        P("hid"),
        P("hid"),
        P(),
        P("hid"),
        P(),
        P("hid"),
        P("hid"),
        P(),
        P("hid"),
        P(),
        P("hid"),
        P(),
        P(),
    )
    return jax.shard_map(body, mesh=mesh, in_specs=in_specs, out_specs=out_specs, check_vma=False)
```

```python
from functools import partial
import math

import jax
import jax.numpy as jnp
from jax import lax
from jax.experimental import pallas as pl
from jax.experimental.pallas import tpu as pltpu
from jax.sharding import PartitionSpec as P

HD = 64
BLOCK = 512
LANES = 128
TILE = 768

norm_eps = 1e-05
gate_temper = 2.0 / 3.0
stretch_low = -0.1
stretch_high = 1.1
target_share = 0.4
masked_score = -1000000000.0
open_shift = gate_temper * math.log(-stretch_low / stretch_high)


f32 = jnp.float32
bf16 = jnp.bfloat16


def to_low(values_in):
    return values_in.astype(bf16)


def contract(first, second, first_dim, second_dim):
    return lax.dot_general(
        first, second, (((first_dim,), (second_dim,)), ((), ())), preferred_element_type=f32
    )


def column_sum(values_in):
    return jnp.sum(values_in, axis=0, keepdims=True)


def row_sum(values_in):
    return jnp.sum(values_in, axis=1, keepdims=True)


def sigmoid(values_in):
    return 1.0 / (1.0 + jnp.exp(-values_in))


def stretched(gate_noise, log_alpha):
    relaxed = sigmoid(
        (jnp.log(gate_noise) - jnp.log(1.0 - gate_noise) + log_alpha) / gate_temper
    )
    return relaxed, relaxed * (stretch_high - stretch_low) + stretch_low


def hard_concrete(gate_noise, log_alpha):
    return jnp.clip(stretched(gate_noise, log_alpha)[1], 0.0, 1.0)


def gate_slope(gate_noise, log_alpha):
    relaxed, wide = stretched(gate_noise, log_alpha)
    slope = relaxed * (1.0 - relaxed) * ((stretch_high - stretch_low) / gate_temper)
    return jnp.where((wide > 0.0) & (wide < 1.0), slope, 0.0)


def open_share(log_alpha):
    return sigmoid(log_alpha - open_shift)


class Pack:
    def __init__(self, width, units):
        self.width, self.units = width, units
        at = 0
        for name in ("b_query", "b_value", "b_attn_out", "gain_one", "shift_one"):
            setattr(self, name, (at, width))
            at += width
        for name in ("b_down", "gain_two", "shift_two", "hidden_alpha", "hidden_noise"):
            setattr(self, name, (at, width))
            at += width
        for name in ("b_up", "unit_alpha", "unit_noise"):
            setattr(self, name, (at, units))
            at += units
        for name in ("head_alpha", "head_noise", "scalars"):
            setattr(self, name, (at, LANES))
            at += LANES
        self.total = at


def pack_kernel(pack, counts, *refs):
    out_ref = refs[-1]
    out_ref[...] = jnp.full(out_ref.shape, 0.5, f32)
    for ref, (spot, lane) in zip(refs[:-1], counts):
        size = ref.shape[0]
        at = slice(spot[0] + lane, spot[0] + lane + size)
        if size > 1:
            out_ref[:, at] = ref[...].reshape(1, size)
        else:
            out_ref[:, at] = jnp.full((1, 1), ref[0], f32)


def take(pack_ref, spot):
    return pack_ref[:, spot[0] : spot[0] + spot[1]]


def natural(core, own, peer):
    at_peer = core.astype(f32)
    at_own = 1.0 - at_peer
    return jnp.concatenate((own * at_own + peer * at_peer, peer * at_own + own * at_peer), axis=1)


def both(core, own_ref, peer_ref, spot):
    return natural(core, take(own_ref, spot), take(peer_ref, spot))


def hidden_gates(core, pack, own_ref, peer_ref):
    return hard_concrete(
        both(core, own_ref, peer_ref, pack.hidden_noise),
        both(core, own_ref, peer_ref, pack.hidden_alpha),
    )


def head_row(pack, own_ref, peer_ref, heads):
    parts = []
    for ref in (own_ref, peer_ref):
        gates = hard_concrete(take(ref, pack.head_noise), take(ref, pack.head_alpha))
        for at in range(heads):
            parts.append(jnp.broadcast_to(gates[:, at : at + 1], (1, HD)))
    return jnp.concatenate(parts, axis=1)


def scalar_gate(pack, own_ref, at):
    numbers = take(own_ref, pack.scalars)
    return hard_concrete(numbers[:, at + 1 : at + 2], numbers[:, at : at + 1])


def half_mask(side, dtype):
    lane = lax.broadcasted_iota(jnp.int32, (1, LANES), 1)
    inside = (lane < HD) if side == 0 else (lane >= HD)
    return jnp.where(inside, 1.0, 0.0).astype(dtype)


def pick_half(first, second):
    lane = lax.broadcasted_iota(jnp.int32, (1, LANES), 1)
    return jnp.where(lane < HD, first, second)


def norm_back(grad_normed, normed, inv_scale):
    width = normed.shape[1]
    mean_grad = row_sum(grad_normed) * (1.0 / width)
    mean_both = row_sum(grad_normed * normed) * (1.0 / width)
    return inv_scale * (grad_normed - mean_grad - normed * mean_both)


def norm_forward(resid):
    width = resid.shape[1]
    row_mean = row_sum(resid) * (1.0 / width)
    row_var = row_sum(resid * resid) * (1.0 / width) - row_mean * row_mean
    inv_scale = lax.rsqrt(row_var + norm_eps)
    return (resid - row_mean) * inv_scale, inv_scale


def own_rows(ref, core):
    return ref[pl.ds(pl.multiple_of(core * BLOCK, BLOCK), BLOCK), :]


def token_line(ref, core):
    lanes_of = BLOCK // LANES
    rows = [ref[pl.ds(core * lanes_of + at, 1), :] for at in range(lanes_of)]
    return jnp.concatenate(rows, axis=1).astype(f32)


def to_side(line):
    return jnp.broadcast_to(line, (LANES, BLOCK)).T[:, 0:1]


def rows_in(core, width, own_ref, peer_ref, out_ref, sems):
    rows = pl.ds(pl.multiple_of(core * BLOCK, BLOCK), BLOCK)
    own_at = pl.multiple_of(core * width, LANES)
    peer_at = pl.multiple_of((1 - core) * width, LANES)
    return (
        pltpu.make_async_copy(own_ref.at[rows, :], out_ref.at[:, pl.ds(own_at, width)], sems.at[0]),
        pltpu.make_async_copy(
            peer_ref.at[rows, :], out_ref.at[:, pl.ds(peer_at, width)], sems.at[1]
        ),
    )


def attend_kernel(
    pack,
    core_ref,
    x_own,
    x_peer,
    wq_own,
    wk_own,
    wv_own,
    wq_peer,
    wk_peer,
    wv_peer,
    wa_own,
    wa_peer,
    pack_own,
    pack_peer,
    segments,
    valid,
    weights_out,
    query_out,
    key_out,
    value_out,
    context_out,
    gated_own_out,
    gated_peer_out,
    stats_out,
    biased_out,
    normed_out,
    hidden_out,
    x_nat,
    mask_bias,
    gate_row,
    weight_in,
    weight_out,
    biases,
    total,
    sems,
):
    pair = pl.program_id(0)
    core = core_ref[0]
    width = pack.width
    heads = width // HD
    own_pairs = pl.num_programs(0) // 2

    @pl.when(pair == 0)
    def _():
        copies = rows_in(core, width, x_own, x_peer, x_nat, sems)
        for copy in copies:
            copy.start()
        gate_row[...] = head_row(pack, pack_own, pack_peer, heads)
        segment_line, valid_line = token_line(segments, core), token_line(valid, core)
        segment_side, valid_side = to_side(segment_line), to_side(valid_line)
        allowed = (segment_side == segment_line) & ((valid_line == 1.0) | (valid_side == 0.0))
        mask_bias[...] = jnp.where(allowed, 0.0, masked_score)
        for copy in copies:
            copy.wait()

    def load(at, pack_ref, query_ref, key_ref, value_ref, out_ref):
        weight_in[:, :LANES] = query_ref[...]
        weight_in[:, LANES : 2 * LANES] = key_ref[...]
        weight_in[:, 2 * LANES :] = value_ref[...]
        weight_out[...] = out_ref[...]
        spot = pl.multiple_of(at * LANES, LANES)
        biases[0:1, :] = pack_ref[:, pl.ds(pack.b_query[0] + spot, LANES)]
        biases[1:2, :] = pack_ref[:, pl.ds(pack.b_value[0] + spot, LANES)]

    @pl.when(pair < own_pairs)
    def _():
        load(pair, pack_own, wq_own, wk_own, wv_own, wa_own)

    @pl.when(pair >= own_pairs)
    def _():
        load(pair - own_pairs, pack_peer, wq_peer, wk_peer, wv_peer, wa_peer)

    columns = pl.ds(pl.multiple_of(pair * LANES, LANES), LANES)
    projected = contract(x_nat[...], weight_in[...], 1, 0)
    query = to_low(projected[:, :LANES] + biases[0:1, :]) * jnp.asarray(HD ** (-0.5), bf16)
    key = to_low(projected[:, LANES : 2 * LANES])
    value = to_low(projected[:, 2 * LANES :] + biases[1:2, :])
    query_out[...] = query
    key_out[...] = key
    value_out[...] = value
    value_wide = jnp.concatenate((value, jnp.ones((BLOCK, LANES), bf16)), axis=1)
    contexts = []
    lane = lax.broadcasted_iota(jnp.int32, (1, LANES), 1)
    stats = stats_out[...]
    for side in range(2):
        scores = contract(query * half_mask(side, bf16), key, 1, 1) + mask_bias[...]
        row_top = jnp.max(scores, axis=1, keepdims=True)
        weights = to_low(jnp.exp(scores - row_top))
        weights_out[side] = weights
        summed = contract(weights, value_wide, 1, 0)
        inverse = 1.0 / summed[:, LANES : 2 * LANES]
        contexts.append(summed[:, :LANES] * inverse)
        stats = jnp.where(lane == 2 * pair + side, inverse, stats)
    stats_out[...] = stats
    context = pick_half(contexts[0], contexts[1])
    context_out[...] = to_low(context)
    gated = to_low(context * gate_row[:, columns])
    attn_part = contract(gated, weight_out[...], 1, 0)

    @pl.when(pair == 0)
    def _():
        total[...] = attn_part

    @pl.when(pair > 0)
    def _():
        total[...] += attn_part

    @pl.when(pair < own_pairs)
    def _():
        gated_own_out[...] = gated

    @pl.when(pair >= own_pairs)
    def _():
        gated_peer_out[...] = gated

    @pl.when(pair == pl.num_programs(0) - 1)
    def _():
        biased = total[...] + both(core, pack_own, pack_peer, pack.b_attn_out)
        biased_out[...] = biased
        gates = hidden_gates(core, pack, pack_own, pack_peer)
        mha_gate = scalar_gate(pack, pack_own, 0)
        resid = x_nat[...].astype(f32) + biased * (mha_gate * gates)
        normed, inv_scale = norm_forward(resid)
        normed_out[...] = normed
        gain = both(core, pack_own, pack_peer, pack.gain_one)
        shift = both(core, pack_own, pack_peer, pack.shift_one)
        hidden_out[...] = to_low((normed * gain + shift) * gates)
        stats_out[...] = jnp.where(lane == LANES - 1, inv_scale, stats)


def gelu_parts(pre_act):
    whole = 0.5 + 0.5 * lax.erf(pre_act * (0.5**0.5))
    return whole, jnp.exp(-0.5 * pre_act * pre_act) * (1.0 / math.sqrt(2.0 * math.pi))


def ffn_forward_kernel(
    pack,
    core_ref,
    hidden,
    normed,
    up_own,
    up_peer,
    down_own,
    down_peer,
    pack_own,
    pack_peer,
    teacher_own,
    teacher_peer,
    valid,
    mixed_own_out,
    mixed_peer_out,
    active_out,
    slope_out,
    output_own,
    output_peer,
    grad_resid_out,
    grad_ffn_out,
    sums_out,
    total,
    normed_in,
    target,
    sems,
):
    step = pl.program_id(0)
    core = core_ref[0]
    own_steps = pl.num_programs(0) // 2
    width = pack.width
    copies = (
        pltpu.make_async_copy(normed, normed_in, sems.at[2]),
        *rows_in(core, width, teacher_own, teacher_peer, target, sems),
    )

    def tile(at, up_ref, down_ref, pack_ref, mixed_ref):
        spot = pl.multiple_of(at * TILE, TILE)

        def cut(place):
            return pack_ref[:, pl.ds(place[0] + spot, TILE)]

        pre_act = contract(hidden[...], up_ref[...], 1, 0) + cut(pack.b_up)
        whole, density = gelu_parts(pre_act)
        active = pre_act * whole
        unit_gate = hard_concrete(cut(pack.unit_noise), cut(pack.unit_alpha))
        mixed = to_low(active * unit_gate)
        mixed_ref[...] = mixed
        active_out[...] = to_low(active)
        slope_out[...] = to_low((whole + pre_act * density) * unit_gate)
        return contract(mixed, down_ref[...], 1, 0)

    @pl.when(step == 0)
    def _():
        for copy in copies:
            copy.start()
        total[...] = tile(step, up_own, down_own, pack_own, mixed_own_out)

    @pl.when((step > 0) & (step < own_steps))
    def _():
        total[...] += tile(step, up_own, down_own, pack_own, mixed_own_out)

    @pl.when(step >= own_steps)
    def _():
        total[...] += tile(step - own_steps, up_peer, down_peer, pack_peer, mixed_peer_out)

    @pl.when(step == pl.num_programs(0) - 1)
    def _():
        gates = hidden_gates(core, pack, pack_own, pack_peer)
        ffn_gate = scalar_gate(pack, pack_own, 2)

        def vector(spot):
            return both(core, pack_own, pack_peer, spot)

        for copy in copies:
            copy.wait()
        biased = total[...] + vector(pack.b_down)
        hidden_one = (normed_in[...] * vector(pack.gain_one) + vector(pack.shift_one)) * gates
        normed_two, inv_two = norm_forward(hidden_one + biased * (ffn_gate * gates))
        gain = vector(pack.gain_two)
        final = (normed_two * gain + vector(pack.shift_two)) * gates
        final_low = to_low(final)

        def split(own_ref, peer_ref, values_in):
            @pl.when(core == 0)
            def _():
                own_ref[...] = values_in[:, :width]
                peer_ref[...] = values_in[:, width:]

            @pl.when(core == 1)
            def _():
                own_ref[...] = values_in[:, width:]
                peer_ref[...] = values_in[:, :width]

        split(output_own, output_peer, final_low)
        valid_side = to_side(token_line(valid, core))
        grad_final = (final - target[...].astype(f32)) * valid_side
        grad_resid = norm_back(grad_final * (gates * gain), normed_two, inv_two)
        grad_resid_out[...] = grad_resid
        grad_ffn_out[...] = to_low(grad_resid * (ffn_gate * gates))
        sums_out[0:1, :] = column_sum(grad_final * normed_two)
        sums_out[1:2, :] = column_sum(grad_final)
        sums_out[2:3, :] = column_sum(grad_resid * biased)
        sums_out[3:4, :] = column_sum(grad_resid)


def ffn_pre_kernel(
    pack,
    core_ref,
    grad_ffn,
    active,
    slope,
    down_own,
    down_peer,
    grad_pre_own,
    grad_pre_peer,
    unit_sums_out,
):
    step = pl.program_id(0)
    core = core_ref[0]
    own_steps = pl.num_programs(0) // 2
    units = pack.units

    def tile(at, side, down_ref, pre_ref):
        grad_mixed = contract(grad_ffn[...], down_ref[...], 1, 1)
        grad_pre = to_low(grad_mixed * slope[...].astype(f32))
        pre_ref[...] = grad_pre
        spot = pl.multiple_of(side * units + at * TILE, TILE)
        unit_sums_out[0:1, pl.ds(spot, TILE)] = column_sum(grad_mixed * active[...].astype(f32))
        unit_sums_out[1:2, pl.ds(spot, TILE)] = column_sum(grad_pre.astype(f32))

    @pl.when(step < own_steps)
    def _():
        tile(step, core, down_own, grad_pre_own)

    @pl.when(step >= own_steps)
    def _():
        tile(step - own_steps, 1 - core, down_peer, grad_pre_peer)


def ffn_backward_kernel(
    pack,
    core_ref,
    grad_pre_own,
    grad_pre_peer,
    grad_resid_two,
    normed,
    biased,
    stats,
    up_own,
    up_peer,
    pack_own,
    pack_peer,
    grad_resid_out,
    grad_attn_out,
    sums_out,
    total,
    resid_in,
    normed_in,
    biased_in,
    sems,
):
    step = pl.program_id(0)
    core = core_ref[0]
    own_steps = pl.num_programs(0) // 2
    copies = (
        pltpu.make_async_copy(grad_resid_two, resid_in, sems.at[0]),
        pltpu.make_async_copy(normed, normed_in, sems.at[1]),
        pltpu.make_async_copy(biased, biased_in, sems.at[2]),
    )

    @pl.when(step == 0)
    def _():
        for copy in copies:
            copy.start()
        total[...] = contract(grad_pre_own[...], up_own[...], 1, 1)

    @pl.when((step > 0) & (step < own_steps))
    def _():
        total[...] += contract(grad_pre_own[...], up_own[...], 1, 1)

    @pl.when(step >= own_steps)
    def _():
        total[...] += contract(grad_pre_peer[...], up_peer[...], 1, 1)

    @pl.when(step == pl.num_programs(0) - 1)
    def _():
        gates = hidden_gates(core, pack, pack_own, pack_peer)
        mha_gate = scalar_gate(pack, pack_own, 0)
        gain = both(core, pack_own, pack_peer, pack.gain_one)
        for copy in copies:
            copy.wait()
        grad_hidden = resid_in[...] + total[...]
        normed_one = normed_in[...]
        sums_out[0:1, :] = column_sum(grad_hidden * normed_one)
        sums_out[1:2, :] = column_sum(grad_hidden)
        inv_scale = stats[:, LANES - 1 : LANES]
        grad_resid = norm_back(grad_hidden * (gates * gain), normed_one, inv_scale)
        grad_resid_out[...] = grad_resid
        grad_attn_out[...] = to_low(grad_resid * (mha_gate * gates))
        sums_out[2:3, :] = column_sum(grad_resid * biased_in[...])
        sums_out[3:4, :] = column_sum(grad_resid)


def attend_back_kernel(
    pack,
    side_is_own,
    core_ref,
    weights,
    query_ref,
    key_ref,
    value_ref,
    context_ref,
    stats,
    grad_attn,
    wa_ref,
    pack_own,
    pack_peer,
    out_ref,
    sums_out,
    gate_row,
):
    at = pl.program_id(0)
    core = core_ref[0]
    width = pack.width
    pair = at if side_is_own else at + pl.num_programs(0)

    @pl.when(at == 0)
    def _():
        gate_row[...] = head_row(pack, pack_own, pack_peer, width // HD)

    columns = pl.ds(pl.multiple_of(pair * LANES, LANES), LANES)
    lane = lax.broadcasted_iota(jnp.int32, (1, LANES), 1)

    query, key, value = query_ref[...], key_ref[...], value_ref[...]
    context = context_ref[...].astype(f32)
    grad_context = contract(grad_attn[...], wa_ref[...], 1, 1)
    spot = pl.ds(pl.multiple_of(at * LANES, LANES), LANES)
    sums_out[0:1, spot] = column_sum(grad_context * context)
    inverses = [
        row_sum(jnp.where(lane == 2 * pair + side, stats[...], 0.0)) for side in range(2)
    ]
    grad_low = to_low(grad_context * gate_row[:, columns] * pick_half(inverses[0], inverses[1]))
    product = grad_low.astype(f32) * context
    found = []
    for side in range(2):
        mask = half_mask(side, f32)
        level = row_sum(product * mask)
        grad_probs = contract(grad_low * mask.astype(bf16), value, 1, 1)
        chosen = weights[side]
        grad_raw = to_low(chosen.astype(f32) * (grad_probs - level))
        found.append(
            (
                contract(grad_raw, key, 1, 0),
                contract(grad_raw, query, 0, 0),
                contract(chosen, grad_low, 0, 0),
            )
        )
    grad_query = to_low(pick_half(found[0][0], found[1][0]) * HD ** (-0.5))
    grad_key = to_low(pick_half(found[0][1], found[1][1]))
    grad_value = to_low(pick_half(found[0][2], found[1][2]))
    for place, grad in enumerate((grad_query, grad_key, grad_value)):
        at_lane = pl.multiple_of(place * width + at * LANES, LANES)
        out_ref[:, pl.ds(at_lane, LANES)] = grad
    sums_out[1:2, spot] = column_sum(grad_query.astype(f32))
    sums_out[2:3, spot] = column_sum(grad_value.astype(f32))


def down_grad_kernel(bit_ref, mixed, mixed_near, grad, grad_near, sent_out, kept_out):
    summed = to_low(
        contract(mixed[...], grad[...], 0, 0) + contract(mixed_near[...], grad_near[...], 0, 0)
    )
    first = pl.program_id(0) < pl.num_programs(0) // 2

    @pl.when(first)
    def _():
        sent_out[...] = summed

    @pl.when(jnp.logical_not(first))
    def _():
        kept_out[...] = summed


def attn_out_grad_kernel(bit_ref, gated, gated_near, grad, grad_near, sent_out, kept_out):
    width = gated.shape[1]
    part = width // 4
    summed = to_low(
        contract(gated[...], grad[...], 0, 0) + contract(gated_near[...], grad_near[...], 0, 0)
    )

    def put(ref):
        for at in range(4):
            ref[:, at * width : (at + 1) * width] = summed[at * part : (at + 1) * part]

    @pl.when(pl.program_id(0) == 0)
    def _():
        put(sent_out)

    @pl.when(pl.program_id(0) == 1)
    def _():
        put(kept_out)


def attend_grad_kernel(
    half_ref,
    core_ref,
    x_own,
    x_peer,
    grad,
    grad_near,
    out_ref,
    source,
    sem,
):
    core = core_ref[0]

    @pl.when(half_ref[0] == core)
    def _():
        copy = pltpu.make_async_copy(x_own, source, sem)
        copy.start()
        copy.wait()

    @pl.when(half_ref[0] != core)
    def _():
        copy = pltpu.make_async_copy(x_peer, source, sem)
        copy.start()
        copy.wait()

    summed = contract(own_rows(source, core), grad[...], 0, 0) + contract(
        own_rows(source, 1 - core), grad_near[...], 0, 0
    )
    out_ref[...] = to_low(summed)


def input_grad_kernel(
    width,
    core_ref,
    grad_resid,
    grad_own,
    grad_peer,
    wq_own,
    wk_own,
    wv_own,
    wq_peer,
    wk_peer,
    wv_peer,
    own_out,
    peer_out,
):
    core = core_ref[0]
    summed = grad_resid[...]
    for grad, weights in (
        (grad_own, (wq_own, wk_own, wv_own)),
        (grad_peer, (wq_peer, wk_peer, wv_peer)),
    ):
        for place, weight in enumerate(weights):
            summed = summed + contract(
                grad[:, place * width : (place + 1) * width], weight[...], 1, 1
            )

    @pl.when(core == 0)
    def _():
        own_out[...] = summed[:, :width]
        peer_out[...] = summed[:, width:]

    @pl.when(core == 1)
    def _():
        own_out[...] = summed[:, width:]
        peer_out[...] = summed[:, :width]


def place_kernel(bit_ref, half, other, out_ref):
    step = pl.program_id(0)

    @pl.when(step < 2)
    def _():
        out_ref[...] = half[...].astype(f32)

    @pl.when(step >= 2)
    def _():
        out_ref[...] = other[...].astype(f32)


def place_up_kernel(bit_ref, half, other, up_out, attn_out):
    width = attn_out.shape[1]
    rows = up_out.shape[0]
    part = width // 4

    def put(ref):
        up_out[...] = ref[:rows, :].astype(f32)
        for at in range(4):
            attn_out[at * part : (at + 1) * part, :] = ref[
                rows:, at * width : (at + 1) * width
            ].astype(f32)

    @pl.when(pl.program_id(0) == 0)
    def _():
        put(half)

    @pl.when(pl.program_id(0) == 1)
    def _():
        put(other)


def place_attend_kernel(bit_ref, half, other, query_out, key_out, value_out):
    width = query_out.shape[1]

    def put(ref):
        for at, out in enumerate((query_out, key_out, value_out)):
            out[...] = ref[:, at * width : (at + 1) * width].astype(f32)

    @pl.when(pl.program_id(0) == 0)
    def _():
        put(half)

    @pl.when(pl.program_id(0) == 1)
    def _():
        put(other)


def finish_kernel(
    pack,
    core_ref,
    sums,
    pack_own,
    pack_peer,
    b_query,
    b_value,
    b_attn_out,
    gain_one,
    shift_one,
    b_up,
    b_down,
    gain_two,
    shift_two,
    head_gate,
    mha_gate,
    unit_gate,
    ffn_gate,
    hidden_gate,
    head_alpha,
    mha_alpha,
    unit_alpha,
    ffn_alpha,
    hidden_alpha,
    share_out,
    penalty_out,
):
    core = core_ref[0]
    width, units = pack.width, pack.units
    columns = pl.ds(pl.multiple_of(core * width, LANES), width)
    heads = width // HD

    def put(out_ref, line):
        out_ref[...] = line.reshape(out_ref.shape)

    def own(row):
        return sums[row : row + 1, columns]

    def vector(spot):
        return take(pack_own, spot)

    gates = hard_concrete(vector(pack.hidden_noise), vector(pack.hidden_alpha))
    mha, ffn = scalar_gate(pack, pack_own, 0), scalar_gate(pack, pack_own, 2)
    put(gain_two, gates * own(0))
    put(shift_two, gates * own(1))
    put(b_down, (ffn * gates) * own(3))
    put(gain_one, gates * own(4))
    put(shift_one, gates * own(5))
    put(b_attn_out, (mha * gates) * own(7))
    put(b_query, own(9))
    put(b_value, own(10))
    grad_hidden = (
        vector(pack.gain_two) * own(0)
        + vector(pack.shift_two) * own(1)
        + ffn * own(2)
        + vector(pack.gain_one) * own(4)
        + vector(pack.shift_one) * own(5)
        + mha * own(6)
    )
    put(hidden_gate, grad_hidden)
    all_gates = hidden_gates(core, pack, pack_own, pack_peer)
    grad_ffn_gate = row_sum(all_gates * sums[2:3, :])
    grad_mha_gate = row_sum(all_gates * sums[6:7, :])
    put(ffn_gate, grad_ffn_gate)
    put(mha_gate, grad_mha_gate)

    unit_rows = units // (2 * width)

    def unit_line(first):
        at = first + core * unit_rows
        return jnp.concatenate([sums[pl.ds(at + k, 1), :] for k in range(unit_rows)], axis=1)

    grad_unit = unit_line(11)
    put(b_up, unit_line(11 + 2 * unit_rows))
    put(unit_gate, grad_unit)
    by_head = own(8)
    lane = lax.broadcasted_iota(jnp.int32, (1, LANES), 1)
    grad_head = jnp.zeros((1, LANES), f32)
    for at in range(heads):
        grad_head = jnp.where(
            lane == at, row_sum(by_head[:, at * HD : (at + 1) * HD]), grad_head
        )
    put(head_gate, grad_head[:, :heads])

    numbers = vector(pack.scalars)
    mha_open, ffn_open = open_share(numbers[:, 0:1]), open_share(numbers[:, 2:3])
    first_weight, second_weight = numbers[:, 4:5], numbers[:, 5:6]

    def open_total(spot, count):
        return row_sum(open_share(take(pack_own, spot)[:, :count])) + row_sum(
            open_share(take(pack_peer, spot)[:, :count])
        )

    head_sum = open_total(pack.head_alpha, heads)
    unit_sum = open_total(pack.unit_alpha, units)
    hidden_sum = open_total(pack.hidden_alpha, width)
    model, inner = 2.0 * width, 2.0 * units
    scale = 1.0 / ((4.0 * model + 2.0 * inner) * model)
    kept = 4.0 * HD * mha_open * head_sum + 2.0 * ffn_open * unit_sum
    share = kept * hidden_sum * scale
    gap = share - target_share
    put(share_out, share)
    put(penalty_out, first_weight * gap + second_weight * gap * gap)
    slope = (first_weight + 2.0 * second_weight * gap) * scale
    by_heads = slope * hidden_sum * (4.0 * HD)
    by_units = slope * hidden_sum * 2.0

    def alpha_grad(noise, alpha, grad_gate, grad_open):
        opened = open_share(alpha)
        return gate_slope(noise, alpha) * grad_gate + grad_open * (opened * (1.0 - opened))

    put(
        head_alpha,
        alpha_grad(
            vector(pack.head_noise), vector(pack.head_alpha), grad_head, by_heads * mha_open
        )[:, :heads],
    )
    put(
        unit_alpha,
        alpha_grad(
            vector(pack.unit_noise), vector(pack.unit_alpha), grad_unit, by_units * ffn_open
        ),
    )
    put(
        hidden_alpha,
        alpha_grad(
            vector(pack.hidden_noise), vector(pack.hidden_alpha), grad_hidden, slope * kept
        ),
    )
    put(
        mha_alpha,
        alpha_grad(numbers[:, 1:2], numbers[:, 0:1], grad_mha_gate, by_heads * head_sum),
    )
    put(
        ffn_alpha,
        alpha_grad(numbers[:, 3:4], numbers[:, 2:3], grad_ffn_gate, by_units * unit_sum),
    )


def full(shape):
    return pl.BlockSpec(shape, lambda *at: (0,) * len(shape), pipeline_mode=pl.Buffered(1))


def anywhere():
    return pl.BlockSpec(memory_space=pl.ANY)


def every(shape, dim):
    return pl.BlockSpec(shape, lambda i: tuple(i if d == dim else 0 for d in range(2)))


def sides(steps):
    def early(shape, dim):
        return pl.BlockSpec(
            shape, lambda i: tuple(jnp.minimum(i, steps - 1) if d == dim else 0 for d in range(2))
        )

    def late(shape, dim):
        return pl.BlockSpec(
            shape, lambda i: tuple(jnp.maximum(i - steps, 0) if d == dim else 0 for d in range(2))
        )

    return early, late


def one_number():
    return pl.BlockSpec(memory_space=pltpu.SMEM)


def shaped(shape, dtype):
    return jax.ShapeDtypeStruct(shape, dtype)


def far(struct):
    return pltpu.HBM(struct.shape, struct.dtype)


ORDER = (
    *("K3a", "KD", "K3b", "KU", "hD", "K4a", "Kao", "qD", "K4b", "hU", "KAs", "sD", "qU", "KAk"),
    *("S0", "hA", "sD", "S", "K6", "sU", "qA", "sD", "S", "O", "sU", "sA", "wD", "S", "sU", "sA"),
    *("sA", "pD", "S", "wU", "wA", "F", "pU", "pA"),
)
ON_PATH = ("D", "U", "A")


class Order:
    def __init__(self):
        self.last = ()
        self.share = 1.0

    def tie(self, values_in):
        if not self.last:
            return values_in
        return lax.optimization_barrier((values_in, *self.last))[0]

    def mark(self, *values_in):
        self.last = values_in


def call(order, kernel, grid, in_specs, out_specs, out_shape, scratch, cost, args, mib=34):
    out = pl.pallas_call(
        kernel,
        grid=grid,
        in_specs=in_specs,
        out_specs=out_specs,
        out_shape=out_shape,
        scratch_shapes=scratch,
        compiler_params=pltpu.CompilerParams(vmem_limit_bytes=mib * 2**20),
        cost_estimate=pl.CostEstimate(
            flops=int(cost[0] * 1e9 * order.share),
            bytes_accessed=int(cost[1] * 1e6 * order.share),
            transcendentals=0,
        ),
    )(order.tie(args[0]), *args[1:])
    order.mark(jax.tree.leaves(out)[-1])
    return out


def call_by_half(order, kernel, grid, in_specs, out_specs, out_shape, cost, half, args, mib=34):
    out = pl.pallas_call(
        kernel,
        grid_spec=pltpu.PrefetchScalarGridSpec(
            num_scalar_prefetch=1, grid=grid, in_specs=in_specs, out_specs=out_specs
        ),
        out_shape=out_shape,
        compiler_params=pltpu.CompilerParams(vmem_limit_bytes=mib * 2**20),
        cost_estimate=pl.CostEstimate(
            flops=int(cost[0] * 1e9 * order.share),
            bytes_accessed=int(cost[1] * 1e6 * order.share),
            transcendentals=0,
        ),
    )(order.tie(half), *args)
    order.mark(jax.tree.leaves(out)[-1])
    return out


def swap_pairs(core_masks):
    rows, cores = lax.axis_size("rows"), lax.axis_size("hid")
    return [
        (row * cores + core, (row ^ core_masks[core]) * cores + core)
        for row in range(rows)
        for core in range(cores)
    ]


def swap(values_in, core_masks):
    return lax.ppermute(values_in, ("rows", "hid"), swap_pairs(core_masks))


def along(values_in, steps):
    rows, cores = lax.axis_size("rows"), lax.axis_size("hid")
    pairs = [
        (row * cores + core, (row + 4 * (steps[row // 4 % 4] - row // 4 % 4)) * cores + core)
        for row in range(rows)
        if row // 4 % 4 in steps
        for core in range(cores)
    ]
    return lax.ppermute(values_in, ("rows", "hid"), pairs)


def in_hbm(values_in):
    return pltpu.with_memory_space_constraint(values_in, pltpu.HBM)


def near(values_in):
    return lax.ppermute(values_in, "hid", [(0, 1), (1, 0)])


def spread_masks():
    rest = lax.axis_size("rows") // 4
    masks = [4 * (2**k * 2 - 1) for k in range(rest.bit_length() - 1)]
    return [(masks[k], masks[len(masks) - 1 - k]) for k in range(len(masks))]


def add_low(first, second):
    return to_low(first.astype(f32) + second.astype(f32))


def pick(values_in, at):
    return lax.dynamic_index_in_dim(values_in, at, 0, keepdims=False)


class RowSum:
    def __init__(self, order, sent_half, first_bit, second_bit):
        self.order = order
        self.first_bit, self.second_bit = first_bit, second_bit
        self.near = swap(sent_half, (1, 2))

    def halve(self, kept):
        at = self.second_bit
        kept = self.order.tie(kept)
        to_send = add_low(pick(kept, 1 - at), pick(self.near, 1 - at))
        self.own = add_low(pick(kept, at), pick(self.near, at))
        self.near = swap(to_send, (2, 1))
        self.order.mark(to_send, self.own)

    def halve_with(self, kept, below, below_near):
        kept = add_low(self.order.tie(kept), self.near)
        below = add_low(self.order.tie(below), below_near)
        rows = (kept.shape[0] + below.shape[0]) // 2
        first, second = kept[:rows], jnp.concatenate((kept[rows:], below), axis=0)
        to_send = jnp.where(self.second_bit == 0, second, first)
        self.own = jnp.where(self.second_bit == 0, first, second)
        self.near = swap(to_send, (2, 1))
        self.order.mark(to_send, self.own)

    def quarter(self, path=False):
        self.own = add_low(self.order.tie(self.own), self.near)
        masks = spread_masks()
        self.left = [partial(swap, core_masks=pair) for pair in masks]
        self.inner = None
        if path:
            steps = [{0: 1, 3: 2}, {1: 2, 2: 1}, {1: 0, 2: 3}]
            self.left = [partial(along, steps=item) for item in steps] + self.left[2:]
            at = lax.rem(lax.axis_index("rows") // 4, 4)
            self.inner = (at == 1) | (at == 2)
            self.until_out = 3
        self.near = self.left.pop(0)(self.own)
        self.order.mark(self.own)

    def spread(self):
        own = self.order.tie(self.own)
        if self.inner is not None:
            self.until_out -= 1
        if self.inner is not None and self.until_out == 0:
            self.own = jnp.where(self.inner, own, self.near)
        else:
            self.own = add_low(own, self.near)
        self.near = self.left.pop(0)(self.own) if self.left else swap(self.own, (2, 1))
        self.order.mark(self.own)

    def spread_all(self):
        while self.left:
            self.spread()
        self.spread()

    def widen(self):
        own, near = self.order.tie(self.own), self.near
        self.half = jnp.where(
            self.second_bit == 0, jnp.stack((own, near)), jnp.stack((near, own))
        )
        self.order.mark(self.half)
        self.near = swap(self.half, (1, 2))

    def parts(self):
        return self.half, self.near


class SmallSum:
    def __init__(self, order, values_in):
        self.order, self.own = order, values_in
        self.left = [(1, 2), (2, 1)] + spread_masks()
        self.near = near(values_in)

    def step(self):
        self.own = self.order.tie(self.own) + self.near
        self.order.mark(self.own)
        if self.left:
            self.near = swap(self.own, self.left.pop(0))
            return True
        return False

    def rest(self):
        while self.step():
            pass
        return self.own


def body(
    hidden_in,
    teacher,
    segment_ids,
    valid_mask,
    w_query,
    b_query,
    w_key,
    w_value,
    b_value,
    w_attn_out,
    b_attn_out,
    gain_one,
    shift_one,
    w_up,
    b_up,
    w_down,
    b_down,
    gain_two,
    shift_two,
    head_alpha,
    mha_alpha,
    unit_alpha,
    ffn_alpha,
    hidden_alpha,
    head_noise,
    mha_noise,
    unit_noise,
    ffn_noise,
    hidden_noise,
    lagrange,
):
    model, width = w_query.shape
    units = w_up.shape[1]
    heads = width // HD
    pairs = model // LANES
    tokens = hidden_in.shape[0] // 2
    pack = Pack(width, units)
    order = Order()
    core = lax.axis_index("hid")
    row = lax.axis_index("rows")
    core_at = jnp.reshape(core, (1,)).astype(jnp.int32)
    low_bit, high_bit = row & 1, (row >> 1) & 1
    first_bit = jnp.where(core == 0, low_bit, high_bit).astype(jnp.int32)
    second_bit = jnp.where(core == 0, high_bit, low_bit).astype(jnp.int32)

    packed = (
        (b_query, pack.b_query, 0),
        (b_value, pack.b_value, 0),
        (b_attn_out, pack.b_attn_out, 0),
        (gain_one, pack.gain_one, 0),
        (shift_one, pack.shift_one, 0),
        (b_down, pack.b_down, 0),
        (gain_two, pack.gain_two, 0),
        (shift_two, pack.shift_two, 0),
        (hidden_alpha, pack.hidden_alpha, 0),
        (hidden_noise, pack.hidden_noise, 0),
        (b_up, pack.b_up, 0),
        (unit_alpha, pack.unit_alpha, 0),
        (unit_noise, pack.unit_noise, 0),
        (head_alpha, pack.head_alpha, 0),
        (head_noise, pack.head_noise, 0),
        (mha_alpha, pack.scalars, 0),
        (mha_noise, pack.scalars, 1),
        (ffn_alpha, pack.scalars, 2),
        (ffn_noise, pack.scalars, 3),
        (lagrange, pack.scalars, 4),
    )
    pack_own = call(
        order,
        partial(pack_kernel, pack, [item[1:] for item in packed]),
        (),
        [full(item[0].shape) if item[0].shape[0] > 1 else one_number() for item in packed],
        full((1, pack.total)),
        shaped((1, pack.total), f32),
        [],
        (0.001, 0.1, 0),
        tuple(in_hbm(item[0]) if item[0].shape[0] > 1 else item[0] for item in packed),
        mib=4,
    )
    x_peer = near(hidden_in)
    pack_peer = near(pack_own)
    wq_peer, wk_peer, wv_peer = near(w_query), near(w_key), near(w_value)
    wa_peer = near(w_attn_out)
    first_peers = (x_peer, pack_peer, wq_peer, wk_peer, wv_peer, wa_peer)
    *first_peers, up_sent, down_sent, teacher_sent = lax.optimization_barrier(
        (*first_peers, w_up, w_down, teacher)
    )
    x_peer, pack_peer, wq_peer, wk_peer, wv_peer, wa_peer = first_peers
    up_peer, down_peer, teacher_peer = near(up_sent), near(down_sent), near(teacher_sent)
    hidden_in, x_peer, teacher, teacher_peer = (
        in_hbm(item) for item in (hidden_in, x_peer, teacher, teacher_peer)
    )
    w_query, w_key, w_value, w_attn_out, w_up, w_down = (
        in_hbm(item) for item in (w_query, w_key, w_value, w_attn_out, w_up, w_down)
    )
    wq_peer, wk_peer, wv_peer, wa_peer, up_peer, down_peer = (
        in_hbm(item) for item in (wq_peer, wk_peer, wv_peer, wa_peer, up_peer, down_peer)
    )
    segments = in_hbm(segment_ids.reshape(-1, LANES))
    valid = in_hbm(valid_mask.reshape(-1, LANES))
    packs = [full((1, pack.total))] * 2
    pair_early, pair_late = sides(pairs // 2)
    token_low = shaped((tokens, model), bf16)
    token_wide = shaped((tokens, model), f32)
    token_half = shaped((tokens, width), bf16)

    (
        weights,
        query,
        key,
        value,
        context,
        gated_own,
        gated_peer,
        stats,
        biased,
        normed,
        hidden,
    ) = call(
        order,
        partial(attend_kernel, pack),
        (pairs,),
        [one_number()]
        + [anywhere()] * 2
        + [pair_early((model, LANES), 1)] * 3
        + [pair_late((model, LANES), 1)] * 3
        + [pair_early((LANES, model), 0), pair_late((LANES, model), 0)]
        + packs
        + [full(segments.shape)] * 2,
        [pl.BlockSpec((2, BLOCK, BLOCK), lambda i: (i, 0, 0))]
        + [every((tokens, LANES), 1)] * 4
        + [pair_early((tokens, LANES), 1), pair_late((tokens, LANES), 1)]
        + [full((tokens, LANES))]
        + [full((tokens, model))] * 3,
        [
            far(shaped((2 * pairs, BLOCK, BLOCK), bf16)),
            far(token_low),
            far(token_low),
            far(token_low),
            far(token_low),
            far(token_half),
            far(token_half),
            shaped((tokens, LANES), f32),
            far(token_wide),
            far(token_wide),
            token_low,
        ],
        [
            pltpu.VMEM((tokens, model), bf16),
            pltpu.VMEM((BLOCK, BLOCK), f32),
            pltpu.VMEM((1, model), f32),
            pltpu.VMEM((model, 3 * LANES), bf16),
            pltpu.VMEM((LANES, model), bf16),
            pltpu.VMEM((8, LANES), f32),
            pltpu.VMEM((tokens, model), f32),
            pltpu.SemaphoreType.DMA((2,)),
        ],
        (4.0, 20, 3),
        (
            core_at,
            hidden_in,
            x_peer,
            w_query,
            w_key,
            w_value,
            wq_peer,
            wk_peer,
            wv_peer,
            w_attn_out,
            wa_peer,
            pack_own,
            pack_peer,
            segments,
            valid,
        ),
    )
    normed, biased = in_hbm(normed), in_hbm(biased)
    hidden_near = near(hidden)
    gated_near = near(gated_peer)

    tiles = units // TILE
    early, late = sides(tiles)

    (
        mixed_own,
        mixed_peer,
        active,
        slope,
        output_own,
        output_peer,
        grad_resid_two,
        grad_ffn,
        sums_two,
    ) = call(
        order,
        partial(ffn_forward_kernel, pack),
        (2 * tiles,),
        [one_number(), full((tokens, model)), anywhere()]
        + [early((model, TILE), 1), late((model, TILE), 1)]
        + [early((TILE, model), 0), late((TILE, model), 0)]
        + packs
        + [anywhere()] * 2
        + [full(valid.shape)],
        [early((tokens, TILE), 1), late((tokens, TILE), 1)]
        + [every((tokens, TILE), 1)] * 2
        + [full((tokens, width))] * 2
        + [full((tokens, model))] * 2
        + [full((4, model))],
        [
            shaped((tokens, units), bf16),
            shaped((tokens, units), bf16),
            shaped((tokens, 2 * units), bf16),
            shaped((tokens, 2 * units), bf16),
            far(token_half),
            far(token_half),
            far(token_wide),
            token_low,
            shaped((4, model), f32),
        ],
        [
            pltpu.VMEM((tokens, model), f32),
            pltpu.VMEM((tokens, model), f32),
            pltpu.VMEM((tokens, model), bf16),
            pltpu.SemaphoreType.DMA((3,)),
        ],
        (5.0, 25, 3),
        (
            core_at,
            hidden,
            normed,
            w_up,
            up_peer,
            w_down,
            down_peer,
            pack_own,
            pack_peer,
            teacher,
            teacher_peer,
            valid,
        ),
    )
    grad_resid_two = in_hbm(grad_resid_two)
    mixed_near = near(mixed_peer)
    grad_ffn_near = near(grad_ffn)
    output_near = near(output_peer)
    up_rows = width + width // 4
    half_units = units // 2
    step_units = half_units // 2

    bit_at = jnp.reshape(first_bit, (1,))

    def at_half(i, steps, bit):
        return jnp.where(i < steps, 1 - bit[0], bit[0])

    def sent_then_kept(shape, steps, dim):
        return [
            pl.BlockSpec(
                shape,
                lambda i, t, at=at: tuple(at(i) if d == dim else 0 for d in range(2)),
            )
            for at in (
                lambda i: jnp.minimum(i, steps - 1),
                lambda i: jnp.maximum(i - steps, 0),
            )
        ]

    own_pairs = pairs // 2
    weights, query, key, value, context = (
        in_hbm(item) for item in (weights, query, key, value, context)
    )

    def attend_back(side_is_own, wa_ref):
        first = 0 if side_is_own else own_pairs
        return call(
            order,
            partial(attend_back_kernel, pack, side_is_own),
            (own_pairs,),
            [one_number(), pl.BlockSpec((2, BLOCK, BLOCK), lambda i: (i + first, 0, 0))]
            + [pl.BlockSpec((tokens, LANES), lambda i: (0, i + first))] * 4
            + [full((tokens, LANES)), full((tokens, model))]
            + [pl.BlockSpec((LANES, model), lambda i: (i, 0))]
            + packs,
            [full((tokens, 3 * width)), full((3, width))],
            [shaped((tokens, 3 * width), bf16), shaped((3, width), f32)],
            [pltpu.VMEM((1, model), f32)],
            (2.0, 10, 0),
            (
                core_at,
                weights,
                query,
                key,
                value,
                context,
                stats,
                grad_attn,
                wa_ref,
                pack_own,
                pack_peer,
            ),
            mib=18,
        )

    def attend_half(half):
        out = call(
            order,
            attend_grad_kernel,
            (),
            [one_number()] * 2 + [anywhere()] * 2 + [full((tokens, 3 * width))] * 2,
            full((width, 3 * width)),
            shaped((width, 3 * width), bf16),
            [pltpu.VMEM(hidden_in.shape, bf16), pltpu.SemaphoreType.DMA],
            (24, 100, 0),
            (jnp.reshape(half, (1,)), core_at, hidden_in, x_peer, grad_own, grad_near),
            mib=12,
        )
        return out.reshape(2, width // 2, 3 * width)

    def place(pieces):
        _, height, across = pieces[0].shape

        def block(at):
            return pl.BlockSpec((1, height, across), at)

        out = call_by_half(
            order,
            place_kernel,
            (4,),
            [
                block(lambda i, t: (jnp.minimum(i, 1), 0, 0)),
                block(lambda i, t: (jnp.maximum(i - 2, 0), 0, 0)),
            ],
            block(lambda i, t: (2 * lax.rem(t[0] + i // 2, 2) + lax.rem(i, 2), 0, 0)),
            shaped((4, height, across), f32),
            (0.001, 7),
            bit_at,
            pieces,
            mib=18,
        )
        return out.reshape(4 * height, across)

    def by_token(own, other):
        own = order.tie(own)
        out = jnp.where(
            core == 0, jnp.concatenate((own, other), axis=0), jnp.concatenate((other, own), axis=0)
        )
        order.mark(out)
        return out

    def by_half(pieces):
        return tuple(piece.reshape(-1, piece.shape[-1]) for piece in pieces)

    def own_half(shape, dim):
        return pl.BlockSpec(
            shape, lambda i, t: tuple(lax.rem(t[0] + i, 2) if d == dim else 0 for d in range(2))
        )

    grad_pre_own = grad_pre_peer = unit_sums = grad_pre_near = down_kept = down_chunk = None
    grad_resid_one = grad_attn = sums_one = grad_attn_near = up_kept = up_chunk = None
    grad_peer = sums_peer = grad_near = attn_kept = attn_near = grad_own = None
    sums_own = attend_chunk = attend_kept = small = input_own = input_peer = None
    input_near = output = grad_input = sum_down = finished = sum_up = None
    sum_attn = sum_query = sum_key = sum_value = None

    def units_back():
        nonlocal grad_pre_own, grad_pre_peer, unit_sums, grad_pre_near
        grad_pre_own, grad_pre_peer, unit_sums = call(
            order,
            partial(ffn_pre_kernel, pack),
            (2 * tiles,),
            [one_number(), full((tokens, model))]
            + [every((tokens, TILE), 1)] * 2
            + [early((TILE, model), 0), late((TILE, model), 0)],
            [early((tokens, TILE), 1), late((tokens, TILE), 1), full((2, 2 * units))],
            [
                shaped((tokens, units), bf16),
                shaped((tokens, units), bf16),
                shaped((2, 2 * units), f32),
            ],
            [],
            (50, 300, 0),
            (core_at, grad_ffn, active, slope, w_down, down_peer),
            mib=18,
        )
        grad_pre_near = near(grad_pre_peer)

    def down_grads():
        nonlocal down_kept, down_chunk
        by_units = pl.BlockSpec(
            (tokens, step_units), lambda i, t: (0, at_half(i, 2, t) * 2 + lax.rem(i, 2))
        )
        down_sent, down_kept = call_by_half(
            order,
            down_grad_kernel,
            (4,),
            [by_units, by_units] + [full((tokens, model))] * 2,
            sent_then_kept((step_units, model), 2, 0),
            [shaped((half_units, model), bf16)] * 2,
            (48, 180),
            bit_at,
            (mixed_own, mixed_near, grad_ffn, grad_ffn_near),
            mib=12,
        )
        down_sent, down_kept = (
            item.reshape(2, half_units // 2, model) for item in (down_sent, down_kept)
        )
        down_chunk = RowSum(order, down_sent, first_bit, second_bit)

    def ffn_back():
        nonlocal grad_resid_one, grad_attn, sums_one, grad_attn_near
        grad_resid_one, grad_attn, sums_one = call(
            order,
            partial(ffn_backward_kernel, pack),
            (2 * tiles,),
            [one_number()]
            + [early((tokens, TILE), 1), late((tokens, TILE), 1)]
            + [anywhere()] * 3
            + [full((tokens, LANES))]
            + [early((model, TILE), 1), late((model, TILE), 1)]
            + packs,
            [full((tokens, model))] * 2 + [full((4, model))],
            [far(token_wide), token_low, shaped((4, model), f32)],
            [pltpu.VMEM((tokens, model), f32)] * 4 + [pltpu.SemaphoreType.DMA((3,))],
            (2.5, 15, 0),
            (
                core_at,
                grad_pre_own,
                grad_pre_peer,
                grad_resid_two,
                normed,
                biased,
                stats,
                w_up,
                up_peer,
                pack_own,
                pack_peer,
            ),
            mib=20,
        )
        grad_attn_near = near(grad_attn)

    def up_grads():
        nonlocal up_kept, up_chunk
        by_features = pl.BlockSpec((tokens, width), lambda i, t: (0, at_half(i, 2, t)))
        by_units = pl.BlockSpec((tokens, half_units), lambda i, t: (0, lax.rem(i, 2)))
        up_sent, up_kept = call_by_half(
            order,
            down_grad_kernel,
            (4,),
            [by_features, by_features, by_units, by_units],
            sent_then_kept((width, half_units), 2, 1),
            [shaped((width, units), bf16)] * 2,
            (2.4, 12),
            bit_at,
            (hidden, hidden_near, grad_pre_own, grad_pre_near),
            mib=18,
        )
        up_chunk = RowSum(order, up_sent, first_bit, second_bit)

    def peer_heads():
        nonlocal grad_peer, sums_peer, grad_near
        grad_peer, sums_peer = attend_back(False, wa_peer)
        grad_near = near(grad_peer)

    def own_heads():
        nonlocal grad_own, sums_own
        grad_own, sums_own = attend_back(True, w_attn_out)

    def out_grads():
        nonlocal attn_kept, attn_near
        by_columns = pl.BlockSpec((tokens, width), lambda i, t: (0, at_half(i, 1, t)))
        attn_sent, attn_kept = call_by_half(
            order,
            attn_out_grad_kernel,
            (2,),
            [full((tokens, width))] * 2 + [by_columns] * 2,
            [full((width // 4, units))] * 2,
            [shaped((width // 4, units), bf16)] * 2,
            (0.6, 3),
            bit_at,
            (gated_own, gated_near, grad_attn, grad_attn_near),
            mib=8,
        )
        attn_near = swap(attn_sent, (1, 2))

    def send_attend():
        nonlocal attend_chunk
        attend_sent = attend_half(1 - first_bit)
        attend_chunk = RowSum(order, attend_sent, first_bit, second_bit)

    def keep_attend():
        nonlocal attend_kept
        attend_kept = attend_half(first_bit)

    def start_small():
        nonlocal small
        sums_attn = jnp.where(
            core == 0,
            jnp.concatenate((sums_own, sums_peer), axis=1),
            jnp.concatenate((sums_peer, sums_own), axis=1),
        )
        small = SmallSum(
            order,
            jnp.concatenate((sums_two, sums_one, sums_attn, unit_sums.reshape(-1, model)), axis=0),
        )

    def inputs_back():
        nonlocal input_own, input_peer, input_near
        input_own, input_peer = call(
            order,
            partial(input_grad_kernel, width),
            (),
            [one_number(), full((tokens, model))]
            + [full((tokens, 3 * width))] * 2
            + [full((model, width))] * 6,
            [full((tokens, width))] * 2,
            [shaped((tokens, width), f32)] * 2,
            [],
            (1.8, 8, 0),
            (
                core_at,
                in_hbm(grad_resid_one),
                grad_own,
                grad_peer,
                w_query,
                w_key,
                w_value,
                wq_peer,
                wk_peer,
                wv_peer,
            ),
            mib=16,
        )
        input_near = near(input_peer)

    def put_output():
        nonlocal output, grad_input
        output = by_token(output_own, output_near)
        grad_input = by_token(input_own, input_near)

    def finish_small():
        nonlocal finished
        small_sums = small.rest()
        sizes = (width,) * 5 + (units,) + (width,) * 3 + (heads, 1, units, 1, width)
        sizes = sizes + (heads, 1, units, 1, width, 1, 1)
        finished = call(
            order,
            partial(finish_kernel, pack),
            (),
            [one_number(), full(small_sums.shape)] + packs,
            [full((size,)) for size in sizes],
            [shaped((size,), f32) for size in sizes],
            [],
            (0.01, 0.3, 0.1),
            (core_at, small_sums, pack_own, pack_peer),
        )

    def place_down():
        nonlocal sum_down
        sum_down = place(down_chunk.parts())

    def place_up():
        nonlocal sum_up, sum_attn
        sum_up, sum_attn = call_by_half(
            order,
            place_up_kernel,
            (2,),
            [full((up_rows, units))] * 2,
            [own_half((width, units), 0), own_half((width, width), 1)],
            [shaped((model, units), f32), shaped((width, model), f32)],
            (0.001, 10),
            bit_at,
            by_half(up_chunk.parts()),
            mib=18,
        )

    def place_attend():
        nonlocal sum_query, sum_key, sum_value
        sum_query, sum_key, sum_value = call_by_half(
            order,
            place_attend_kernel,
            (2,),
            [full((width, 3 * width))] * 2,
            [own_half((width, width), 0)] * 3,
            [shaped((model, width), f32)] * 3,
            (0.001, 7),
            bit_at,
            by_half(attend_chunk.parts()),
            mib=18,
        )

    steps = dict(
        K3a=units_back,
        KD=down_grads,
        K3b=ffn_back,
        KU=up_grads,
        K4a=peer_heads,
        K4b=own_heads,
        Kao=out_grads,
        KAs=send_attend,
        KAk=keep_attend,
        S0=start_small,
        S=lambda: small.step(),
        K6=inputs_back,
        O=put_output,
        F=finish_small,
        hD=lambda: down_chunk.halve(down_kept),
        qD=lambda: down_chunk.quarter("D" in ON_PATH),
        sD=lambda: down_chunk.spread(),
        wD=lambda: down_chunk.widen(),
        pD=place_down,
        hU=lambda: up_chunk.halve_with(up_kept, attn_kept, attn_near),
        qU=lambda: up_chunk.quarter("U" in ON_PATH),
        sU=lambda: up_chunk.spread(),
        wU=lambda: up_chunk.widen(),
        pU=place_up,
        hA=lambda: attend_chunk.halve(attend_kept),
        qA=lambda: attend_chunk.quarter("A" in ON_PATH),
        sA=lambda: attend_chunk.spread(),
        wA=lambda: attend_chunk.widen(),
        pA=place_attend,
    )
    for name in ORDER:
        steps[name]()
    return (
        output,
        grad_input,
        sum_query,
        finished[0],
        sum_key,
        sum_value,
        finished[1],
        sum_attn,
        finished[2],
        finished[3],
        finished[4],
        sum_up,
        finished[5],
        sum_down,
        *finished[6:],
    )


def solution(mesh):
    in_specs = (
        P("rows", "hid"),
        P("rows", "hid"),
        P("rows"),
        P("rows"),
        P(None, "hid"),
        P("hid"),
        P(None, "hid"),
        P(None, "hid"),
        P("hid"),
        P("hid", None),
        P("hid"),
        P("hid"),
        P("hid"),
        P(None, "hid"),
        P("hid"),
        P("hid", None),
        P("hid"),
        P("hid"),
        P("hid"),
        P("hid"),
        P(),
        P("hid"),
        P(),
        P("hid"),
        P("hid"),
        P(),
        P("hid"),
        P(),
        P("hid"),
        P(),
    )
    out_specs = (
        P("rows", "hid"),
        P("rows", "hid"),
        P(None, "hid"),
        P("hid"),
        P(None, "hid"),
        P(None, "hid"),
        P("hid"),
        P("hid", None),
        P("hid"),
        P("hid"),
        P("hid"),
        P(None, "hid"),
        P("hid"),
        P("hid", None),
        P("hid"),
        P("hid"),
        P("hid"),
        P("hid"),
        P(),
        P("hid"),
        P(),
        P("hid"),
        P("hid"),
        P(),
        P("hid"),
        P(),
        P("hid"),
        P(),
        P(),
    )
    return jax.shard_map(body, mesh=mesh, in_specs=in_specs, out_specs=out_specs, check_vma=False)
```

```python
from functools import partial
import math

import jax
import jax.numpy as jnp
from jax import lax
from jax.experimental import pallas as pl
from jax.experimental.pallas import tpu as pltpu
from jax.sharding import PartitionSpec as P

HD = 64
BLOCK = 512
LANES = 128
TILE = 768

norm_eps = 1e-05
gate_temper = 2.0 / 3.0
stretch_low = -0.1
stretch_high = 1.1
target_share = 0.4
masked_score = -1000000000.0
open_shift = gate_temper * math.log(-stretch_low / stretch_high)


f32 = jnp.float32
bf16 = jnp.bfloat16


def to_low(values_in):
    return values_in.astype(bf16)


def contract(first, second, first_dim, second_dim):
    return lax.dot_general(
        first, second, (((first_dim,), (second_dim,)), ((), ())), preferred_element_type=f32
    )


def column_sum(values_in):
    return jnp.sum(values_in, axis=0, keepdims=True)


def row_sum(values_in):
    return jnp.sum(values_in, axis=1, keepdims=True)


def sigmoid(values_in):
    return 1.0 / (1.0 + jnp.exp(-values_in))


def stretched(gate_noise, log_alpha):
    relaxed = sigmoid(
        (jnp.log(gate_noise) - jnp.log(1.0 - gate_noise) + log_alpha) / gate_temper
    )
    return relaxed, relaxed * (stretch_high - stretch_low) + stretch_low


def hard_concrete(gate_noise, log_alpha):
    return jnp.clip(stretched(gate_noise, log_alpha)[1], 0.0, 1.0)


def gate_slope(gate_noise, log_alpha):
    relaxed, wide = stretched(gate_noise, log_alpha)
    slope = relaxed * (1.0 - relaxed) * ((stretch_high - stretch_low) / gate_temper)
    return jnp.where((wide > 0.0) & (wide < 1.0), slope, 0.0)


def open_share(log_alpha):
    return sigmoid(log_alpha - open_shift)


class Pack:
    def __init__(self, width, units):
        self.width, self.units = width, units
        at = 0
        for name in ("b_query", "b_value", "b_attn_out", "gain_one", "shift_one"):
            setattr(self, name, (at, width))
            at += width
        for name in ("b_down", "gain_two", "shift_two", "hidden_alpha", "hidden_noise"):
            setattr(self, name, (at, width))
            at += width
        for name in ("b_up", "unit_alpha", "unit_noise"):
            setattr(self, name, (at, units))
            at += units
        for name in ("head_alpha", "head_noise", "scalars"):
            setattr(self, name, (at, LANES))
            at += LANES
        self.total = at


def pack_kernel(pack, counts, *refs):
    out_ref = refs[-1]
    out_ref[...] = jnp.full(out_ref.shape, 0.5, f32)
    for ref, (spot, lane) in zip(refs[:-1], counts):
        size = ref.shape[0]
        at = slice(spot[0] + lane, spot[0] + lane + size)
        if size > 1:
            out_ref[:, at] = ref[...].reshape(1, size)
        else:
            out_ref[:, at] = jnp.full((1, 1), ref[0], f32)


def take(pack_ref, spot):
    return pack_ref[:, spot[0] : spot[0] + spot[1]]


def natural(core, own, peer):
    at_peer = core.astype(f32)
    at_own = 1.0 - at_peer
    return jnp.concatenate((own * at_own + peer * at_peer, peer * at_own + own * at_peer), axis=1)


def both(core, own_ref, peer_ref, spot):
    return natural(core, take(own_ref, spot), take(peer_ref, spot))


def hidden_gates(core, pack, own_ref, peer_ref):
    return hard_concrete(
        both(core, own_ref, peer_ref, pack.hidden_noise),
        both(core, own_ref, peer_ref, pack.hidden_alpha),
    )


def head_row(pack, pack_ref):
    gates = hard_concrete(take(pack_ref, pack.head_noise), take(pack_ref, pack.head_alpha))
    parts = [jnp.broadcast_to(gates[:, at : at + 1], (1, HD)) for at in range(pack.width // HD)]
    return jnp.concatenate(parts, axis=1)


def scalar_gate(pack, own_ref, at):
    numbers = take(own_ref, pack.scalars)
    return hard_concrete(numbers[:, at + 1 : at + 2], numbers[:, at : at + 1])


def half_mask(side, dtype):
    lane = lax.broadcasted_iota(jnp.int32, (1, LANES), 1)
    inside = (lane < HD) if side == 0 else (lane >= HD)
    return jnp.where(inside, 1.0, 0.0).astype(dtype)


def pick_half(first, second):
    lane = lax.broadcasted_iota(jnp.int32, (1, LANES), 1)
    return jnp.where(lane < HD, first, second)


def norm_back(grad_normed, normed, inv_scale):
    width = normed.shape[1]
    mean_grad = row_sum(grad_normed) * (1.0 / width)
    mean_both = row_sum(grad_normed * normed) * (1.0 / width)
    return inv_scale * (grad_normed - mean_grad - normed * mean_both)


def norm_forward(resid):
    width = resid.shape[1]
    row_mean = row_sum(resid) * (1.0 / width)
    row_var = row_sum(resid * resid) * (1.0 / width) - row_mean * row_mean
    inv_scale = lax.rsqrt(row_var + norm_eps)
    return (resid - row_mean) * inv_scale, inv_scale


def own_rows(ref, core):
    return ref[pl.ds(pl.multiple_of(core * BLOCK, BLOCK), BLOCK), :]


def token_line(ref, core):
    lanes_of = BLOCK // LANES
    rows = [ref[pl.ds(core * lanes_of + at, 1), :] for at in range(lanes_of)]
    return jnp.concatenate(rows, axis=1).astype(f32)


def to_side(line):
    return jnp.broadcast_to(line, (LANES, BLOCK)).T[:, 0:1]


def rows_in(core, width, own_ref, peer_ref, out_ref, sems):
    rows = pl.ds(pl.multiple_of(core * BLOCK, BLOCK), BLOCK)
    own_at = pl.multiple_of(core * width, LANES)
    peer_at = pl.multiple_of((1 - core) * width, LANES)
    return (
        pltpu.make_async_copy(own_ref.at[rows, :], out_ref.at[:, pl.ds(own_at, width)], sems.at[0]),
        pltpu.make_async_copy(
            peer_ref.at[rows, :], out_ref.at[:, pl.ds(peer_at, width)], sems.at[1]
        ),
    )


def attend_pair(
    pack, first, source, weight_refs, pack_ref, mask_bias, gate_row, stats, out_refs
):
    at = pl.program_id(0)
    spot = pl.multiple_of(at * LANES, LANES)

    def cut(place):
        return pack_ref[:, pl.ds(place[0] + spot, LANES)]

    wq_ref, wk_ref, wv_ref, wa_ref = weight_refs
    weights_out, query_out, key_out, value_out, context_out, gated_out = out_refs
    weight_in = jnp.concatenate((wq_ref[...], wk_ref[...], wv_ref[...]), axis=1)
    projected = contract(source, weight_in, 1, 0)
    query = to_low(projected[:, :LANES] + cut(pack.b_query)) * jnp.asarray(HD ** (-0.5), bf16)
    key = to_low(projected[:, LANES : 2 * LANES])
    value = to_low(projected[:, 2 * LANES :] + cut(pack.b_value))
    query_out[...] = query
    key_out[...] = key
    value_out[...] = value
    value_wide = jnp.concatenate((value, jnp.ones((BLOCK, LANES), bf16)), axis=1)
    contexts = []
    lane = lax.broadcasted_iota(jnp.int32, (1, LANES), 1)
    for side in range(2):
        scores = contract(query * half_mask(side, bf16), key, 1, 1) + mask_bias[...]
        row_top = jnp.max(scores, axis=1, keepdims=True)
        weights = to_low(jnp.exp(scores - row_top))
        weights_out[side] = weights
        summed = contract(weights, value_wide, 1, 0)
        inverse = 1.0 / summed[:, LANES : 2 * LANES]
        contexts.append(summed[:, :LANES] * inverse)
        stats = jnp.where(lane == 2 * (first + at) + side, inverse, stats)
    context = pick_half(contexts[0], contexts[1])
    context_out[...] = to_low(context)
    gated = to_low(context * gate_row[:, pl.ds(spot, LANES)])
    gated_out[...] = gated
    return contract(gated, wa_ref[...], 1, 0), stats


def attend_own_kernel(
    pack,
    core_ref,
    x_own,
    x_peer,
    wq_ref,
    wk_ref,
    wv_ref,
    wa_ref,
    pack_ref,
    segments,
    valid,
    weights_out,
    query_out,
    key_out,
    value_out,
    context_out,
    gated_out,
    stats_out,
    x_nat,
    mask_bias,
    total,
    gate_row,
    sems,
):
    at = pl.program_id(0)
    core = core_ref[0]

    @pl.when(at == 0)
    def _():
        copies = rows_in(core, pack.width, x_own, x_peer, x_nat, sems)
        for copy in copies:
            copy.start()
        gate_row[...] = head_row(pack, pack_ref)
        segment_line, valid_line = token_line(segments, core), token_line(valid, core)
        segment_side, valid_side = to_side(segment_line), to_side(valid_line)
        allowed = (segment_side == segment_line) & ((valid_line == 1.0) | (valid_side == 0.0))
        mask_bias[...] = jnp.where(allowed, 0.0, masked_score)
        stats_out[...] = jnp.zeros(stats_out.shape, f32)
        total[...] = jnp.zeros(total.shape, f32)
        for copy in copies:
            copy.wait()

    part, stats = attend_pair(
        pack,
        0,
        x_nat[...],
        (wq_ref, wk_ref, wv_ref, wa_ref),
        pack_ref,
        mask_bias,
        gate_row,
        stats_out[...],
        (weights_out, query_out, key_out, value_out, context_out, gated_out),
    )
    stats_out[...] = stats
    total[...] += part


def attend_peer_kernel(
    pack,
    core_ref,
    x_nat,
    mask_bias,
    total_in,
    stats_in,
    wq_ref,
    wk_ref,
    wv_ref,
    wa_ref,
    pack_own,
    pack_peer,
    weights_out,
    query_out,
    key_out,
    value_out,
    context_out,
    gated_out,
    stats_out,
    biased_out,
    normed_out,
    hidden_out,
    total,
    gate_row,
):
    at = pl.program_id(0)
    core = core_ref[0]

    @pl.when(at == 0)
    def _():
        gate_row[...] = head_row(pack, pack_peer)
        stats_out[...] = stats_in[...]
        total[...] = total_in[...]

    part, stats = attend_pair(
        pack,
        pl.num_programs(0),
        x_nat[...],
        (wq_ref, wk_ref, wv_ref, wa_ref),
        pack_peer,
        mask_bias,
        gate_row,
        stats_out[...],
        (weights_out, query_out, key_out, value_out, context_out, gated_out),
    )
    stats_out[...] = stats
    total[...] += part

    @pl.when(at == pl.num_programs(0) - 1)
    def _():
        biased = total[...] + both(core, pack_own, pack_peer, pack.b_attn_out)
        biased_out[...] = biased
        gates = hidden_gates(core, pack, pack_own, pack_peer)
        mha_gate = scalar_gate(pack, pack_own, 0)
        resid = x_nat[...].astype(f32) + biased * (mha_gate * gates)
        normed, inv_scale = norm_forward(resid)
        normed_out[...] = normed
        gain = both(core, pack_own, pack_peer, pack.gain_one)
        shift = both(core, pack_own, pack_peer, pack.shift_one)
        hidden_out[...] = to_low((normed * gain + shift) * gates)
        lane = lax.broadcasted_iota(jnp.int32, (1, LANES), 1)
        stats_out[...] = jnp.where(lane == LANES - 1, inv_scale, stats)


def gelu_parts(pre_act):
    whole = 0.5 + 0.5 * lax.erf(pre_act * (0.5**0.5))
    return whole, jnp.exp(-0.5 * pre_act * pre_act) * (1.0 / math.sqrt(2.0 * math.pi))


def ffn_forward_kernel(
    pack,
    core_ref,
    hidden,
    normed,
    up_own,
    up_peer,
    down_own,
    down_peer,
    pack_own,
    pack_peer,
    teacher_own,
    teacher_peer,
    valid,
    mixed_own_out,
    mixed_peer_out,
    active_out,
    slope_out,
    output_own,
    output_peer,
    grad_resid_out,
    grad_ffn_out,
    sums_out,
    total,
    normed_in,
    target,
    sems,
):
    step = pl.program_id(0)
    core = core_ref[0]
    own_steps = pl.num_programs(0) // 2
    width = pack.width
    copies = (
        pltpu.make_async_copy(normed, normed_in, sems.at[2]),
        *rows_in(core, width, teacher_own, teacher_peer, target, sems),
    )

    def tile(at, up_ref, down_ref, pack_ref, mixed_ref):
        spot = pl.multiple_of(at * TILE, TILE)

        def cut(place):
            return pack_ref[:, pl.ds(place[0] + spot, TILE)]

        pre_act = contract(hidden[...], up_ref[...], 1, 0) + cut(pack.b_up)
        whole, density = gelu_parts(pre_act)
        active = pre_act * whole
        unit_gate = hard_concrete(cut(pack.unit_noise), cut(pack.unit_alpha))
        mixed = to_low(active * unit_gate)
        mixed_ref[...] = mixed
        active_out[...] = to_low(active)
        slope_out[...] = to_low((whole + pre_act * density) * unit_gate)
        return contract(mixed, down_ref[...], 1, 0)

    @pl.when(step == 0)
    def _():
        for copy in copies:
            copy.start()
        total[...] = tile(step, up_own, down_own, pack_own, mixed_own_out)

    @pl.when((step > 0) & (step < own_steps))
    def _():
        total[...] += tile(step, up_own, down_own, pack_own, mixed_own_out)

    @pl.when(step >= own_steps)
    def _():
        total[...] += tile(step - own_steps, up_peer, down_peer, pack_peer, mixed_peer_out)

    @pl.when(step == pl.num_programs(0) - 1)
    def _():
        gates = hidden_gates(core, pack, pack_own, pack_peer)
        ffn_gate = scalar_gate(pack, pack_own, 2)

        def vector(spot):
            return both(core, pack_own, pack_peer, spot)

        for copy in copies:
            copy.wait()
        biased = total[...] + vector(pack.b_down)
        hidden_one = (normed_in[...] * vector(pack.gain_one) + vector(pack.shift_one)) * gates
        normed_two, inv_two = norm_forward(hidden_one + biased * (ffn_gate * gates))
        gain = vector(pack.gain_two)
        final = (normed_two * gain + vector(pack.shift_two)) * gates
        final_low = to_low(final)

        def split(own_ref, peer_ref, values_in):
            @pl.when(core == 0)
            def _():
                own_ref[...] = values_in[:, :width]
                peer_ref[...] = values_in[:, width:]

            @pl.when(core == 1)
            def _():
                own_ref[...] = values_in[:, width:]
                peer_ref[...] = values_in[:, :width]

        split(output_own, output_peer, final_low)
        valid_side = to_side(token_line(valid, core))
        grad_final = (final - target[...].astype(f32)) * valid_side
        grad_resid = norm_back(grad_final * (gates * gain), normed_two, inv_two)
        grad_resid_out[...] = grad_resid
        grad_ffn_out[...] = to_low(grad_resid * (ffn_gate * gates))
        sums_out[0:1, :] = column_sum(grad_final * normed_two)
        sums_out[1:2, :] = column_sum(grad_final)
        sums_out[2:3, :] = column_sum(grad_resid * biased)
        sums_out[3:4, :] = column_sum(grad_resid)


def ffn_pre_kernel(
    pack,
    core_ref,
    grad_ffn,
    active,
    slope,
    down_own,
    down_peer,
    grad_pre_own,
    grad_pre_peer,
    unit_sums_out,
):
    step = pl.program_id(0)
    core = core_ref[0]
    own_steps = pl.num_programs(0) // 2
    units = pack.units

    def tile(at, side, down_ref, pre_ref):
        grad_mixed = contract(grad_ffn[...], down_ref[...], 1, 1)
        grad_pre = to_low(grad_mixed * slope[...].astype(f32))
        pre_ref[...] = grad_pre
        spot = pl.multiple_of(side * units + at * TILE, TILE)
        unit_sums_out[0:1, pl.ds(spot, TILE)] = column_sum(grad_mixed * active[...].astype(f32))
        unit_sums_out[1:2, pl.ds(spot, TILE)] = column_sum(grad_pre.astype(f32))

    @pl.when(step < own_steps)
    def _():
        tile(step, core, down_own, grad_pre_own)

    @pl.when(step >= own_steps)
    def _():
        tile(step - own_steps, 1 - core, down_peer, grad_pre_peer)


def ffn_backward_kernel(
    pack,
    core_ref,
    grad_pre_own,
    grad_pre_peer,
    grad_resid_two,
    normed,
    biased,
    stats,
    up_own,
    up_peer,
    pack_own,
    pack_peer,
    grad_resid_out,
    grad_attn_out,
    sums_out,
    total,
    resid_in,
    normed_in,
    biased_in,
    sems,
):
    step = pl.program_id(0)
    core = core_ref[0]
    own_steps = pl.num_programs(0) // 2
    copies = (
        pltpu.make_async_copy(grad_resid_two, resid_in, sems.at[0]),
        pltpu.make_async_copy(normed, normed_in, sems.at[1]),
        pltpu.make_async_copy(biased, biased_in, sems.at[2]),
    )

    @pl.when(step == 0)
    def _():
        for copy in copies:
            copy.start()
        total[...] = contract(grad_pre_own[...], up_own[...], 1, 1)

    @pl.when((step > 0) & (step < own_steps))
    def _():
        total[...] += contract(grad_pre_own[...], up_own[...], 1, 1)

    @pl.when(step >= own_steps)
    def _():
        total[...] += contract(grad_pre_peer[...], up_peer[...], 1, 1)

    @pl.when(step == pl.num_programs(0) - 1)
    def _():
        gates = hidden_gates(core, pack, pack_own, pack_peer)
        mha_gate = scalar_gate(pack, pack_own, 0)
        gain = both(core, pack_own, pack_peer, pack.gain_one)
        for copy in copies:
            copy.wait()
        grad_hidden = resid_in[...] + total[...]
        normed_one = normed_in[...]
        sums_out[0:1, :] = column_sum(grad_hidden * normed_one)
        sums_out[1:2, :] = column_sum(grad_hidden)
        inv_scale = stats[:, LANES - 1 : LANES]
        grad_resid = norm_back(grad_hidden * (gates * gain), normed_one, inv_scale)
        grad_resid_out[...] = grad_resid
        grad_attn_out[...] = to_low(grad_resid * (mha_gate * gates))
        sums_out[2:3, :] = column_sum(grad_resid * biased_in[...])
        sums_out[3:4, :] = column_sum(grad_resid)


def attend_back_kernel(
    pack,
    side_is_own,
    core_ref,
    weights,
    query_ref,
    key_ref,
    value_ref,
    context_ref,
    stats,
    grad_attn,
    wa_ref,
    pack_ref,
    out_ref,
    sums_out,
    gate_row,
):
    at = pl.program_id(0)
    core = core_ref[0]
    width = pack.width
    pair = at if side_is_own else at + pl.num_programs(0)

    @pl.when(at == 0)
    def _():
        gate_row[...] = head_row(pack, pack_ref)

    columns = pl.ds(pl.multiple_of(at * LANES, LANES), LANES)
    lane = lax.broadcasted_iota(jnp.int32, (1, LANES), 1)

    query, key, value = query_ref[...], key_ref[...], value_ref[...]
    context = context_ref[...].astype(f32)
    grad_context = contract(grad_attn[...], wa_ref[...], 1, 1)
    spot = pl.ds(pl.multiple_of(at * LANES, LANES), LANES)
    sums_out[0:1, spot] = column_sum(grad_context * context)
    inverses = [
        row_sum(jnp.where(lane == 2 * pair + side, stats[...], 0.0)) for side in range(2)
    ]
    grad_low = to_low(grad_context * gate_row[:, columns] * pick_half(inverses[0], inverses[1]))
    product = grad_low.astype(f32) * context
    found = []
    for side in range(2):
        mask = half_mask(side, f32)
        level = row_sum(product * mask)
        grad_probs = contract(grad_low * mask.astype(bf16), value, 1, 1)
        chosen = weights[side]
        grad_raw = to_low(chosen.astype(f32) * (grad_probs - level))
        found.append(
            (
                contract(grad_raw, key, 1, 0),
                contract(grad_raw, query, 0, 0),
                contract(chosen, grad_low, 0, 0),
            )
        )
    grad_query = to_low(pick_half(found[0][0], found[1][0]) * HD ** (-0.5))
    grad_key = to_low(pick_half(found[0][1], found[1][1]))
    grad_value = to_low(pick_half(found[0][2], found[1][2]))
    for place, grad in enumerate((grad_query, grad_key, grad_value)):
        at_lane = pl.multiple_of(place * width + at * LANES, LANES)
        out_ref[:, pl.ds(at_lane, LANES)] = grad
    sums_out[1:2, spot] = column_sum(grad_query.astype(f32))
    sums_out[2:3, spot] = column_sum(grad_value.astype(f32))


def down_grad_kernel(bit_ref, mixed, mixed_near, grad, grad_near, sent_out, kept_out):
    summed = to_low(
        contract(mixed[...], grad[...], 0, 0) + contract(mixed_near[...], grad_near[...], 0, 0)
    )
    first = pl.program_id(0) < pl.num_programs(0) // 2

    @pl.when(first)
    def _():
        sent_out[...] = summed

    @pl.when(jnp.logical_not(first))
    def _():
        kept_out[...] = summed


def attn_out_grad_kernel(bit_ref, gated, gated_near, grad, grad_near, sent_out, kept_out):
    width = gated.shape[1]
    part = width // 4
    summed = to_low(
        contract(gated[...], grad[...], 0, 0) + contract(gated_near[...], grad_near[...], 0, 0)
    )

    def put(ref):
        for at in range(4):
            ref[:, at * width : (at + 1) * width] = summed[at * part : (at + 1) * part]

    @pl.when(pl.program_id(0) == 0)
    def _():
        put(sent_out)

    @pl.when(pl.program_id(0) == 1)
    def _():
        put(kept_out)


def attend_grad_kernel(
    half_ref,
    core_ref,
    x_own,
    x_peer,
    grad,
    grad_near,
    out_ref,
    source,
    sem,
):
    core = core_ref[0]

    @pl.when(half_ref[0] == core)
    def _():
        copy = pltpu.make_async_copy(x_own, source, sem)
        copy.start()
        copy.wait()

    @pl.when(half_ref[0] != core)
    def _():
        copy = pltpu.make_async_copy(x_peer, source, sem)
        copy.start()
        copy.wait()

    summed = contract(own_rows(source, core), grad[...], 0, 0) + contract(
        own_rows(source, 1 - core), grad_near[...], 0, 0
    )
    out_ref[...] = to_low(summed)


def input_grad_kernel(
    width,
    core_ref,
    grad_resid,
    grad_own,
    grad_peer,
    wq_own,
    wk_own,
    wv_own,
    wq_peer,
    wk_peer,
    wv_peer,
    own_out,
    peer_out,
):
    core = core_ref[0]
    summed = grad_resid[...]
    for grad, weights in (
        (grad_own, (wq_own, wk_own, wv_own)),
        (grad_peer, (wq_peer, wk_peer, wv_peer)),
    ):
        for place, weight in enumerate(weights):
            summed = summed + contract(
                grad[:, place * width : (place + 1) * width], weight[...], 1, 1
            )

    @pl.when(core == 0)
    def _():
        own_out[...] = summed[:, :width]
        peer_out[...] = summed[:, width:]

    @pl.when(core == 1)
    def _():
        own_out[...] = summed[:, width:]
        peer_out[...] = summed[:, :width]


def place_kernel(bit_ref, half, other, out_ref):
    step = pl.program_id(0)

    @pl.when(step < 2)
    def _():
        out_ref[...] = half[...].astype(f32)

    @pl.when(step >= 2)
    def _():
        out_ref[...] = other[...].astype(f32)


def place_up_kernel(bit_ref, half, other, up_out, attn_out):
    width = attn_out.shape[1]
    rows = up_out.shape[0]
    part = width // 4

    def put(ref):
        up_out[...] = ref[:rows, :].astype(f32)
        for at in range(4):
            attn_out[at * part : (at + 1) * part, :] = ref[
                rows:, at * width : (at + 1) * width
            ].astype(f32)

    @pl.when(pl.program_id(0) == 0)
    def _():
        put(half)

    @pl.when(pl.program_id(0) == 1)
    def _():
        put(other)


def place_attend_kernel(bit_ref, half, other, query_out, key_out, value_out):
    width = query_out.shape[1]

    def put(ref):
        for at, out in enumerate((query_out, key_out, value_out)):
            out[...] = ref[:, at * width : (at + 1) * width].astype(f32)

    @pl.when(pl.program_id(0) == 0)
    def _():
        put(half)

    @pl.when(pl.program_id(0) == 1)
    def _():
        put(other)


def finish_kernel(
    pack,
    core_ref,
    sums,
    pack_own,
    pack_peer,
    b_query,
    b_value,
    b_attn_out,
    gain_one,
    shift_one,
    b_up,
    b_down,
    gain_two,
    shift_two,
    head_gate,
    mha_gate,
    unit_gate,
    ffn_gate,
    hidden_gate,
    head_alpha,
    mha_alpha,
    unit_alpha,
    ffn_alpha,
    hidden_alpha,
    share_out,
    penalty_out,
):
    core = core_ref[0]
    width, units = pack.width, pack.units
    columns = pl.ds(pl.multiple_of(core * width, LANES), width)
    heads = width // HD

    def put(out_ref, line):
        out_ref[...] = line.reshape(out_ref.shape)

    def own(row):
        return sums[row : row + 1, columns]

    def vector(spot):
        return take(pack_own, spot)

    gates = hard_concrete(vector(pack.hidden_noise), vector(pack.hidden_alpha))
    mha, ffn = scalar_gate(pack, pack_own, 0), scalar_gate(pack, pack_own, 2)
    put(gain_two, gates * own(0))
    put(shift_two, gates * own(1))
    put(b_down, (ffn * gates) * own(3))
    put(gain_one, gates * own(4))
    put(shift_one, gates * own(5))
    put(b_attn_out, (mha * gates) * own(7))
    put(b_query, own(9))
    put(b_value, own(10))
    grad_hidden = (
        vector(pack.gain_two) * own(0)
        + vector(pack.shift_two) * own(1)
        + ffn * own(2)
        + vector(pack.gain_one) * own(4)
        + vector(pack.shift_one) * own(5)
        + mha * own(6)
    )
    put(hidden_gate, grad_hidden)
    all_gates = hidden_gates(core, pack, pack_own, pack_peer)
    grad_ffn_gate = row_sum(all_gates * sums[2:3, :])
    grad_mha_gate = row_sum(all_gates * sums[6:7, :])
    put(ffn_gate, grad_ffn_gate)
    put(mha_gate, grad_mha_gate)

    unit_rows = units // (2 * width)

    def unit_line(first):
        at = first + core * unit_rows
        return jnp.concatenate([sums[pl.ds(at + k, 1), :] for k in range(unit_rows)], axis=1)

    grad_unit = unit_line(11)
    put(b_up, unit_line(11 + 2 * unit_rows))
    put(unit_gate, grad_unit)
    by_head = own(8)
    lane = lax.broadcasted_iota(jnp.int32, (1, LANES), 1)
    grad_head = jnp.zeros((1, LANES), f32)
    for at in range(heads):
        grad_head = jnp.where(
            lane == at, row_sum(by_head[:, at * HD : (at + 1) * HD]), grad_head
        )
    put(head_gate, grad_head[:, :heads])

    numbers = vector(pack.scalars)
    mha_open, ffn_open = open_share(numbers[:, 0:1]), open_share(numbers[:, 2:3])
    first_weight, second_weight = numbers[:, 4:5], numbers[:, 5:6]

    def open_total(spot, count):
        return row_sum(open_share(take(pack_own, spot)[:, :count])) + row_sum(
            open_share(take(pack_peer, spot)[:, :count])
        )

    head_sum = open_total(pack.head_alpha, heads)
    unit_sum = open_total(pack.unit_alpha, units)
    hidden_sum = open_total(pack.hidden_alpha, width)
    model, inner = 2.0 * width, 2.0 * units
    scale = 1.0 / ((4.0 * model + 2.0 * inner) * model)
    kept = 4.0 * HD * mha_open * head_sum + 2.0 * ffn_open * unit_sum
    share = kept * hidden_sum * scale
    gap = share - target_share
    put(share_out, share)
    put(penalty_out, first_weight * gap + second_weight * gap * gap)
    slope = (first_weight + 2.0 * second_weight * gap) * scale
    by_heads = slope * hidden_sum * (4.0 * HD)
    by_units = slope * hidden_sum * 2.0

    def alpha_grad(noise, alpha, grad_gate, grad_open):
        opened = open_share(alpha)
        return gate_slope(noise, alpha) * grad_gate + grad_open * (opened * (1.0 - opened))

    put(
        head_alpha,
        alpha_grad(
            vector(pack.head_noise), vector(pack.head_alpha), grad_head, by_heads * mha_open
        )[:, :heads],
    )
    put(
        unit_alpha,
        alpha_grad(
            vector(pack.unit_noise), vector(pack.unit_alpha), grad_unit, by_units * ffn_open
        ),
    )
    put(
        hidden_alpha,
        alpha_grad(
            vector(pack.hidden_noise), vector(pack.hidden_alpha), grad_hidden, slope * kept
        ),
    )
    put(
        mha_alpha,
        alpha_grad(numbers[:, 1:2], numbers[:, 0:1], grad_mha_gate, by_heads * head_sum),
    )
    put(
        ffn_alpha,
        alpha_grad(numbers[:, 3:4], numbers[:, 2:3], grad_ffn_gate, by_units * unit_sum),
    )


def full(shape):
    return pl.BlockSpec(shape, lambda *at: (0,) * len(shape), pipeline_mode=pl.Buffered(1))


def anywhere():
    return pl.BlockSpec(memory_space=pl.ANY)


def every(shape, dim):
    return pl.BlockSpec(shape, lambda i: tuple(i if d == dim else 0 for d in range(2)))


def sides(steps):
    def early(shape, dim):
        return pl.BlockSpec(
            shape, lambda i: tuple(jnp.minimum(i, steps - 1) if d == dim else 0 for d in range(2))
        )

    def late(shape, dim):
        return pl.BlockSpec(
            shape, lambda i: tuple(jnp.maximum(i - steps, 0) if d == dim else 0 for d in range(2))
        )

    return early, late


def one_number():
    return pl.BlockSpec(memory_space=pltpu.SMEM)


def shaped(shape, dtype):
    return jax.ShapeDtypeStruct(shape, dtype)


def far(struct):
    return pltpu.HBM(struct.shape, struct.dtype)


ORDER = (
    *("K3a", "KD", "K3b", "KU", "hD", "K4a", "Kao", "qD", "hU", "K4b", "KAs", "sD", "qU"),
    *("KAk", "S0", "hA", "sD", "sU", "S", "K6", "qA", "sD", "S", "wD", "sU", "O"),
    *("sA", "S", "pD", "sU", "sA", "wU", "sA", "wA", "S", "F", "pU", "pA"),
)
ON_PATH = ("D", "U", "A")


class Order:
    def __init__(self):
        self.last = ()
        self.share = 1.0

    def tie(self, values_in):
        if not self.last:
            return values_in
        return lax.optimization_barrier((values_in, *self.last))[0]

    def mark(self, *values_in):
        self.last = values_in


def call(order, kernel, grid, in_specs, out_specs, out_shape, scratch, cost, args, mib=28):
    out = pl.pallas_call(
        kernel,
        grid=grid,
        in_specs=in_specs,
        out_specs=out_specs,
        out_shape=out_shape,
        scratch_shapes=scratch,
        compiler_params=pltpu.CompilerParams(vmem_limit_bytes=mib * 2**20),
        cost_estimate=pl.CostEstimate(
            flops=int(cost[0] * 1e9 * order.share),
            bytes_accessed=int(cost[1] * 1e6 * order.share),
            transcendentals=0,
        ),
    )(order.tie(args[0]), *args[1:])
    order.mark(jax.tree.leaves(out)[-1])
    return out


def call_by_half(order, kernel, grid, in_specs, out_specs, out_shape, cost, half, args, mib=28):
    out = pl.pallas_call(
        kernel,
        grid_spec=pltpu.PrefetchScalarGridSpec(
            num_scalar_prefetch=1, grid=grid, in_specs=in_specs, out_specs=out_specs
        ),
        out_shape=out_shape,
        compiler_params=pltpu.CompilerParams(vmem_limit_bytes=mib * 2**20),
        cost_estimate=pl.CostEstimate(
            flops=int(cost[0] * 1e9 * order.share),
            bytes_accessed=int(cost[1] * 1e6 * order.share),
            transcendentals=0,
        ),
    )(order.tie(half), *args)
    order.mark(jax.tree.leaves(out)[-1])
    return out


def swap_pairs(core_masks):
    rows, cores = lax.axis_size("rows"), lax.axis_size("hid")
    return [
        (row * cores + core, (row ^ core_masks[core]) * cores + core)
        for row in range(rows)
        for core in range(cores)
    ]


def swap(values_in, core_masks):
    return lax.ppermute(values_in, ("rows", "hid"), swap_pairs(core_masks))


def along(values_in, steps):
    rows, cores = lax.axis_size("rows"), lax.axis_size("hid")
    pairs = [
        (row * cores + core, (row + 4 * (steps[row // 4 % 4] - row // 4 % 4)) * cores + core)
        for row in range(rows)
        if row // 4 % 4 in steps
        for core in range(cores)
    ]
    return lax.ppermute(values_in, ("rows", "hid"), pairs)


def in_hbm(values_in):
    return pltpu.with_memory_space_constraint(values_in, pltpu.HBM)


def near(values_in):
    return lax.ppermute(values_in, "hid", [(0, 1), (1, 0)])


def spread_masks():
    rest = lax.axis_size("rows") // 4
    masks = [4 * (2**k * 2 - 1) for k in range(rest.bit_length() - 1)]
    return [(masks[k], masks[len(masks) - 1 - k]) for k in range(len(masks))]


def add_low(first, second):
    return to_low(first.astype(f32) + second.astype(f32))


def pick(values_in, at):
    return lax.dynamic_index_in_dim(values_in, at, 0, keepdims=False)


class RowSum:
    def __init__(self, order, sent_half, first_bit, second_bit):
        self.order = order
        self.first_bit, self.second_bit = first_bit, second_bit
        self.near = swap(sent_half, (1, 2))

    def halve(self, kept):
        at = self.second_bit
        kept = self.order.tie(kept)
        to_send = add_low(pick(kept, 1 - at), pick(self.near, 1 - at))
        self.own = add_low(pick(kept, at), pick(self.near, at))
        self.near = swap(to_send, (2, 1))
        self.order.mark(to_send, self.own)

    def halve_with(self, kept, below, below_near):
        kept = add_low(self.order.tie(kept), self.near)
        below = add_low(self.order.tie(below), below_near)
        rows = (kept.shape[0] + below.shape[0]) // 2
        first, second = kept[:rows], jnp.concatenate((kept[rows:], below), axis=0)
        to_send = jnp.where(self.second_bit == 0, second, first)
        self.own = jnp.where(self.second_bit == 0, first, second)
        self.near = swap(to_send, (2, 1))
        self.order.mark(to_send, self.own)

    def quarter(self, path=False):
        self.own = add_low(self.order.tie(self.own), self.near)
        masks = spread_masks()
        self.left = [partial(swap, core_masks=pair) for pair in masks]
        self.inner = None
        if path:
            steps = [{0: 1, 3: 2}, {1: 2, 2: 1}, {1: 0, 2: 3}]
            self.left = [partial(along, steps=item) for item in steps] + self.left[2:]
            at = lax.rem(lax.axis_index("rows") // 4, 4)
            self.inner = (at == 1) | (at == 2)
            self.until_out = 3
        self.near = self.left.pop(0)(self.own)
        self.order.mark(self.own)

    def spread(self):
        own = self.order.tie(self.own)
        if self.inner is not None:
            self.until_out -= 1
        if self.inner is not None and self.until_out == 0:
            self.own = jnp.where(self.inner, own, self.near)
        else:
            self.own = add_low(own, self.near)
        self.near = self.left.pop(0)(self.own) if self.left else swap(self.own, (2, 1))
        self.order.mark(self.own)

    def spread_all(self):
        while self.left:
            self.spread()
        self.spread()

    def widen(self):
        own, near = self.order.tie(self.own), self.near
        self.half = jnp.where(
            self.second_bit == 0, jnp.stack((own, near)), jnp.stack((near, own))
        )
        self.order.mark(self.half)
        self.near = swap(self.half, (1, 2))

    def parts(self):
        return self.half, self.near


class SmallSum:
    def __init__(self, order, values_in):
        self.order, self.own = order, values_in
        self.left = [(1, 2), (2, 1)] + spread_masks()
        self.near = near(values_in)

    def step(self):
        self.own = self.order.tie(self.own) + self.near
        self.order.mark(self.own)
        if self.left:
            self.near = swap(self.own, self.left.pop(0))
            return True
        return False

    def rest(self):
        while self.step():
            pass
        return self.own


def body(
    hidden_in,
    teacher,
    segment_ids,
    valid_mask,
    w_query,
    b_query,
    w_key,
    w_value,
    b_value,
    w_attn_out,
    b_attn_out,
    gain_one,
    shift_one,
    w_up,
    b_up,
    w_down,
    b_down,
    gain_two,
    shift_two,
    head_alpha,
    mha_alpha,
    unit_alpha,
    ffn_alpha,
    hidden_alpha,
    head_noise,
    mha_noise,
    unit_noise,
    ffn_noise,
    hidden_noise,
    lagrange,
):
    model, width = w_query.shape
    units = w_up.shape[1]
    heads = width // HD
    pairs = model // LANES
    tokens = hidden_in.shape[0] // 2
    pack = Pack(width, units)
    order = Order()
    core = lax.axis_index("hid")
    row = lax.axis_index("rows")
    core_at = jnp.reshape(core, (1,)).astype(jnp.int32)
    low_bit, high_bit = row & 1, (row >> 1) & 1
    first_bit = jnp.where(core == 0, low_bit, high_bit).astype(jnp.int32)
    second_bit = jnp.where(core == 0, high_bit, low_bit).astype(jnp.int32)

    packed = (
        (b_query, pack.b_query, 0),
        (b_value, pack.b_value, 0),
        (b_attn_out, pack.b_attn_out, 0),
        (gain_one, pack.gain_one, 0),
        (shift_one, pack.shift_one, 0),
        (b_down, pack.b_down, 0),
        (gain_two, pack.gain_two, 0),
        (shift_two, pack.shift_two, 0),
        (hidden_alpha, pack.hidden_alpha, 0),
        (hidden_noise, pack.hidden_noise, 0),
        (b_up, pack.b_up, 0),
        (unit_alpha, pack.unit_alpha, 0),
        (unit_noise, pack.unit_noise, 0),
        (head_alpha, pack.head_alpha, 0),
        (head_noise, pack.head_noise, 0),
        (mha_alpha, pack.scalars, 0),
        (mha_noise, pack.scalars, 1),
        (ffn_alpha, pack.scalars, 2),
        (ffn_noise, pack.scalars, 3),
        (lagrange, pack.scalars, 4),
    )
    pack_own = call(
        order,
        partial(pack_kernel, pack, [item[1:] for item in packed]),
        (),
        [full(item[0].shape) if item[0].shape[0] > 1 else one_number() for item in packed],
        full((1, pack.total)),
        far(shaped((1, pack.total), f32)),
        [],
        (0.001, 0.1, 0),
        tuple(in_hbm(item[0]) if item[0].shape[0] > 1 else item[0] for item in packed),
        mib=4,
    )
    x_peer = near(hidden_in)
    pack_peer = near(pack_own)
    wq_peer, wk_peer, wv_peer = near(w_query), near(w_key), near(w_value)
    wa_peer = near(w_attn_out)
    x_peer, up_sent, down_sent, teacher_sent = lax.optimization_barrier(
        (x_peer, w_up, w_down, teacher)
    )
    up_peer, down_peer, teacher_peer = near(up_sent), near(down_sent), near(teacher_sent)
    hidden_in, teacher, w_query, w_key, w_value, w_attn_out, w_up, w_down = (
        in_hbm(item)
        for item in (hidden_in, teacher, w_query, w_key, w_value, w_attn_out, w_up, w_down)
    )
    wq_peer, wk_peer, wv_peer, wa_peer = (
        in_hbm(item) for item in (wq_peer, wk_peer, wv_peer, wa_peer)
    )
    pack_own, pack_peer = in_hbm(pack_own), in_hbm(pack_peer)
    segments = in_hbm(segment_ids.reshape(-1, LANES))
    valid = in_hbm(valid_mask.reshape(-1, LANES))
    packs = [full((1, pack.total))] * 2
    token_low = shaped((tokens, model), bf16)
    token_wide = shaped((tokens, model), f32)
    token_half = shaped((tokens, width), bf16)

    own_pairs = pairs // 2
    one_side = (own_pairs,)
    by_pair = every((tokens, LANES), 1)
    head_outs = [pl.BlockSpec((2, BLOCK, BLOCK), lambda i: (i, 0, 0))] + [by_pair] * 5
    head_shapes = [far(shaped((2 * own_pairs, BLOCK, BLOCK), bf16))] + [far(token_half)] * 5
    head_weights = [every((model, LANES), 1)] * 3 + [every((LANES, model), 0)]
    token_stats = far(shaped((tokens, LANES), f32))
    *heads_own, gated_own, stats, x_nat, mask_bias, attn_part = call(
        order,
        partial(attend_own_kernel, pack),
        one_side,
        [one_number()]
        + [anywhere()] * 2
        + head_weights
        + [full((1, pack.total))]
        + [full(segments.shape)] * 2,
        head_outs
        + [full((tokens, LANES)), full((tokens, model))]
        + [full((BLOCK, BLOCK)), full((tokens, model))],
        head_shapes + [token_stats, token_low, shaped((BLOCK, BLOCK), f32), token_wide],
        [pltpu.VMEM((1, width), f32), pltpu.SemaphoreType.DMA((2,))],
        (40, 200, 3),
        (
            core_at,
            hidden_in,
            x_peer,
            w_query,
            w_key,
            w_value,
            w_attn_out,
            pack_own,
            segments,
            valid,
        ),
    )
    *heads_peer, gated_peer, stats, biased, normed, hidden = call(
        order,
        partial(attend_peer_kernel, pack),
        one_side,
        [one_number(), full((tokens, model)), full((BLOCK, BLOCK)), full((tokens, model))]
        + [full((tokens, LANES))]
        + head_weights
        + packs,
        head_outs + [full((tokens, LANES))] + [full((tokens, model))] * 3,
        head_shapes + [token_stats, far(token_wide), far(token_wide), token_low],
        [pltpu.VMEM((tokens, model), f32), pltpu.VMEM((1, width), f32)],
        (40, 200, 3),
        (
            core_at,
            x_nat,
            mask_bias,
            attn_part,
            in_hbm(stats),
            wq_peer,
            wk_peer,
            wv_peer,
            wa_peer,
            pack_own,
            pack_peer,
        ),
    )
    normed, biased, stats = in_hbm(normed), in_hbm(biased), in_hbm(stats)
    hidden_near = near(hidden)
    gated_near = near(gated_peer)

    tiles = units // TILE
    early, late = sides(tiles)

    (
        mixed_own,
        mixed_peer,
        active,
        slope,
        output_own,
        output_peer,
        grad_resid_two,
        grad_ffn,
        sums_two,
    ) = call(
        order,
        partial(ffn_forward_kernel, pack),
        (2 * tiles,),
        [one_number(), full((tokens, model)), anywhere()]
        + [early((model, TILE), 1), late((model, TILE), 1)]
        + [early((TILE, model), 0), late((TILE, model), 0)]
        + packs
        + [anywhere()] * 2
        + [full(valid.shape)],
        [early((tokens, TILE), 1), late((tokens, TILE), 1)]
        + [every((tokens, TILE), 1)] * 2
        + [full((tokens, width))] * 2
        + [full((tokens, model))] * 2
        + [full((4, model))],
        [
            shaped((tokens, units), bf16),
            shaped((tokens, units), bf16),
            shaped((tokens, 2 * units), bf16),
            shaped((tokens, 2 * units), bf16),
            far(token_half),
            far(token_half),
            far(token_wide),
            token_low,
            shaped((4, model), f32),
        ],
        [
            pltpu.VMEM((tokens, model), f32),
            pltpu.VMEM((tokens, model), f32),
            pltpu.VMEM((tokens, model), bf16),
            pltpu.SemaphoreType.DMA((3,)),
        ],
        (5.0, 25, 3),
        (
            core_at,
            hidden,
            normed,
            w_up,
            up_peer,
            w_down,
            down_peer,
            pack_own,
            pack_peer,
            teacher,
            teacher_peer,
            valid,
        ),
    )
    grad_resid_two = in_hbm(grad_resid_two)
    mixed_near = near(mixed_peer)
    grad_ffn_near = near(grad_ffn)
    output_near = near(output_peer)
    up_rows = width + width // 4
    half_units = units // 2
    step_units = half_units // 2

    bit_at = jnp.reshape(first_bit, (1,))

    def at_half(i, steps, bit):
        return jnp.where(i < steps, 1 - bit[0], bit[0])

    def sent_then_kept(shape, steps, dim):
        return [
            pl.BlockSpec(
                shape,
                lambda i, t, at=at: tuple(at(i) if d == dim else 0 for d in range(2)),
            )
            for at in (
                lambda i: jnp.minimum(i, steps - 1),
                lambda i: jnp.maximum(i - steps, 0),
            )
        ]

    def attend_back(side_is_own, wa_ref):
        arrays = heads_own if side_is_own else heads_peer
        return call(
            order,
            partial(attend_back_kernel, pack, side_is_own),
            one_side,
            [one_number(), pl.BlockSpec((2, BLOCK, BLOCK), lambda i: (i, 0, 0))]
            + [by_pair] * 4
            + [full((tokens, LANES)), full((tokens, model))]
            + [every((LANES, model), 0)]
            + [full((1, pack.total))],
            [full((tokens, 3 * width)), full((3, width))],
            [shaped((tokens, 3 * width), bf16), shaped((3, width), f32)],
            [pltpu.VMEM((1, width), f32)],
            (2.0, 10, 0),
            (
                core_at,
                *(in_hbm(item) for item in arrays),
                stats,
                grad_attn,
                wa_ref,
                pack_own if side_is_own else pack_peer,
            ),
            mib=18,
        )

    def attend_half(half):
        out = call(
            order,
            attend_grad_kernel,
            (),
            [one_number()] * 2 + [anywhere()] * 2 + [full((tokens, 3 * width))] * 2,
            full((width, 3 * width)),
            shaped((width, 3 * width), bf16),
            [pltpu.VMEM(hidden_in.shape, bf16), pltpu.SemaphoreType.DMA],
            (24, 100, 0),
            (jnp.reshape(half, (1,)), core_at, hidden_in, x_peer, grad_own, grad_near),
            mib=12,
        )
        return out.reshape(2, width // 2, 3 * width)

    def place(pieces):
        _, height, across = pieces[0].shape

        def block(at):
            return pl.BlockSpec((1, height, across), at)

        out = call_by_half(
            order,
            place_kernel,
            (4,),
            [
                block(lambda i, t: (jnp.minimum(i, 1), 0, 0)),
                block(lambda i, t: (jnp.maximum(i - 2, 0), 0, 0)),
            ],
            block(lambda i, t: (2 * lax.rem(t[0] + i // 2, 2) + lax.rem(i, 2), 0, 0)),
            shaped((4, height, across), f32),
            (0.001, 7),
            bit_at,
            pieces,
            mib=18,
        )
        return out.reshape(4 * height, across)

    def by_token(own, other):
        own = order.tie(own)
        out = jnp.where(
            core == 0, jnp.concatenate((own, other), axis=0), jnp.concatenate((other, own), axis=0)
        )
        order.mark(out)
        return out

    def by_half(pieces):
        return tuple(piece.reshape(-1, piece.shape[-1]) for piece in pieces)

    def own_half(shape, dim):
        return pl.BlockSpec(
            shape, lambda i, t: tuple(lax.rem(t[0] + i, 2) if d == dim else 0 for d in range(2))
        )

    grad_pre_own = grad_pre_peer = unit_sums = grad_pre_near = down_kept = down_chunk = None
    grad_resid_one = grad_attn = sums_one = grad_attn_near = up_kept = up_chunk = None
    grad_peer = sums_peer = grad_near = attn_kept = attn_near = grad_own = None
    sums_own = attend_chunk = attend_kept = small = input_own = input_peer = None
    input_near = output = grad_input = sum_down = finished = sum_up = None
    sum_attn = sum_query = sum_key = sum_value = None

    def units_back():
        nonlocal grad_pre_own, grad_pre_peer, unit_sums, grad_pre_near
        grad_pre_own, grad_pre_peer, unit_sums = call(
            order,
            partial(ffn_pre_kernel, pack),
            (2 * tiles,),
            [one_number(), full((tokens, model))]
            + [every((tokens, TILE), 1)] * 2
            + [early((TILE, model), 0), late((TILE, model), 0)],
            [early((tokens, TILE), 1), late((tokens, TILE), 1), full((2, 2 * units))],
            [
                shaped((tokens, units), bf16),
                shaped((tokens, units), bf16),
                shaped((2, 2 * units), f32),
            ],
            [],
            (50, 300, 0),
            (core_at, grad_ffn, active, slope, w_down, down_peer),
            mib=18,
        )
        grad_pre_near = near(grad_pre_peer)

    def down_grads():
        nonlocal down_kept, down_chunk
        by_units = pl.BlockSpec(
            (tokens, step_units), lambda i, t: (0, at_half(i, 2, t) * 2 + lax.rem(i, 2))
        )
        down_sent, down_kept = call_by_half(
            order,
            down_grad_kernel,
            (4,),
            [by_units, by_units] + [full((tokens, model))] * 2,
            sent_then_kept((step_units, model), 2, 0),
            [shaped((half_units, model), bf16)] * 2,
            (48, 180),
            bit_at,
            (mixed_own, mixed_near, grad_ffn, grad_ffn_near),
            mib=12,
        )
        down_sent, down_kept = (
            item.reshape(2, half_units // 2, model) for item in (down_sent, down_kept)
        )
        down_chunk = RowSum(order, down_sent, first_bit, second_bit)

    def ffn_back():
        nonlocal grad_resid_one, grad_attn, sums_one, grad_attn_near
        grad_resid_one, grad_attn, sums_one = call(
            order,
            partial(ffn_backward_kernel, pack),
            (2 * tiles,),
            [one_number()]
            + [early((tokens, TILE), 1), late((tokens, TILE), 1)]
            + [anywhere()] * 3
            + [full((tokens, LANES))]
            + [early((model, TILE), 1), late((model, TILE), 1)]
            + packs,
            [full((tokens, model))] * 2 + [full((4, model))],
            [far(token_wide), token_low, shaped((4, model), f32)],
            [pltpu.VMEM((tokens, model), f32)] * 4 + [pltpu.SemaphoreType.DMA((3,))],
            (2.5, 15, 0),
            (
                core_at,
                grad_pre_own,
                grad_pre_peer,
                grad_resid_two,
                normed,
                biased,
                stats,
                w_up,
                up_peer,
                pack_own,
                pack_peer,
            ),
            mib=20,
        )
        grad_attn_near = near(grad_attn)

    def up_grads():
        nonlocal up_kept, up_chunk
        by_features = pl.BlockSpec((tokens, width), lambda i, t: (0, at_half(i, 2, t)))
        by_units = pl.BlockSpec((tokens, half_units), lambda i, t: (0, lax.rem(i, 2)))
        up_sent, up_kept = call_by_half(
            order,
            down_grad_kernel,
            (4,),
            [by_features, by_features, by_units, by_units],
            sent_then_kept((width, half_units), 2, 1),
            [shaped((width, units), bf16)] * 2,
            (2.4, 12),
            bit_at,
            (hidden, hidden_near, grad_pre_own, grad_pre_near),
            mib=18,
        )
        up_chunk = RowSum(order, up_sent, first_bit, second_bit)

    def peer_heads():
        nonlocal grad_peer, sums_peer, grad_near
        grad_peer, sums_peer = attend_back(False, wa_peer)
        grad_near = near(grad_peer)

    def own_heads():
        nonlocal grad_own, sums_own
        grad_own, sums_own = attend_back(True, w_attn_out)

    def out_grads():
        nonlocal attn_kept, attn_near
        by_columns = pl.BlockSpec((tokens, width), lambda i, t: (0, at_half(i, 1, t)))
        attn_sent, attn_kept = call_by_half(
            order,
            attn_out_grad_kernel,
            (2,),
            [full((tokens, width))] * 2 + [by_columns] * 2,
            [full((width // 4, units))] * 2,
            [shaped((width // 4, units), bf16)] * 2,
            (0.6, 3),
            bit_at,
            (gated_own, gated_near, grad_attn, grad_attn_near),
            mib=8,
        )
        attn_near = swap(attn_sent, (1, 2))

    def send_attend():
        nonlocal attend_chunk
        attend_sent = attend_half(1 - first_bit)
        attend_chunk = RowSum(order, attend_sent, first_bit, second_bit)

    def keep_attend():
        nonlocal attend_kept
        attend_kept = attend_half(first_bit)

    def start_small():
        nonlocal small
        sums_late = order.tie(sums_own)
        sums_attn = jnp.where(
            core == 0,
            jnp.concatenate((sums_late, sums_peer), axis=1),
            jnp.concatenate((sums_peer, sums_late), axis=1),
        )
        small = SmallSum(
            order,
            jnp.concatenate((sums_two, sums_one, sums_attn, unit_sums.reshape(-1, model)), axis=0),
        )

    def inputs_back():
        nonlocal input_own, input_peer, input_near
        input_own, input_peer = call(
            order,
            partial(input_grad_kernel, width),
            (),
            [one_number(), full((tokens, model))]
            + [full((tokens, 3 * width))] * 2
            + [full((model, width))] * 6,
            [full((tokens, width))] * 2,
            [shaped((tokens, width), f32)] * 2,
            [],
            (1.8, 8, 0),
            (
                core_at,
                in_hbm(grad_resid_one),
                grad_own,
                grad_peer,
                w_query,
                w_key,
                w_value,
                wq_peer,
                wk_peer,
                wv_peer,
            ),
            mib=16,
        )
        input_near = near(input_peer)

    def put_output():
        nonlocal output, grad_input
        output = by_token(output_own, output_near)
        grad_input = by_token(input_own, input_near)

    def finish_small():
        nonlocal finished
        small_sums = small.rest()
        sizes = (width,) * 5 + (units,) + (width,) * 3 + (heads, 1, units, 1, width)
        sizes = sizes + (heads, 1, units, 1, width, 1, 1)
        finished = call(
            order,
            partial(finish_kernel, pack),
            (),
            [one_number(), full(small_sums.shape)] + packs,
            [full((size,)) for size in sizes],
            [shaped((size,), f32) for size in sizes],
            [],
            (0.01, 0.3, 0.1),
            (core_at, small_sums, pack_own, pack_peer),
        )

    def place_down():
        nonlocal sum_down
        sum_down = place(down_chunk.parts())

    def place_up():
        nonlocal sum_up, sum_attn
        sum_up, sum_attn = call_by_half(
            order,
            place_up_kernel,
            (2,),
            [full((up_rows, units))] * 2,
            [own_half((width, units), 0), own_half((width, width), 1)],
            [shaped((model, units), f32), shaped((width, model), f32)],
            (0.001, 10),
            bit_at,
            by_half(up_chunk.parts()),
            mib=18,
        )

    def place_attend():
        nonlocal sum_query, sum_key, sum_value
        sum_query, sum_key, sum_value = call_by_half(
            order,
            place_attend_kernel,
            (2,),
            [full((width, 3 * width))] * 2,
            [own_half((width, width), 0)] * 3,
            [shaped((model, width), f32)] * 3,
            (0.001, 7),
            bit_at,
            by_half(attend_chunk.parts()),
            mib=18,
        )

    steps = dict(
        K3a=units_back,
        KD=down_grads,
        K3b=ffn_back,
        KU=up_grads,
        K4a=peer_heads,
        K4b=own_heads,
        Kao=out_grads,
        KAs=send_attend,
        KAk=keep_attend,
        S0=start_small,
        S=lambda: small.step(),
        K6=inputs_back,
        O=put_output,
        F=finish_small,
        hD=lambda: down_chunk.halve(down_kept),
        qD=lambda: down_chunk.quarter("D" in ON_PATH),
        sD=lambda: down_chunk.spread(),
        wD=lambda: down_chunk.widen(),
        pD=place_down,
        hU=lambda: up_chunk.halve_with(up_kept, attn_kept, attn_near),
        qU=lambda: up_chunk.quarter("U" in ON_PATH),
        sU=lambda: up_chunk.spread(),
        wU=lambda: up_chunk.widen(),
        pU=place_up,
        hA=lambda: attend_chunk.halve(attend_kept),
        qA=lambda: attend_chunk.quarter("A" in ON_PATH),
        sA=lambda: attend_chunk.spread(),
        wA=lambda: attend_chunk.widen(),
        pA=place_attend,
    )
    for name in ORDER:
        steps[name]()
    return (
        output,
        grad_input,
        sum_query,
        finished[0],
        sum_key,
        sum_value,
        finished[1],
        sum_attn,
        finished[2],
        finished[3],
        finished[4],
        sum_up,
        finished[5],
        sum_down,
        *finished[6:],
    )


def solution(mesh):
    in_specs = (
        P("rows", "hid"),
        P("rows", "hid"),
        P("rows"),
        P("rows"),
        P(None, "hid"),
        P("hid"),
        P(None, "hid"),
        P(None, "hid"),
        P("hid"),
        P("hid", None),
        P("hid"),
        P("hid"),
        P("hid"),
        P(None, "hid"),
        P("hid"),
        P("hid", None),
        P("hid"),
        P("hid"),
        P("hid"),
        P("hid"),
        P(),
        P("hid"),
        P(),
        P("hid"),
        P("hid"),
        P(),
        P("hid"),
        P(),
        P("hid"),
        P(),
    )
    out_specs = (
        P("rows", "hid"),
        P("rows", "hid"),
        P(None, "hid"),
        P("hid"),
        P(None, "hid"),
        P(None, "hid"),
        P("hid"),
        P("hid", None),
        P("hid"),
        P("hid"),
        P("hid"),
        P(None, "hid"),
        P("hid"),
        P("hid", None),
        P("hid"),
        P("hid"),
        P("hid"),
        P("hid"),
        P(),
        P("hid"),
        P(),
        P("hid"),
        P("hid"),
        P(),
        P("hid"),
        P(),
        P("hid"),
        P(),
        P(),
    )
    return jax.shard_map(body, mesh=mesh, in_specs=in_specs, out_specs=out_specs, check_vma=False)
```

```python
from functools import partial
import math

import jax
import jax.numpy as jnp
from jax import lax
from jax.experimental import pallas as pl
from jax.experimental.pallas import tpu as pltpu
from jax.sharding import PartitionSpec as P

HD = 64
BLOCK = 512
LANES = 128
TILE = 768

norm_eps = 1e-05
gate_temper = 2.0 / 3.0
stretch_low = -0.1
stretch_high = 1.1
target_share = 0.4
masked_score = -1000000000.0
open_shift = gate_temper * math.log(-stretch_low / stretch_high)


f32 = jnp.float32
bf16 = jnp.bfloat16


def to_low(values_in):
    return values_in.astype(bf16)


def contract(first, second, first_dim, second_dim):
    return lax.dot_general(
        first, second, (((first_dim,), (second_dim,)), ((), ())), preferred_element_type=f32
    )


def column_sum(values_in):
    return jnp.sum(values_in, axis=0, keepdims=True)


def row_sum(values_in):
    return jnp.sum(values_in, axis=1, keepdims=True)


def sigmoid(values_in):
    return 1.0 / (1.0 + jnp.exp(-values_in))


def stretched(gate_noise, log_alpha):
    relaxed = sigmoid(
        (jnp.log(gate_noise) - jnp.log(1.0 - gate_noise) + log_alpha) / gate_temper
    )
    return relaxed, relaxed * (stretch_high - stretch_low) + stretch_low


def hard_concrete(gate_noise, log_alpha):
    return jnp.clip(stretched(gate_noise, log_alpha)[1], 0.0, 1.0)


def gate_slope(gate_noise, log_alpha):
    relaxed, wide = stretched(gate_noise, log_alpha)
    slope = relaxed * (1.0 - relaxed) * ((stretch_high - stretch_low) / gate_temper)
    return jnp.where((wide > 0.0) & (wide < 1.0), slope, 0.0)


def open_share(log_alpha):
    return sigmoid(log_alpha - open_shift)


class Pack:
    def __init__(self, width, units):
        self.width, self.units = width, units
        at = 0
        for name in ("b_query", "b_value", "b_attn_out", "gain_one", "shift_one"):
            setattr(self, name, (at, width))
            at += width
        for name in ("b_down", "gain_two", "shift_two", "hidden_alpha", "hidden_noise"):
            setattr(self, name, (at, width))
            at += width
        for name in ("b_up", "unit_alpha", "unit_noise"):
            setattr(self, name, (at, units))
            at += units
        for name in ("head_alpha", "head_noise", "scalars"):
            setattr(self, name, (at, LANES))
            at += LANES
        self.total = at


def pack_kernel(pack, counts, *refs):
    out_ref = refs[-1]
    out_ref[...] = jnp.full(out_ref.shape, 0.5, f32)
    for ref, (spot, lane) in zip(refs[:-1], counts):
        size = ref.shape[0]
        at = slice(spot[0] + lane, spot[0] + lane + size)
        if size > 1:
            out_ref[:, at] = ref[...].reshape(1, size)
        else:
            out_ref[:, at] = jnp.full((1, 1), ref[0], f32)


def take(pack_ref, spot):
    return pack_ref[:, spot[0] : spot[0] + spot[1]]


def natural(core, own, peer):
    at_peer = core.astype(f32)
    at_own = 1.0 - at_peer
    return jnp.concatenate((own * at_own + peer * at_peer, peer * at_own + own * at_peer), axis=1)


def both(core, own_ref, peer_ref, spot):
    return natural(core, take(own_ref, spot), take(peer_ref, spot))


def hidden_gates(core, pack, own_ref, peer_ref):
    return hard_concrete(
        both(core, own_ref, peer_ref, pack.hidden_noise),
        both(core, own_ref, peer_ref, pack.hidden_alpha),
    )


def head_row(pack, pack_ref):
    gates = hard_concrete(take(pack_ref, pack.head_noise), take(pack_ref, pack.head_alpha))
    parts = [jnp.broadcast_to(gates[:, at : at + 1], (1, HD)) for at in range(pack.width // HD)]
    return jnp.concatenate(parts, axis=1)


def scalar_gate(pack, own_ref, at):
    numbers = take(own_ref, pack.scalars)
    return hard_concrete(numbers[:, at + 1 : at + 2], numbers[:, at : at + 1])


def half_mask(side, dtype):
    lane = lax.broadcasted_iota(jnp.int32, (1, LANES), 1)
    inside = (lane < HD) if side == 0 else (lane >= HD)
    return jnp.where(inside, 1.0, 0.0).astype(dtype)


def pick_half(first, second):
    lane = lax.broadcasted_iota(jnp.int32, (1, LANES), 1)
    return jnp.where(lane < HD, first, second)


def norm_back(grad_normed, normed, inv_scale):
    width = normed.shape[1]
    mean_grad = row_sum(grad_normed) * (1.0 / width)
    mean_both = row_sum(grad_normed * normed) * (1.0 / width)
    return inv_scale * (grad_normed - mean_grad - normed * mean_both)


def norm_forward(resid):
    width = resid.shape[1]
    row_mean = row_sum(resid) * (1.0 / width)
    row_var = row_sum(resid * resid) * (1.0 / width) - row_mean * row_mean
    inv_scale = lax.rsqrt(row_var + norm_eps)
    return (resid - row_mean) * inv_scale, inv_scale


def own_rows(ref, core):
    return ref[pl.ds(pl.multiple_of(core * BLOCK, BLOCK), BLOCK), :]


def token_line(ref, core):
    lanes_of = BLOCK // LANES
    rows = [ref[pl.ds(core * lanes_of + at, 1), :] for at in range(lanes_of)]
    return jnp.concatenate(rows, axis=1).astype(f32)


def to_side(line):
    return jnp.broadcast_to(line, (LANES, BLOCK)).T[:, 0:1]


def rows_in(core, width, own_ref, peer_ref, out_ref, sems):
    rows = pl.ds(pl.multiple_of(core * BLOCK, BLOCK), BLOCK)
    own_at = pl.multiple_of(core * width, LANES)
    peer_at = pl.multiple_of((1 - core) * width, LANES)
    return (
        pltpu.make_async_copy(own_ref.at[rows, :], out_ref.at[:, pl.ds(own_at, width)], sems.at[0]),
        pltpu.make_async_copy(
            peer_ref.at[rows, :], out_ref.at[:, pl.ds(peer_at, width)], sems.at[1]
        ),
    )


def attend_pair(
    pack, first, source, weight_refs, pack_ref, mask_bias, gate_row, stats, out_refs
):
    at = pl.program_id(0)
    spot = pl.multiple_of(at * LANES, LANES)

    def cut(place):
        return pack_ref[:, pl.ds(place[0] + spot, LANES)]

    wq_ref, wk_ref, wv_ref, wa_ref = weight_refs
    weights_out, query_out, key_out, value_out, context_out, gated_out = out_refs
    weight_in = jnp.concatenate((wq_ref[...], wk_ref[...], wv_ref[...]), axis=1)
    projected = contract(source, weight_in, 1, 0)
    query = to_low(projected[:, :LANES] + cut(pack.b_query)) * jnp.asarray(HD ** (-0.5), bf16)
    key = to_low(projected[:, LANES : 2 * LANES])
    value = to_low(projected[:, 2 * LANES :] + cut(pack.b_value))
    query_out[...] = query
    key_out[...] = key
    value_out[...] = value
    value_wide = jnp.concatenate((value, jnp.ones((BLOCK, LANES), bf16)), axis=1)
    contexts = []
    lane = lax.broadcasted_iota(jnp.int32, (1, LANES), 1)
    for side in range(2):
        scores = contract(query * half_mask(side, bf16), key, 1, 1) + mask_bias[...]
        row_top = jnp.max(scores, axis=1, keepdims=True)
        weights = to_low(jnp.exp(scores - row_top))
        weights_out[side] = weights
        summed = contract(weights, value_wide, 1, 0)
        inverse = 1.0 / summed[:, LANES : 2 * LANES]
        contexts.append(summed[:, :LANES] * inverse)
        stats = jnp.where(lane == 2 * (first + at) + side, inverse, stats)
    context = pick_half(contexts[0], contexts[1])
    context_out[...] = to_low(context)
    gated = to_low(context * gate_row[:, pl.ds(spot, LANES)])
    gated_out[...] = gated
    return contract(gated, wa_ref[...], 1, 0), stats


def attend_own_kernel(
    pack,
    core_ref,
    x_own,
    x_peer,
    wq_ref,
    wk_ref,
    wv_ref,
    wa_ref,
    pack_ref,
    segments,
    valid,
    weights_out,
    query_out,
    key_out,
    value_out,
    context_out,
    gated_out,
    stats_out,
    x_nat,
    mask_bias,
    total,
    gate_row,
    sems,
):
    at = pl.program_id(0)
    core = core_ref[0]

    @pl.when(at == 0)
    def _():
        copies = rows_in(core, pack.width, x_own, x_peer, x_nat, sems)
        for copy in copies:
            copy.start()
        gate_row[...] = head_row(pack, pack_ref)
        segment_line, valid_line = token_line(segments, core), token_line(valid, core)
        segment_side, valid_side = to_side(segment_line), to_side(valid_line)
        allowed = (segment_side == segment_line) & ((valid_line == 1.0) | (valid_side == 0.0))
        mask_bias[...] = jnp.where(allowed, 0.0, masked_score)
        stats_out[...] = jnp.zeros(stats_out.shape, f32)
        total[...] = jnp.zeros(total.shape, f32)
        for copy in copies:
            copy.wait()

    part, stats = attend_pair(
        pack,
        0,
        x_nat[...],
        (wq_ref, wk_ref, wv_ref, wa_ref),
        pack_ref,
        mask_bias,
        gate_row,
        stats_out[...],
        (weights_out, query_out, key_out, value_out, context_out, gated_out),
    )
    stats_out[...] = stats
    total[...] += part


def attend_peer_kernel(
    pack,
    core_ref,
    x_nat,
    mask_bias,
    total_in,
    stats_in,
    wq_ref,
    wk_ref,
    wv_ref,
    wa_ref,
    pack_own,
    pack_peer,
    weights_out,
    query_out,
    key_out,
    value_out,
    context_out,
    gated_out,
    stats_out,
    biased_out,
    normed_out,
    hidden_out,
    total,
    gate_row,
):
    at = pl.program_id(0)
    core = core_ref[0]

    @pl.when(at == 0)
    def _():
        gate_row[...] = head_row(pack, pack_peer)
        stats_out[...] = stats_in[...]
        total[...] = total_in[...]

    part, stats = attend_pair(
        pack,
        pl.num_programs(0),
        x_nat[...],
        (wq_ref, wk_ref, wv_ref, wa_ref),
        pack_peer,
        mask_bias,
        gate_row,
        stats_out[...],
        (weights_out, query_out, key_out, value_out, context_out, gated_out),
    )
    stats_out[...] = stats
    total[...] += part

    @pl.when(at == pl.num_programs(0) - 1)
    def _():
        biased = total[...] + both(core, pack_own, pack_peer, pack.b_attn_out)
        biased_out[...] = biased
        gates = hidden_gates(core, pack, pack_own, pack_peer)
        mha_gate = scalar_gate(pack, pack_own, 0)
        resid = x_nat[...].astype(f32) + biased * (mha_gate * gates)
        normed, inv_scale = norm_forward(resid)
        normed_out[...] = normed
        gain = both(core, pack_own, pack_peer, pack.gain_one)
        shift = both(core, pack_own, pack_peer, pack.shift_one)
        hidden_out[...] = to_low((normed * gain + shift) * gates)
        lane = lax.broadcasted_iota(jnp.int32, (1, LANES), 1)
        stats_out[...] = jnp.where(lane == LANES - 1, inv_scale, stats)


def gelu_parts(pre_act):
    whole = 0.5 + 0.5 * lax.erf(pre_act * (0.5**0.5))
    return whole, jnp.exp(-0.5 * pre_act * pre_act) * (1.0 / math.sqrt(2.0 * math.pi))


def ffn_forward_kernel(
    pack,
    core_ref,
    hidden,
    normed,
    up_own,
    up_peer,
    down_own,
    down_peer,
    pack_own,
    pack_peer,
    teacher_own,
    teacher_peer,
    valid,
    mixed_own_out,
    mixed_peer_out,
    active_out,
    slope_out,
    output_own,
    output_peer,
    grad_resid_out,
    grad_ffn_out,
    sums_out,
    total,
    normed_in,
    target,
    sems,
):
    step = pl.program_id(0)
    core = core_ref[0]
    own_steps = pl.num_programs(0) // 2
    width = pack.width
    copies = (
        pltpu.make_async_copy(normed, normed_in, sems.at[2]),
        *rows_in(core, width, teacher_own, teacher_peer, target, sems),
    )

    def tile(at, up_ref, down_ref, pack_ref, mixed_ref):
        spot = pl.multiple_of(at * TILE, TILE)

        def cut(place):
            return pack_ref[:, pl.ds(place[0] + spot, TILE)]

        pre_act = contract(hidden[...], up_ref[...], 1, 0) + cut(pack.b_up)
        whole, density = gelu_parts(pre_act)
        active = pre_act * whole
        unit_gate = hard_concrete(cut(pack.unit_noise), cut(pack.unit_alpha))
        mixed = to_low(active * unit_gate)
        mixed_ref[...] = mixed
        active_out[...] = to_low(active)
        slope_out[...] = to_low((whole + pre_act * density) * unit_gate)
        return contract(mixed, down_ref[...], 1, 0)

    @pl.when(step == 0)
    def _():
        for copy in copies:
            copy.start()
        total[...] = tile(step, up_own, down_own, pack_own, mixed_own_out)

    @pl.when((step > 0) & (step < own_steps))
    def _():
        total[...] += tile(step, up_own, down_own, pack_own, mixed_own_out)

    @pl.when(step >= own_steps)
    def _():
        total[...] += tile(step - own_steps, up_peer, down_peer, pack_peer, mixed_peer_out)

    @pl.when(step == pl.num_programs(0) - 1)
    def _():
        gates = hidden_gates(core, pack, pack_own, pack_peer)
        ffn_gate = scalar_gate(pack, pack_own, 2)

        def vector(spot):
            return both(core, pack_own, pack_peer, spot)

        for copy in copies:
            copy.wait()
        biased = total[...] + vector(pack.b_down)
        hidden_one = (normed_in[...] * vector(pack.gain_one) + vector(pack.shift_one)) * gates
        normed_two, inv_two = norm_forward(hidden_one + biased * (ffn_gate * gates))
        gain = vector(pack.gain_two)
        final = (normed_two * gain + vector(pack.shift_two)) * gates
        final_low = to_low(final)

        def split(own_ref, peer_ref, values_in):
            @pl.when(core == 0)
            def _():
                own_ref[...] = values_in[:, :width]
                peer_ref[...] = values_in[:, width:]

            @pl.when(core == 1)
            def _():
                own_ref[...] = values_in[:, width:]
                peer_ref[...] = values_in[:, :width]

        split(output_own, output_peer, final_low)
        valid_side = to_side(token_line(valid, core))
        grad_final = (final - target[...].astype(f32)) * valid_side
        grad_resid = norm_back(grad_final * (gates * gain), normed_two, inv_two)
        grad_resid_out[...] = grad_resid
        grad_ffn_out[...] = to_low(grad_resid * (ffn_gate * gates))
        sums_out[0:1, :] = column_sum(grad_final * normed_two)
        sums_out[1:2, :] = column_sum(grad_final)
        sums_out[2:3, :] = column_sum(grad_resid * biased)
        sums_out[3:4, :] = column_sum(grad_resid)


def ffn_pre_kernel(
    pack,
    core_ref,
    grad_ffn,
    active,
    slope,
    down_own,
    down_peer,
    grad_pre_own,
    grad_pre_peer,
    unit_sums_out,
):
    step = pl.program_id(0)
    core = core_ref[0]
    own_steps = pl.num_programs(0) // 2
    units = pack.units

    def tile(at, side, down_ref, pre_ref):
        grad_mixed = contract(grad_ffn[...], down_ref[...], 1, 1)
        grad_pre = to_low(grad_mixed * slope[...].astype(f32))
        pre_ref[...] = grad_pre
        spot = pl.multiple_of(side * units + at * TILE, TILE)
        unit_sums_out[0:1, pl.ds(spot, TILE)] = column_sum(grad_mixed * active[...].astype(f32))
        unit_sums_out[1:2, pl.ds(spot, TILE)] = column_sum(grad_pre.astype(f32))

    @pl.when(step < own_steps)
    def _():
        tile(step, core, down_own, grad_pre_own)

    @pl.when(step >= own_steps)
    def _():
        tile(step - own_steps, 1 - core, down_peer, grad_pre_peer)


def ffn_backward_kernel(
    pack,
    core_ref,
    grad_pre_own,
    grad_pre_peer,
    grad_resid_two,
    normed,
    biased,
    stats,
    up_own,
    up_peer,
    pack_own,
    pack_peer,
    grad_resid_out,
    grad_attn_out,
    sums_out,
    total,
    resid_in,
    normed_in,
    biased_in,
    sems,
):
    step = pl.program_id(0)
    core = core_ref[0]
    own_steps = pl.num_programs(0) // 2
    copies = (
        pltpu.make_async_copy(grad_resid_two, resid_in, sems.at[0]),
        pltpu.make_async_copy(normed, normed_in, sems.at[1]),
        pltpu.make_async_copy(biased, biased_in, sems.at[2]),
    )

    @pl.when(step == 0)
    def _():
        for copy in copies:
            copy.start()
        total[...] = contract(grad_pre_own[...], up_own[...], 1, 1)

    @pl.when((step > 0) & (step < own_steps))
    def _():
        total[...] += contract(grad_pre_own[...], up_own[...], 1, 1)

    @pl.when(step >= own_steps)
    def _():
        total[...] += contract(grad_pre_peer[...], up_peer[...], 1, 1)

    @pl.when(step == pl.num_programs(0) - 1)
    def _():
        gates = hidden_gates(core, pack, pack_own, pack_peer)
        mha_gate = scalar_gate(pack, pack_own, 0)
        gain = both(core, pack_own, pack_peer, pack.gain_one)
        for copy in copies:
            copy.wait()
        grad_hidden = resid_in[...] + total[...]
        normed_one = normed_in[...]
        sums_out[0:1, :] = column_sum(grad_hidden * normed_one)
        sums_out[1:2, :] = column_sum(grad_hidden)
        inv_scale = stats[:, LANES - 1 : LANES]
        grad_resid = norm_back(grad_hidden * (gates * gain), normed_one, inv_scale)
        grad_resid_out[...] = grad_resid
        grad_attn_out[...] = to_low(grad_resid * (mha_gate * gates))
        sums_out[2:3, :] = column_sum(grad_resid * biased_in[...])
        sums_out[3:4, :] = column_sum(grad_resid)


def attend_back_kernel(
    pack,
    side_is_own,
    core_ref,
    weights,
    query_ref,
    key_ref,
    value_ref,
    context_ref,
    stats,
    grad_attn,
    wa_ref,
    pack_ref,
    out_ref,
    sums_out,
    gate_row,
):
    at = pl.program_id(0)
    core = core_ref[0]
    width = pack.width
    pair = at if side_is_own else at + pl.num_programs(0)

    @pl.when(at == 0)
    def _():
        gate_row[...] = head_row(pack, pack_ref)

    columns = pl.ds(pl.multiple_of(at * LANES, LANES), LANES)
    lane = lax.broadcasted_iota(jnp.int32, (1, LANES), 1)

    query, key, value = query_ref[...], key_ref[...], value_ref[...]
    context = context_ref[...].astype(f32)
    grad_context = contract(grad_attn[...], wa_ref[...], 1, 1)
    spot = pl.ds(pl.multiple_of(at * LANES, LANES), LANES)
    sums_out[0:1, spot] = column_sum(grad_context * context)
    inverses = [
        row_sum(jnp.where(lane == 2 * pair + side, stats[...], 0.0)) for side in range(2)
    ]
    grad_low = to_low(grad_context * gate_row[:, columns] * pick_half(inverses[0], inverses[1]))
    product = grad_low.astype(f32) * context
    found = []
    for side in range(2):
        mask = half_mask(side, f32)
        level = row_sum(product * mask)
        grad_probs = contract(grad_low * mask.astype(bf16), value, 1, 1)
        chosen = weights[side]
        grad_raw = to_low(chosen.astype(f32) * (grad_probs - level))
        found.append(
            (
                contract(grad_raw, key, 1, 0),
                contract(grad_raw, query, 0, 0),
                contract(chosen, grad_low, 0, 0),
            )
        )
    grad_query = to_low(pick_half(found[0][0], found[1][0]) * HD ** (-0.5))
    grad_key = to_low(pick_half(found[0][1], found[1][1]))
    grad_value = to_low(pick_half(found[0][2], found[1][2]))
    for place, grad in enumerate((grad_query, grad_key, grad_value)):
        at_lane = pl.multiple_of(place * width + at * LANES, LANES)
        out_ref[:, pl.ds(at_lane, LANES)] = grad
    sums_out[1:2, spot] = column_sum(grad_query.astype(f32))
    sums_out[2:3, spot] = column_sum(grad_value.astype(f32))


def down_grad_kernel(bit_ref, mixed, mixed_near, grad, grad_near, sent_out, kept_out):
    summed = to_low(
        contract(mixed[...], grad[...], 0, 0) + contract(mixed_near[...], grad_near[...], 0, 0)
    )
    first = pl.program_id(0) < pl.num_programs(0) // 2

    @pl.when(first)
    def _():
        sent_out[...] = summed

    @pl.when(jnp.logical_not(first))
    def _():
        kept_out[...] = summed


def attn_out_grad_kernel(bit_ref, gated, gated_near, grad, grad_near, sent_out, kept_out):
    width = gated.shape[1]
    part = width // 4
    summed = to_low(
        contract(gated[...], grad[...], 0, 0) + contract(gated_near[...], grad_near[...], 0, 0)
    )

    def put(ref):
        for at in range(4):
            ref[:, at * width : (at + 1) * width] = summed[at * part : (at + 1) * part]

    @pl.when(pl.program_id(0) == 0)
    def _():
        put(sent_out)

    @pl.when(pl.program_id(0) == 1)
    def _():
        put(kept_out)


def attend_grad_kernel(
    half_ref,
    core_ref,
    x_own,
    x_peer,
    grad,
    grad_near,
    out_ref,
    source,
    sem,
):
    core = core_ref[0]

    @pl.when(half_ref[0] == core)
    def _():
        copy = pltpu.make_async_copy(x_own, source, sem)
        copy.start()
        copy.wait()

    @pl.when(half_ref[0] != core)
    def _():
        copy = pltpu.make_async_copy(x_peer, source, sem)
        copy.start()
        copy.wait()

    summed = contract(own_rows(source, core), grad[...], 0, 0) + contract(
        own_rows(source, 1 - core), grad_near[...], 0, 0
    )
    out_ref[...] = to_low(summed)


def input_grad_kernel(
    width,
    core_ref,
    grad_resid,
    grad_own,
    grad_peer,
    wq_own,
    wk_own,
    wv_own,
    wq_peer,
    wk_peer,
    wv_peer,
    own_out,
    peer_out,
):
    core = core_ref[0]
    summed = grad_resid[...]
    for grad, weights in (
        (grad_own, (wq_own, wk_own, wv_own)),
        (grad_peer, (wq_peer, wk_peer, wv_peer)),
    ):
        for place, weight in enumerate(weights):
            summed = summed + contract(
                grad[:, place * width : (place + 1) * width], weight[...], 1, 1
            )

    @pl.when(core == 0)
    def _():
        own_out[...] = summed[:, :width]
        peer_out[...] = summed[:, width:]

    @pl.when(core == 1)
    def _():
        own_out[...] = summed[:, width:]
        peer_out[...] = summed[:, :width]


def place_kernel(bit_ref, half, other, out_ref):
    step = pl.program_id(0)

    @pl.when(step < 2)
    def _():
        out_ref[...] = half[...].astype(f32)

    @pl.when(step >= 2)
    def _():
        out_ref[...] = other[...].astype(f32)


def place_up_kernel(bit_ref, half, other, up_out, attn_out):
    width = attn_out.shape[1]
    rows = up_out.shape[0]
    part = width // 4

    def put(ref):
        up_out[...] = ref[:rows, :].astype(f32)
        for at in range(4):
            attn_out[at * part : (at + 1) * part, :] = ref[
                rows:, at * width : (at + 1) * width
            ].astype(f32)

    @pl.when(pl.program_id(0) == 0)
    def _():
        put(half)

    @pl.when(pl.program_id(0) == 1)
    def _():
        put(other)


def place_attend_kernel(bit_ref, half, other, query_out, key_out, value_out):
    width = query_out.shape[1]

    def put(ref):
        for at, out in enumerate((query_out, key_out, value_out)):
            out[...] = ref[:, at * width : (at + 1) * width].astype(f32)

    @pl.when(pl.program_id(0) == 0)
    def _():
        put(half)

    @pl.when(pl.program_id(0) == 1)
    def _():
        put(other)


def finish_kernel(
    pack,
    core_ref,
    sums,
    pack_own,
    pack_peer,
    b_query,
    b_value,
    b_attn_out,
    gain_one,
    shift_one,
    b_up,
    b_down,
    gain_two,
    shift_two,
    head_gate,
    mha_gate,
    unit_gate,
    ffn_gate,
    hidden_gate,
    head_alpha,
    mha_alpha,
    unit_alpha,
    ffn_alpha,
    hidden_alpha,
    share_out,
    penalty_out,
):
    core = core_ref[0]
    width, units = pack.width, pack.units
    columns = pl.ds(pl.multiple_of(core * width, LANES), width)
    heads = width // HD

    def put(out_ref, line):
        out_ref[...] = line.reshape(out_ref.shape)

    def own(row):
        return sums[row : row + 1, columns]

    def vector(spot):
        return take(pack_own, spot)

    gates = hard_concrete(vector(pack.hidden_noise), vector(pack.hidden_alpha))
    mha, ffn = scalar_gate(pack, pack_own, 0), scalar_gate(pack, pack_own, 2)
    put(gain_two, gates * own(0))
    put(shift_two, gates * own(1))
    put(b_down, (ffn * gates) * own(3))
    put(gain_one, gates * own(4))
    put(shift_one, gates * own(5))
    put(b_attn_out, (mha * gates) * own(7))
    put(b_query, own(9))
    put(b_value, own(10))
    grad_hidden = (
        vector(pack.gain_two) * own(0)
        + vector(pack.shift_two) * own(1)
        + ffn * own(2)
        + vector(pack.gain_one) * own(4)
        + vector(pack.shift_one) * own(5)
        + mha * own(6)
    )
    put(hidden_gate, grad_hidden)
    all_gates = hidden_gates(core, pack, pack_own, pack_peer)
    grad_ffn_gate = row_sum(all_gates * sums[2:3, :])
    grad_mha_gate = row_sum(all_gates * sums[6:7, :])
    put(ffn_gate, grad_ffn_gate)
    put(mha_gate, grad_mha_gate)

    unit_rows = units // (2 * width)

    def unit_line(first):
        at = first + core * unit_rows
        return jnp.concatenate([sums[pl.ds(at + k, 1), :] for k in range(unit_rows)], axis=1)

    grad_unit = unit_line(11)
    put(b_up, unit_line(11 + 2 * unit_rows))
    put(unit_gate, grad_unit)
    by_head = own(8)
    lane = lax.broadcasted_iota(jnp.int32, (1, LANES), 1)
    grad_head = jnp.zeros((1, LANES), f32)
    for at in range(heads):
        grad_head = jnp.where(
            lane == at, row_sum(by_head[:, at * HD : (at + 1) * HD]), grad_head
        )
    put(head_gate, grad_head[:, :heads])

    numbers = vector(pack.scalars)
    mha_open, ffn_open = open_share(numbers[:, 0:1]), open_share(numbers[:, 2:3])
    first_weight, second_weight = numbers[:, 4:5], numbers[:, 5:6]

    def open_total(spot, count):
        return row_sum(open_share(take(pack_own, spot)[:, :count])) + row_sum(
            open_share(take(pack_peer, spot)[:, :count])
        )

    head_sum = open_total(pack.head_alpha, heads)
    unit_sum = open_total(pack.unit_alpha, units)
    hidden_sum = open_total(pack.hidden_alpha, width)
    model, inner = 2.0 * width, 2.0 * units
    scale = 1.0 / ((4.0 * model + 2.0 * inner) * model)
    kept = 4.0 * HD * mha_open * head_sum + 2.0 * ffn_open * unit_sum
    share = kept * hidden_sum * scale
    gap = share - target_share
    put(share_out, share)
    put(penalty_out, first_weight * gap + second_weight * gap * gap)
    slope = (first_weight + 2.0 * second_weight * gap) * scale
    by_heads = slope * hidden_sum * (4.0 * HD)
    by_units = slope * hidden_sum * 2.0

    def alpha_grad(noise, alpha, grad_gate, grad_open):
        opened = open_share(alpha)
        return gate_slope(noise, alpha) * grad_gate + grad_open * (opened * (1.0 - opened))

    put(
        head_alpha,
        alpha_grad(
            vector(pack.head_noise), vector(pack.head_alpha), grad_head, by_heads * mha_open
        )[:, :heads],
    )
    put(
        unit_alpha,
        alpha_grad(
            vector(pack.unit_noise), vector(pack.unit_alpha), grad_unit, by_units * ffn_open
        ),
    )
    put(
        hidden_alpha,
        alpha_grad(
            vector(pack.hidden_noise), vector(pack.hidden_alpha), grad_hidden, slope * kept
        ),
    )
    put(
        mha_alpha,
        alpha_grad(numbers[:, 1:2], numbers[:, 0:1], grad_mha_gate, by_heads * head_sum),
    )
    put(
        ffn_alpha,
        alpha_grad(numbers[:, 3:4], numbers[:, 2:3], grad_ffn_gate, by_units * unit_sum),
    )


def full(shape):
    return pl.BlockSpec(shape, lambda *at: (0,) * len(shape), pipeline_mode=pl.Buffered(1))


def anywhere():
    return pl.BlockSpec(memory_space=pl.ANY)


def every(shape, dim):
    return pl.BlockSpec(shape, lambda i: tuple(i if d == dim else 0 for d in range(2)))


def sides(steps):
    def early(shape, dim):
        return pl.BlockSpec(
            shape, lambda i: tuple(jnp.minimum(i, steps - 1) if d == dim else 0 for d in range(2))
        )

    def late(shape, dim):
        return pl.BlockSpec(
            shape, lambda i: tuple(jnp.maximum(i - steps, 0) if d == dim else 0 for d in range(2))
        )

    return early, late


def one_number():
    return pl.BlockSpec(memory_space=pltpu.SMEM)


def shaped(shape, dtype):
    return jax.ShapeDtypeStruct(shape, dtype)


def far(struct):
    return pltpu.HBM(struct.shape, struct.dtype)


ORDER = (
    *("K3a", "KD", "K3b", "KU", "hD", "K4a", "Kao", "qD", "hU", "K4b", "KAs", "sD", "qU"),
    *("KAk", "S0", "hA", "sD", "sU", "S", "K6", "qA", "sD", "S", "wD", "sU", "O"),
    *("sA", "S", "pD", "sU", "sA", "wU", "sA", "S", "wA", "pU", "S", "F", "pA"),
)
ON_PATH = ("D", "U", "A")


class Order:
    def __init__(self):
        self.last = ()
        self.share = 1.0

    def tie(self, values_in):
        if not self.last:
            return values_in
        return lax.optimization_barrier((values_in, *self.last))[0]

    def mark(self, *values_in):
        self.last = values_in


def call(order, kernel, grid, in_specs, out_specs, out_shape, scratch, cost, args, mib=28):
    out = pl.pallas_call(
        kernel,
        grid=grid,
        in_specs=in_specs,
        out_specs=out_specs,
        out_shape=out_shape,
        scratch_shapes=scratch,
        compiler_params=pltpu.CompilerParams(vmem_limit_bytes=mib * 2**20),
        cost_estimate=pl.CostEstimate(
            flops=int(cost[0] * 1e9 * order.share),
            bytes_accessed=int(cost[1] * 1e6 * order.share),
            transcendentals=0,
        ),
    )(order.tie(args[0]), *args[1:])
    order.mark(jax.tree.leaves(out)[-1])
    return out


def call_by_half(order, kernel, grid, in_specs, out_specs, out_shape, cost, half, args, mib=28):
    out = pl.pallas_call(
        kernel,
        grid_spec=pltpu.PrefetchScalarGridSpec(
            num_scalar_prefetch=1, grid=grid, in_specs=in_specs, out_specs=out_specs
        ),
        out_shape=out_shape,
        compiler_params=pltpu.CompilerParams(vmem_limit_bytes=mib * 2**20),
        cost_estimate=pl.CostEstimate(
            flops=int(cost[0] * 1e9 * order.share),
            bytes_accessed=int(cost[1] * 1e6 * order.share),
            transcendentals=0,
        ),
    )(order.tie(half), *args)
    order.mark(jax.tree.leaves(out)[-1])
    return out


def swap_pairs(core_masks):
    rows, cores = lax.axis_size("rows"), lax.axis_size("hid")
    return [
        (row * cores + core, (row ^ core_masks[core]) * cores + core)
        for row in range(rows)
        for core in range(cores)
    ]


def swap(values_in, core_masks):
    return lax.ppermute(values_in, ("rows", "hid"), swap_pairs(core_masks))


def along(values_in, steps):
    rows, cores = lax.axis_size("rows"), lax.axis_size("hid")
    pairs = [
        (row * cores + core, (row + 4 * (steps[row // 4 % 4] - row // 4 % 4)) * cores + core)
        for row in range(rows)
        if row // 4 % 4 in steps
        for core in range(cores)
    ]
    return lax.ppermute(values_in, ("rows", "hid"), pairs)


def in_hbm(values_in):
    return pltpu.with_memory_space_constraint(values_in, pltpu.HBM)


def near(values_in):
    return lax.ppermute(values_in, "hid", [(0, 1), (1, 0)])


def spread_masks():
    rest = lax.axis_size("rows") // 4
    masks = [4 * (2**k * 2 - 1) for k in range(rest.bit_length() - 1)]
    return [(masks[k], masks[len(masks) - 1 - k]) for k in range(len(masks))]


def add_low(first, second):
    return to_low(first.astype(f32) + second.astype(f32))


def pick(values_in, at):
    return lax.dynamic_index_in_dim(values_in, at, 0, keepdims=False)


class RowSum:
    def __init__(self, order, sent_half, first_bit, second_bit):
        self.order = order
        self.first_bit, self.second_bit = first_bit, second_bit
        self.near = swap(sent_half, (1, 2))

    def halve(self, kept):
        at = self.second_bit
        kept = self.order.tie(kept)
        to_send = add_low(pick(kept, 1 - at), pick(self.near, 1 - at))
        self.own = add_low(pick(kept, at), pick(self.near, at))
        self.near = swap(to_send, (2, 1))
        self.order.mark(to_send, self.own)

    def halve_with(self, kept, below, below_near):
        kept = add_low(self.order.tie(kept), self.near)
        below = add_low(self.order.tie(below), below_near)
        rows = (kept.shape[0] + below.shape[0]) // 2
        first, second = kept[:rows], jnp.concatenate((kept[rows:], below), axis=0)
        to_send = jnp.where(self.second_bit == 0, second, first)
        self.own = jnp.where(self.second_bit == 0, first, second)
        self.near = swap(to_send, (2, 1))
        self.order.mark(to_send, self.own)

    def quarter(self, path=False):
        self.own = add_low(self.order.tie(self.own), self.near)
        masks = spread_masks()
        self.left = [partial(swap, core_masks=pair) for pair in masks]
        self.inner = None
        if path:
            steps = [{0: 1, 3: 2}, {1: 2, 2: 1}, {1: 0, 2: 3}]
            self.left = [partial(along, steps=item) for item in steps] + self.left[2:]
            at = lax.rem(lax.axis_index("rows") // 4, 4)
            self.inner = (at == 1) | (at == 2)
            self.until_out = 3
        self.near = self.left.pop(0)(self.own)
        self.order.mark(self.own)

    def spread(self):
        own = self.order.tie(self.own)
        if self.inner is not None:
            self.until_out -= 1
        if self.inner is not None and self.until_out == 0:
            self.own = jnp.where(self.inner, own, self.near)
        else:
            self.own = add_low(own, self.near)
        self.near = self.left.pop(0)(self.own) if self.left else swap(self.own, (2, 1))
        self.order.mark(self.own)

    def spread_all(self):
        while self.left:
            self.spread()
        self.spread()

    def widen(self):
        own, near = self.order.tie(self.own), self.near
        self.half = jnp.where(
            self.second_bit == 0, jnp.stack((own, near)), jnp.stack((near, own))
        )
        self.order.mark(self.half)
        self.near = swap(self.half, (1, 2))

    def parts(self):
        return self.half, self.near


class SmallSum:
    def __init__(self, order, values_in):
        self.order, self.own = order, values_in
        self.left = [(1, 2), (2, 1)] + spread_masks()
        self.near = near(values_in)

    def step(self):
        if self.near is None:
            return False
        self.own = self.order.tie(self.own) + self.near
        self.order.mark(self.own)
        self.near = swap(self.own, self.left.pop(0)) if self.left else None
        return True

    def rest(self):
        while self.step():
            pass
        return self.own


def body(
    hidden_in,
    teacher,
    segment_ids,
    valid_mask,
    w_query,
    b_query,
    w_key,
    w_value,
    b_value,
    w_attn_out,
    b_attn_out,
    gain_one,
    shift_one,
    w_up,
    b_up,
    w_down,
    b_down,
    gain_two,
    shift_two,
    head_alpha,
    mha_alpha,
    unit_alpha,
    ffn_alpha,
    hidden_alpha,
    head_noise,
    mha_noise,
    unit_noise,
    ffn_noise,
    hidden_noise,
    lagrange,
):
    model, width = w_query.shape
    units = w_up.shape[1]
    heads = width // HD
    pairs = model // LANES
    tokens = hidden_in.shape[0] // 2
    pack = Pack(width, units)
    order = Order()
    core = lax.axis_index("hid")
    row = lax.axis_index("rows")
    core_at = jnp.reshape(core, (1,)).astype(jnp.int32)
    low_bit, high_bit = row & 1, (row >> 1) & 1
    first_bit = jnp.where(core == 0, low_bit, high_bit).astype(jnp.int32)
    second_bit = jnp.where(core == 0, high_bit, low_bit).astype(jnp.int32)

    packed = (
        (b_query, pack.b_query, 0),
        (b_value, pack.b_value, 0),
        (b_attn_out, pack.b_attn_out, 0),
        (gain_one, pack.gain_one, 0),
        (shift_one, pack.shift_one, 0),
        (b_down, pack.b_down, 0),
        (gain_two, pack.gain_two, 0),
        (shift_two, pack.shift_two, 0),
        (hidden_alpha, pack.hidden_alpha, 0),
        (hidden_noise, pack.hidden_noise, 0),
        (b_up, pack.b_up, 0),
        (unit_alpha, pack.unit_alpha, 0),
        (unit_noise, pack.unit_noise, 0),
        (head_alpha, pack.head_alpha, 0),
        (head_noise, pack.head_noise, 0),
        (mha_alpha, pack.scalars, 0),
        (mha_noise, pack.scalars, 1),
        (ffn_alpha, pack.scalars, 2),
        (ffn_noise, pack.scalars, 3),
        (lagrange, pack.scalars, 4),
    )
    pack_own = call(
        order,
        partial(pack_kernel, pack, [item[1:] for item in packed]),
        (),
        [full(item[0].shape) if item[0].shape[0] > 1 else one_number() for item in packed],
        full((1, pack.total)),
        far(shaped((1, pack.total), f32)),
        [],
        (0.001, 0.1, 0),
        tuple(in_hbm(item[0]) if item[0].shape[0] > 1 else item[0] for item in packed),
        mib=4,
    )
    x_peer = near(hidden_in)
    pack_peer = near(pack_own)
    wq_peer, wk_peer, wv_peer = near(w_query), near(w_key), near(w_value)
    wa_peer = near(w_attn_out)
    x_peer, up_sent, down_sent, teacher_sent = lax.optimization_barrier(
        (x_peer, w_up, w_down, teacher)
    )
    up_peer, down_peer, teacher_peer = near(up_sent), near(down_sent), near(teacher_sent)
    hidden_in, teacher, w_query, w_key, w_value, w_attn_out, w_up, w_down = (
        in_hbm(item)
        for item in (hidden_in, teacher, w_query, w_key, w_value, w_attn_out, w_up, w_down)
    )
    wq_peer, wk_peer, wv_peer, wa_peer = (
        in_hbm(item) for item in (wq_peer, wk_peer, wv_peer, wa_peer)
    )
    pack_own, pack_peer = in_hbm(pack_own), in_hbm(pack_peer)
    segments = in_hbm(segment_ids.reshape(-1, LANES))
    valid = in_hbm(valid_mask.reshape(-1, LANES))
    packs = [full((1, pack.total))] * 2
    token_low = shaped((tokens, model), bf16)
    token_wide = shaped((tokens, model), f32)
    token_half = shaped((tokens, width), bf16)

    own_pairs = pairs // 2
    one_side = (own_pairs,)
    by_pair = every((tokens, LANES), 1)
    head_outs = [pl.BlockSpec((2, BLOCK, BLOCK), lambda i: (i, 0, 0))] + [by_pair] * 5
    head_shapes = [far(shaped((2 * own_pairs, BLOCK, BLOCK), bf16))] + [far(token_half)] * 5
    head_weights = [every((model, LANES), 1)] * 3 + [every((LANES, model), 0)]
    token_stats = far(shaped((tokens, LANES), f32))
    *heads_own, gated_own, stats, x_nat, mask_bias, attn_part = call(
        order,
        partial(attend_own_kernel, pack),
        one_side,
        [one_number()]
        + [anywhere()] * 2
        + head_weights
        + [full((1, pack.total))]
        + [full(segments.shape)] * 2,
        head_outs
        + [full((tokens, LANES)), full((tokens, model))]
        + [full((BLOCK, BLOCK)), full((tokens, model))],
        head_shapes + [token_stats, token_low, shaped((BLOCK, BLOCK), f32), token_wide],
        [pltpu.VMEM((1, width), f32), pltpu.SemaphoreType.DMA((2,))],
        (40, 200, 3),
        (
            core_at,
            hidden_in,
            x_peer,
            w_query,
            w_key,
            w_value,
            w_attn_out,
            pack_own,
            segments,
            valid,
        ),
    )
    *heads_peer, gated_peer, stats, biased, normed, hidden = call(
        order,
        partial(attend_peer_kernel, pack),
        one_side,
        [one_number(), full((tokens, model)), full((BLOCK, BLOCK)), full((tokens, model))]
        + [full((tokens, LANES))]
        + head_weights
        + packs,
        head_outs + [full((tokens, LANES))] + [full((tokens, model))] * 3,
        head_shapes + [token_stats, far(token_wide), far(token_wide), token_low],
        [pltpu.VMEM((tokens, model), f32), pltpu.VMEM((1, width), f32)],
        (40, 200, 3),
        (
            core_at,
            x_nat,
            mask_bias,
            attn_part,
            in_hbm(stats),
            wq_peer,
            wk_peer,
            wv_peer,
            wa_peer,
            pack_own,
            pack_peer,
        ),
    )
    normed, biased, stats = in_hbm(normed), in_hbm(biased), in_hbm(stats)
    hidden_near = near(hidden)
    gated_near = near(gated_peer)

    tiles = units // TILE
    early, late = sides(tiles)

    (
        mixed_own,
        mixed_peer,
        active,
        slope,
        output_own,
        output_peer,
        grad_resid_two,
        grad_ffn,
        sums_two,
    ) = call(
        order,
        partial(ffn_forward_kernel, pack),
        (2 * tiles,),
        [one_number(), full((tokens, model)), anywhere()]
        + [early((model, TILE), 1), late((model, TILE), 1)]
        + [early((TILE, model), 0), late((TILE, model), 0)]
        + packs
        + [anywhere()] * 2
        + [full(valid.shape)],
        [early((tokens, TILE), 1), late((tokens, TILE), 1)]
        + [every((tokens, TILE), 1)] * 2
        + [full((tokens, width))] * 2
        + [full((tokens, model))] * 2
        + [full((4, model))],
        [
            shaped((tokens, units), bf16),
            shaped((tokens, units), bf16),
            shaped((tokens, 2 * units), bf16),
            shaped((tokens, 2 * units), bf16),
            far(token_half),
            far(token_half),
            far(token_wide),
            token_low,
            shaped((4, model), f32),
        ],
        [
            pltpu.VMEM((tokens, model), f32),
            pltpu.VMEM((tokens, model), f32),
            pltpu.VMEM((tokens, model), bf16),
            pltpu.SemaphoreType.DMA((3,)),
        ],
        (5.0, 25, 3),
        (
            core_at,
            hidden,
            normed,
            w_up,
            up_peer,
            w_down,
            down_peer,
            pack_own,
            pack_peer,
            teacher,
            teacher_peer,
            valid,
        ),
    )
    grad_resid_two = in_hbm(grad_resid_two)
    mixed_near = near(mixed_peer)
    grad_ffn_near = near(grad_ffn)
    output_near = near(output_peer)
    up_rows = width + width // 4
    half_units = units // 2
    step_units = half_units // 2

    bit_at = jnp.reshape(first_bit, (1,))

    def at_half(i, steps, bit):
        return jnp.where(i < steps, 1 - bit[0], bit[0])

    def sent_then_kept(shape, steps, dim):
        return [
            pl.BlockSpec(
                shape,
                lambda i, t, at=at: tuple(at(i) if d == dim else 0 for d in range(2)),
            )
            for at in (
                lambda i: jnp.minimum(i, steps - 1),
                lambda i: jnp.maximum(i - steps, 0),
            )
        ]

    def attend_back(side_is_own, wa_ref):
        arrays = heads_own if side_is_own else heads_peer
        return call(
            order,
            partial(attend_back_kernel, pack, side_is_own),
            one_side,
            [one_number(), pl.BlockSpec((2, BLOCK, BLOCK), lambda i: (i, 0, 0))]
            + [by_pair] * 4
            + [full((tokens, LANES)), full((tokens, model))]
            + [every((LANES, model), 0)]
            + [full((1, pack.total))],
            [full((tokens, 3 * width)), full((3, width))],
            [shaped((tokens, 3 * width), bf16), shaped((3, width), f32)],
            [pltpu.VMEM((1, width), f32)],
            (2.0, 10, 0),
            (
                core_at,
                *(in_hbm(item) for item in arrays),
                stats,
                grad_attn,
                wa_ref,
                pack_own if side_is_own else pack_peer,
            ),
            mib=18,
        )

    def attend_half(half):
        out = call(
            order,
            attend_grad_kernel,
            (),
            [one_number()] * 2 + [anywhere()] * 2 + [full((tokens, 3 * width))] * 2,
            full((width, 3 * width)),
            shaped((width, 3 * width), bf16),
            [pltpu.VMEM(hidden_in.shape, bf16), pltpu.SemaphoreType.DMA],
            (24, 100, 0),
            (jnp.reshape(half, (1,)), core_at, hidden_in, x_peer, grad_own, grad_near),
            mib=12,
        )
        return out.reshape(2, width // 2, 3 * width)

    def place(pieces):
        _, height, across = pieces[0].shape

        def block(at):
            return pl.BlockSpec((1, height, across), at)

        out = call_by_half(
            order,
            place_kernel,
            (4,),
            [
                block(lambda i, t: (jnp.minimum(i, 1), 0, 0)),
                block(lambda i, t: (jnp.maximum(i - 2, 0), 0, 0)),
            ],
            block(lambda i, t: (2 * lax.rem(t[0] + i // 2, 2) + lax.rem(i, 2), 0, 0)),
            shaped((4, height, across), f32),
            (0.001, 7),
            bit_at,
            pieces,
            mib=18,
        )
        return out.reshape(4 * height, across)

    def by_token(own, other):
        own = order.tie(own)
        out = jnp.where(
            core == 0, jnp.concatenate((own, other), axis=0), jnp.concatenate((other, own), axis=0)
        )
        order.mark(out)
        return out

    def by_half(pieces):
        return tuple(piece.reshape(-1, piece.shape[-1]) for piece in pieces)

    def own_half(shape, dim):
        return pl.BlockSpec(
            shape, lambda i, t: tuple(lax.rem(t[0] + i, 2) if d == dim else 0 for d in range(2))
        )

    grad_pre_own = grad_pre_peer = unit_sums = grad_pre_near = down_kept = down_chunk = None
    grad_resid_one = grad_attn = sums_one = grad_attn_near = up_kept = up_chunk = None
    grad_peer = sums_peer = grad_near = attn_kept = attn_near = grad_own = None
    sums_own = attend_chunk = attend_kept = small = input_own = input_peer = None
    input_near = output = grad_input = sum_down = finished = sum_up = None
    sum_attn = sum_query = sum_key = sum_value = None

    def units_back():
        nonlocal grad_pre_own, grad_pre_peer, unit_sums, grad_pre_near
        grad_pre_own, grad_pre_peer, unit_sums = call(
            order,
            partial(ffn_pre_kernel, pack),
            (2 * tiles,),
            [one_number(), full((tokens, model))]
            + [every((tokens, TILE), 1)] * 2
            + [early((TILE, model), 0), late((TILE, model), 0)],
            [early((tokens, TILE), 1), late((tokens, TILE), 1), full((2, 2 * units))],
            [
                shaped((tokens, units), bf16),
                shaped((tokens, units), bf16),
                shaped((2, 2 * units), f32),
            ],
            [],
            (50, 300, 0),
            (core_at, grad_ffn, active, slope, w_down, down_peer),
            mib=18,
        )
        grad_pre_near = near(grad_pre_peer)

    def down_grads():
        nonlocal down_kept, down_chunk
        by_units = pl.BlockSpec(
            (tokens, step_units), lambda i, t: (0, at_half(i, 2, t) * 2 + lax.rem(i, 2))
        )
        down_sent, down_kept = call_by_half(
            order,
            down_grad_kernel,
            (4,),
            [by_units, by_units] + [full((tokens, model))] * 2,
            sent_then_kept((step_units, model), 2, 0),
            [shaped((half_units, model), bf16)] * 2,
            (48, 180),
            bit_at,
            (mixed_own, mixed_near, grad_ffn, grad_ffn_near),
            mib=12,
        )
        down_sent, down_kept = (
            item.reshape(2, half_units // 2, model) for item in (down_sent, down_kept)
        )
        down_chunk = RowSum(order, down_sent, first_bit, second_bit)

    def ffn_back():
        nonlocal grad_resid_one, grad_attn, sums_one, grad_attn_near
        grad_resid_one, grad_attn, sums_one = call(
            order,
            partial(ffn_backward_kernel, pack),
            (2 * tiles,),
            [one_number()]
            + [early((tokens, TILE), 1), late((tokens, TILE), 1)]
            + [anywhere()] * 3
            + [full((tokens, LANES))]
            + [early((model, TILE), 1), late((model, TILE), 1)]
            + packs,
            [full((tokens, model))] * 2 + [full((4, model))],
            [far(token_wide), token_low, shaped((4, model), f32)],
            [pltpu.VMEM((tokens, model), f32)] * 4 + [pltpu.SemaphoreType.DMA((3,))],
            (2.5, 15, 0),
            (
                core_at,
                grad_pre_own,
                grad_pre_peer,
                grad_resid_two,
                normed,
                biased,
                stats,
                w_up,
                up_peer,
                pack_own,
                pack_peer,
            ),
            mib=20,
        )
        grad_attn_near = near(grad_attn)

    def up_grads():
        nonlocal up_kept, up_chunk
        by_features = pl.BlockSpec((tokens, width), lambda i, t: (0, at_half(i, 2, t)))
        by_units = pl.BlockSpec((tokens, half_units), lambda i, t: (0, lax.rem(i, 2)))
        up_sent, up_kept = call_by_half(
            order,
            down_grad_kernel,
            (4,),
            [by_features, by_features, by_units, by_units],
            sent_then_kept((width, half_units), 2, 1),
            [shaped((width, units), bf16)] * 2,
            (2.4, 12),
            bit_at,
            (hidden, hidden_near, grad_pre_own, grad_pre_near),
            mib=18,
        )
        up_chunk = RowSum(order, up_sent, first_bit, second_bit)

    def peer_heads():
        nonlocal grad_peer, sums_peer, grad_near
        grad_peer, sums_peer = attend_back(False, wa_peer)
        grad_near = near(grad_peer)

    def own_heads():
        nonlocal grad_own, sums_own
        grad_own, sums_own = attend_back(True, w_attn_out)

    def out_grads():
        nonlocal attn_kept, attn_near
        by_columns = pl.BlockSpec((tokens, width), lambda i, t: (0, at_half(i, 1, t)))
        attn_sent, attn_kept = call_by_half(
            order,
            attn_out_grad_kernel,
            (2,),
            [full((tokens, width))] * 2 + [by_columns] * 2,
            [full((width // 4, units))] * 2,
            [shaped((width // 4, units), bf16)] * 2,
            (0.6, 3),
            bit_at,
            (gated_own, gated_near, grad_attn, grad_attn_near),
            mib=8,
        )
        attn_near = swap(attn_sent, (1, 2))

    def send_attend():
        nonlocal attend_chunk
        attend_sent = attend_half(1 - first_bit)
        attend_chunk = RowSum(order, attend_sent, first_bit, second_bit)

    def keep_attend():
        nonlocal attend_kept
        attend_kept = attend_half(first_bit)

    def start_small():
        nonlocal small
        sums_late = order.tie(sums_own)
        sums_attn = jnp.where(
            core == 0,
            jnp.concatenate((sums_late, sums_peer), axis=1),
            jnp.concatenate((sums_peer, sums_late), axis=1),
        )
        small = SmallSum(
            order,
            jnp.concatenate((sums_two, sums_one, sums_attn, unit_sums.reshape(-1, model)), axis=0),
        )

    def inputs_back():
        nonlocal input_own, input_peer, input_near
        input_own, input_peer = call(
            order,
            partial(input_grad_kernel, width),
            (),
            [one_number(), full((tokens, model))]
            + [full((tokens, 3 * width))] * 2
            + [full((model, width))] * 6,
            [full((tokens, width))] * 2,
            [shaped((tokens, width), f32)] * 2,
            [],
            (1.8, 8, 0),
            (
                core_at,
                in_hbm(grad_resid_one),
                grad_own,
                grad_peer,
                w_query,
                w_key,
                w_value,
                wq_peer,
                wk_peer,
                wv_peer,
            ),
            mib=16,
        )
        input_near = near(input_peer)

    def put_output():
        nonlocal output, grad_input
        output = by_token(output_own, output_near)
        grad_input = by_token(input_own, input_near)

    def finish_small():
        nonlocal finished
        small_sums = small.rest()
        sizes = (width,) * 5 + (units,) + (width,) * 3 + (heads, 1, units, 1, width)
        sizes = sizes + (heads, 1, units, 1, width, 1, 1)
        finished = call(
            order,
            partial(finish_kernel, pack),
            (),
            [one_number(), full(small_sums.shape)] + packs,
            [full((size,)) for size in sizes],
            [shaped((size,), f32) for size in sizes],
            [],
            (0.01, 0.3, 0.1),
            (core_at, small_sums, pack_own, pack_peer),
        )

    def place_down():
        nonlocal sum_down
        sum_down = place(down_chunk.parts())

    def place_up():
        nonlocal sum_up, sum_attn
        sum_up, sum_attn = call_by_half(
            order,
            place_up_kernel,
            (2,),
            [full((up_rows, units))] * 2,
            [own_half((width, units), 0), own_half((width, width), 1)],
            [shaped((model, units), f32), shaped((width, model), f32)],
            (0.001, 10),
            bit_at,
            by_half(up_chunk.parts()),
            mib=18,
        )

    def place_attend():
        nonlocal sum_query, sum_key, sum_value
        sum_query, sum_key, sum_value = call_by_half(
            order,
            place_attend_kernel,
            (2,),
            [full((width, 3 * width))] * 2,
            [own_half((width, width), 0)] * 3,
            [shaped((model, width), f32)] * 3,
            (0.001, 7),
            bit_at,
            by_half(attend_chunk.parts()),
            mib=18,
        )

    steps = dict(
        K3a=units_back,
        KD=down_grads,
        K3b=ffn_back,
        KU=up_grads,
        K4a=peer_heads,
        K4b=own_heads,
        Kao=out_grads,
        KAs=send_attend,
        KAk=keep_attend,
        S0=start_small,
        S=lambda: small.step(),
        K6=inputs_back,
        O=put_output,
        F=finish_small,
        hD=lambda: down_chunk.halve(down_kept),
        qD=lambda: down_chunk.quarter("D" in ON_PATH),
        sD=lambda: down_chunk.spread(),
        wD=lambda: down_chunk.widen(),
        pD=place_down,
        hU=lambda: up_chunk.halve_with(up_kept, attn_kept, attn_near),
        qU=lambda: up_chunk.quarter("U" in ON_PATH),
        sU=lambda: up_chunk.spread(),
        wU=lambda: up_chunk.widen(),
        pU=place_up,
        hA=lambda: attend_chunk.halve(attend_kept),
        qA=lambda: attend_chunk.quarter("A" in ON_PATH),
        sA=lambda: attend_chunk.spread(),
        wA=lambda: attend_chunk.widen(),
        pA=place_attend,
    )
    for name in ORDER:
        steps[name]()
    return (
        output,
        grad_input,
        sum_query,
        finished[0],
        sum_key,
        sum_value,
        finished[1],
        sum_attn,
        finished[2],
        finished[3],
        finished[4],
        sum_up,
        finished[5],
        sum_down,
        *finished[6:],
    )


def solution(mesh):
    in_specs = (
        P("rows", "hid"),
        P("rows", "hid"),
        P("rows"),
        P("rows"),
        P(None, "hid"),
        P("hid"),
        P(None, "hid"),
        P(None, "hid"),
        P("hid"),
        P("hid", None),
        P("hid"),
        P("hid"),
        P("hid"),
        P(None, "hid"),
        P("hid"),
        P("hid", None),
        P("hid"),
        P("hid"),
        P("hid"),
        P("hid"),
        P(),
        P("hid"),
        P(),
        P("hid"),
        P("hid"),
        P(),
        P("hid"),
        P(),
        P("hid"),
        P(),
    )
    out_specs = (
        P("rows", "hid"),
        P("rows", "hid"),
        P(None, "hid"),
        P("hid"),
        P(None, "hid"),
        P(None, "hid"),
        P("hid"),
        P("hid", None),
        P("hid"),
        P("hid"),
        P("hid"),
        P(None, "hid"),
        P("hid"),
        P("hid", None),
        P("hid"),
        P("hid"),
        P("hid"),
        P("hid"),
        P(),
        P("hid"),
        P(),
        P("hid"),
        P("hid"),
        P(),
        P("hid"),
        P(),
        P("hid"),
        P(),
        P(),
    )
    return jax.shard_map(body, mesh=mesh, in_specs=in_specs, out_specs=out_specs, check_vma=False)
```
